32 devices in a mesh: date: 8 (over z, y), rng: 4 (over x, core).
Axes of the slice: x: 2, y: 2, z: 4, core: 2. Of those that a mesh axis runs over, the one named last changes fastest.
Arguments:
- slc: bfloat16 [8, 2, 64, 4096], P('date', None, None, 'rng'), may hold values from -9 to 9
- ref_date: int32 [1], replicated, may hold values from 0 to 7
- int_offset: int32 [8, 1, 64], P('date', None, 'rng'), may hold values from -4 to 4
- frac_offset: float32 [8, 1, 64], P('date', None, 'rng'), may hold values from 0 to 1
- partners: int32 [8, 4], P('date'), may hold values from 0 to 1, as said below
Outputs:
- surface: float32 [8, 1, 64, 1024], P('date', None, 'rng')
- coherence: bfloat16 [8, 4, 64, 4096], P('date', None, None, 'rng')
The draws below stay inside these ranges and needn't reach their ends.
Inputs may be any that keep to these rules, and one draw needn't show every extreme that they name: `partners`: each row holds 2 to 4 ones.
All inputs are finite; a program needn't handle non-finite values.
Results may differ from the reference program's by a relative error of at most 0.009.
Values may be sent and summed in bfloat16 or wider, within the bound.
No kernel may reach another device: no remote copies, remote signals or barrier semaphores. Data moves between devices by JAX's collectives and lax.ppermute only.
A program may use at most 64 MiB of HBM per device.

```python
import jax
import jax.numpy as jnp
from jax import lax

BLK = 64
OVS = 2
LAGS = 32
IMAX = 4
SPAN = 4
BOXA = 5
BOXR = 19
AZ = 64
DATES = 8
NRG = 4096


def shift_table(key):
    table = jax.random.randint(jax.random.fold_in(key, 11), (DATES, AZ // BLK, NRG // BLK), -IMAX, IMAX + 1)
    table = table.at[0, 0, 0].set(IMAX)
    table = table.at[DATES - 1, AZ // BLK - 1, NRG // BLK - 1].set(-IMAX)
    return table.astype(jnp.int32)


def draw_int_offset(key, part):
    return shift_table(key)


def draw_slc(key, part):
    table = shift_table(key)
    width = NRG + 2 * IMAX
    scene = jnp.clip(jax.random.normal(jax.random.fold_in(key, 21), (2, AZ, width), jnp.float32), -6.0, 6.0)
    noise = 0.5 * jnp.clip(jax.random.normal(jax.random.fold_in(key, 22), (DATES, 2, AZ, NRG), jnp.float32), -6.0, 6.0)
    columns = jnp.arange(NRG, dtype=jnp.int32)

    def one_date(pair):
        shifts, extra = pair
        full = jnp.repeat(jnp.repeat(shifts, BLK, axis=0), BLK, axis=1)
        index = columns[None, :] + IMAX - full
        index = jnp.broadcast_to(index[None], (2, AZ, NRG))
        return jnp.take_along_axis(scene, index, axis=2) + extra
    return lax.map(one_date, (table, noise)).astype(jnp.bfloat16)


def draw_partners(key, part):
    counts = jax.random.randint(jax.random.fold_in(key, 31), (DATES, 1), 2, SPAN + 1)
    scores = jax.random.randint(jax.random.fold_in(key, 32), (DATES, SPAN), 0, 1000) * SPAN + jnp.arange(SPAN, dtype=jnp.int32)[None, :]
    ranks = jnp.argsort(jnp.argsort(scores, axis=1), axis=1)
    return (ranks < counts).astype(jnp.int32)


def shard_levels(stream_key, shape, cuts, smallest, high):
    factor_of = 1.0
    for axis_at, parts in cuts:
        steps = jax.random.uniform(jax.random.fold_in(jax.random.fold_in(stream_key, 6), axis_at), (parts,), jnp.float32, smallest / len(cuts), high / len(cuts))
        factor_of = factor_of * jnp.repeat(jnp.exp(steps), shape[axis_at] // parts).reshape((-1,) + (1,) * (len(shape) - 1 - axis_at))
    return factor_of


def setup_inputs(seed: int = 0) -> dict:
    keys = jax.random.split(jax.random.key(seed), 6)
    slc = draw_slc(jax.random.fold_in(keys[5], 71), 0)
    ref_date = jax.random.randint(keys[1], (1,), 0, DATES).astype(jnp.int32)
    int_offset = draw_int_offset(jax.random.fold_in(keys[5], 71), 0)
    frac_offset = jnp.clip(1.0 * jax.random.uniform(keys[3], (DATES, AZ // BLK, NRG // BLK), jnp.float32) ** shard_levels(keys[3], (DATES, AZ // BLK, NRG // BLK), ((0, 8), (2, 4)), -0.2, 0.2), 0.0, 1.0)
    partners = draw_partners(jax.random.fold_in(keys[5], 71), 0)
    return {"slc": slc, "ref_date": ref_date, "int_offset": int_offset, "frac_offset": frac_offset, "partners": partners}


HIGHEST = lax.Precision.HIGHEST

def dft_tables(block, lags, factor):
    index = jnp.arange(block, dtype=jnp.int32)
    phase = index[:, None] * index[None, :] % block
    angle = 2.0 * jnp.pi / block * phase.astype(jnp.float32)
    upsampled = factor * block
    signed = jnp.where(index < block // 2, index, index - block)
    lag_index = jnp.arange(lags, dtype=jnp.int32) - lags // 2
    lag_phase = lag_index[:, None] * signed[None, :] % upsampled
    lag_angle = 2.0 * jnp.pi / upsampled * lag_phase.astype(jnp.float32)
    return (jnp.cos(angle), jnp.sin(angle), jnp.cos(lag_angle), jnp.sin(lag_angle))

def amplitude(slab):
    real_part = slab[0].astype(jnp.float32)
    imag_part = slab[1].astype(jnp.float32)
    return jnp.sqrt(real_part * real_part + imag_part * imag_part + 1e-06).astype(jnp.bfloat16)

def prepare(amplitude_map, block):
    rows, cols = amplitude_map.shape
    blocks = amplitude_map.astype(jnp.float32).reshape(rows // block, block, cols // block, block)
    blocks = blocks.transpose(0, 2, 1, 3)
    centered = blocks - lax.optimization_barrier(jnp.mean(blocks, axis=(2, 3), keepdims=True))
    energy = lax.optimization_barrier(jnp.sum(centered * centered, axis=(2, 3)))
    return (centered, energy)

def spectra(centered, cosine, sine):
    first_real = jnp.einsum('kn,abnm->abkm', cosine, centered, precision=HIGHEST)
    first_imag = -jnp.einsum('kn,abnm->abkm', sine, centered, precision=HIGHEST)
    real_part = jnp.einsum('abkn,ln->abkl', first_real, cosine, precision=HIGHEST) + jnp.einsum('abkn,ln->abkl', first_imag, sine, precision=HIGHEST)
    imag_part = jnp.einsum('abkn,ln->abkl', first_imag, cosine, precision=HIGHEST) - jnp.einsum('abkn,ln->abkl', first_real, sine, precision=HIGHEST)
    return (real_part, imag_part)

def correlate(own_amplitude, ref_amplitude):
    cosine, sine, lag_cos, lag_sin = dft_tables(BLK, LAGS, OVS)
    own_blocks, own_energy = prepare(own_amplitude, BLK)
    ref_blocks, ref_energy = prepare(ref_amplitude, BLK)
    own_real, own_imag = spectra(own_blocks, cosine, sine)
    ref_real, ref_imag = spectra(ref_blocks, cosine, sine)
    cross_real = own_real * ref_real + own_imag * ref_imag
    cross_imag = own_imag * ref_real - own_real * ref_imag
    left_real = jnp.einsum('mk,abkl->abml', lag_cos, cross_real, precision=HIGHEST) - jnp.einsum('mk,abkl->abml', lag_sin, cross_imag, precision=HIGHEST)
    left_imag = jnp.einsum('mk,abkl->abml', lag_cos, cross_imag, precision=HIGHEST) + jnp.einsum('mk,abkl->abml', lag_sin, cross_real, precision=HIGHEST)
    values = jnp.einsum('abml,nl->abmn', left_real, lag_cos, precision=HIGHEST) - jnp.einsum('abml,nl->abmn', left_imag, lag_sin, precision=HIGHEST)
    scale = BLK * jnp.sqrt(own_energy * ref_energy + 1e-06)
    values = values / scale[:, :, None, None]
    return values.reshape(values.shape[0], values.shape[1], LAGS * LAGS)

def resample(padded, shifts, fractions, block, rim):
    block_rows, block_cols = shifts.shape
    row_start = jnp.broadcast_to((jnp.arange(block_rows, dtype=jnp.int32) * block)[:, None], (block_rows, block_cols)).reshape(-1)
    col_start = ((jnp.arange(block_cols, dtype=jnp.int32) * block)[None, :] + shifts.astype(jnp.int32) + (rim - 3)).reshape(-1)
    anchor = jnp.zeros((), jnp.int32)

    def tile(row, col):
        return lax.dynamic_slice(padded, (anchor, row, col), (2, block, block + 7))
    tiles = jax.vmap(tile)(row_start, col_start)
    distance = jnp.arange(8, dtype=jnp.float32)[None, :] - 3.0 - fractions.reshape(-1)[:, None]
    weights = jnp.sinc(distance) * (0.5 + 0.5 * jnp.cos(jnp.pi * distance / 4.0))
    result = weights[:, 0, None, None, None] * tiles[..., 0:block].astype(jnp.float32)
    for tap in range(1, 8):
        result = result + weights[:, tap, None, None, None] * tiles[..., tap:tap + block].astype(jnp.float32)
    result = result.reshape(block_rows, block_cols, 2, block, block).transpose(2, 0, 3, 1, 4)
    return result.reshape(2, block_rows * block, block_cols * block).astype(jnp.bfloat16)

def boxcar(field, box_rows, box_cols):
    half = box_rows // 2
    padded = jnp.pad(field, ((half, half), (0, 0)))
    rows = field.shape[0]
    summed = padded[0:rows]
    for offset in range(1, box_rows):
        summed = summed + padded[offset:offset + rows]
    width = field.shape[1] - (box_cols - 1)
    total = summed[:, 0:width]
    for offset in range(1, box_cols):
        total = total + summed[:, offset:offset + width]
    return total

def coherence_map(own_ext, partner_ext, weight):
    own_real = own_ext[0].astype(jnp.float32)
    own_imag = own_ext[1].astype(jnp.float32)
    other_real = partner_ext[0].astype(jnp.float32)
    other_imag = partner_ext[1].astype(jnp.float32)
    box_re = boxcar(own_real * other_real + own_imag * other_imag, BOXA, BOXR)
    box_im = boxcar(own_imag * other_real - own_real * other_imag, BOXA, BOXR)
    box_own = boxcar(own_real * own_real + own_imag * own_imag, BOXA, BOXR)
    box_partner = boxcar(other_real * other_real + other_imag * other_imag, BOXA, BOXR)
    value = weight.astype(jnp.float32) * (box_re * box_re + box_im * box_im) / (box_own * box_partner + 1e-06)
    return value.astype(jnp.bfloat16)

def reference(slc, ref_date, int_offset, frac_offset, partners):
    amplitudes = lax.map(amplitude, slc)
    ref_amplitude = lax.dynamic_index_in_dim(amplitudes, ref_date[0], 0, keepdims=False)
    surfaces = lax.map(lambda own: correlate(own, ref_amplitude), amplitudes)
    rim = IMAX + 4

    def resample_date(triple):
        slab, shifts, fractions = triple
        padded = jnp.pad(slab, ((0, 0), (0, 0), (rim, rim)))
        return resample(padded, shifts, fractions, BLK, rim)
    resampled = lax.map(resample_date, (slc, int_offset, frac_offset))
    half = BOXR // 2
    extended = jnp.pad(resampled, ((0, 0), (0, 0), (0, 0), (half, half)))
    results = []
    for ahead in range(1, SPAN + 1):
        partner = jnp.concatenate([extended[ahead:], jnp.zeros_like(extended[:ahead])], axis=0)
        results.append(lax.map(lambda triple: coherence_map(triple[0], triple[1], triple[2]), (extended, partner, partners[:, ahead - 1])))
    return (surfaces, jnp.stack(results, axis=1))
```

```python
import jax
import jax.numpy as jnp
import numpy as np
from jax import lax
from jax.experimental import pallas as pl
from jax.experimental.pallas import tpu as pltpu
from jax.sharding import PartitionSpec as P

BLK = 64
OVS = 2
LAGS = 32
SPAN = 4
BOXA = 5
BOXR = 19
TAPS = 8
LANES = 128
PAD = 16
EDGE = 32
F32 = jnp.float32
BF16 = jnp.bfloat16
HIGHEST = lax.Precision.HIGHEST
VMEM = pl.BlockSpec(memory_space=pltpu.VMEM)
SMEM = pl.BlockSpec(memory_space=pltpu.SMEM)


def dot(a, b):
    return jnp.dot(a, b, preferred_element_type=F32)


def iota(shape, dim):
    return lax.broadcasted_iota(jnp.int32, shape, dim)


def band(table):
    top = 96
    rows = 2 * LANES - top
    step = iota((rows, LANES), 0) + top - iota((rows, LANES), 1) - (LANES - PAD - 3)
    step = step.astype(F32) - table[TAPS : TAPS + 1, :]
    out = jnp.zeros((rows, LANES), F32)
    for tap in range(TAPS):
        out = jnp.where(step == float(tap), table[tap : tap + 1, :], out)
    return jnp.concatenate([jnp.zeros((top, LANES), BF16), out.astype(BF16)], axis=0)


def prep_kernel(slc_ref, off_ref, frac_ref, res_ref, amp_ref, low_ref, high_ref):
    _, rows, cols = slc_ref.shape
    blocks = cols // BLK
    tiles = cols // LANES
    real = slc_ref[0].astype(F32)
    imag = slc_ref[1].astype(F32)
    amp_ref[...] = jnp.sqrt(real * real + imag * imag + 1e-06).astype(BF16)
    dist = iota((TAPS, blocks), 0).astype(F32) - 3.0 - frac_ref[...]
    arg = jnp.pi * dist
    sinc = jnp.where(arg == 0.0, 1.0, jnp.sin(arg) / jnp.where(arg == 0.0, 1.0, arg))
    weights = sinc * (0.5 + 0.5 * jnp.cos(arg / 4.0))
    shifts = jnp.broadcast_to(off_ref[...].astype(F32), (TAPS, blocks))
    small = jnp.concatenate([weights, shifts], axis=0).astype(BF16)
    place = (iota((blocks, cols), 1) - PAD) >> 6 == iota((blocks, cols), 0)
    table = dot(small, place.astype(BF16))
    ends = iota((blocks, 2 * LANES), 0) == jnp.where(iota((blocks, 2 * LANES), 1) < LANES, 0, blocks - 1)
    ends = dot(small, ends.astype(BF16)).astype(BF16)
    low_ref[0 : 2 * rows, :] = slc_ref[:, :, 0:LANES].reshape(2 * rows, LANES)
    low_ref[2 * rows :, :] = ends[:, 0:LANES]
    high_ref[0 : 2 * rows, :] = slc_ref[:, :, cols - LANES :].reshape(2 * rows, LANES)
    high_ref[2 * rows :, :] = ends[:, LANES:]
    for p in range(tiles):
        taps = band(table[:, p * LANES : (p + 1) * LANES])
        if p == 0:
            window, taps = slc_ref[:, :, 0:LANES], taps[LANES:]
        else:
            window = slc_ref[:, :, (p - 1) * LANES : (p + 1) * LANES]
        out = dot(window.reshape(2 * rows, window.shape[2]), taps)
        res_ref[:, :, p * LANES : (p + 1) * LANES] = out.astype(BF16).reshape(2, rows, LANES)


def edge_kernel(low_ref, high_ref, left_ref, right_ref, out_ref):
    rows = out_ref.shape[0]
    lane = iota((2 * TAPS, LANES), 1)

    def tile(before, after):
        table = jnp.where(lane < PAD, before[2 * rows :, :].astype(F32), after[2 * rows :, :].astype(F32))
        window = jnp.concatenate([before[0 : 2 * rows, :], after[0 : 2 * rows, :]], axis=1)
        return dot(window, band(table))

    first = tile(left_ref, low_ref)
    last = pltpu.roll(tile(high_ref, right_ref), EDGE, 1)
    lane = iota((2 * rows, LANES), 1)
    both = jnp.where(lane < EDGE, first, jnp.where(lane < 2 * EDGE, last, 0.0))
    out_ref[...] = (both[0:rows] + pltpu.roll(both[rows:], 2 * EDGE, 1)).astype(BF16)


def range_box():
    gap = iota((2 * LANES, LANES), 0) - iota((2 * LANES, LANES), 1) - PAD
    return (jnp.abs(gap) <= BOXR // 2).astype(BF16)


def line_box(field):
    rows, lanes = field.shape
    base = jnp.concatenate([field, jnp.zeros((8, lanes), F32)], axis=0)
    two = base + pltpu.roll(base, 1, 0)
    four = two + pltpu.roll(two, 2, 0)
    five = four + pltpu.roll(base, 4, 0)
    return pltpu.roll(five, rows + 8 - BOXA // 2, 0)[0:rows]


def extended(main_ref, edge_ref, p):
    tiles = main_ref.shape[2] // LANES
    if 0 < p < tiles:
        return tuple(main_ref[c, :, p * LANES : (p + 1) * LANES].astype(F32) for c in range(2))
    edge = edge_ref[...].astype(F32)
    lane = iota(edge.shape, 1)
    if p == 0:
        inner = [main_ref[c, :, 0:LANES].astype(F32) for c in range(2)]
        outer = [edge, pltpu.roll(edge, LANES - 2 * EDGE, 1)]
    else:
        inner = [jnp.zeros(edge.shape, F32)] * 2
        outer = [pltpu.roll(edge, LANES - EDGE, 1), pltpu.roll(edge, LANES - 3 * EDGE, 1)]
    return tuple(jnp.where(lane < EDGE, o, i) for o, i in zip(outer, inner))


def coherence_kernel(count, *refs):
    flag_ref, own_ref, own_edge_ref = refs[0:3]
    others = refs[3 : 3 + 2 * count]
    out_ref, fields_ref = refs[3 + 2 * count :]
    _, rows, cols = own_ref.shape
    tiles = cols // LANES
    for p in range(tiles + 1):
        lanes = slice(p * LANES, (p + 1) * LANES)
        own_r, own_i = extended(own_ref, own_edge_ref, p)
        fields_ref[0:rows, lanes] = (own_r * own_r + own_i * own_i).astype(BF16)
        for h in range(count):
            r, i = extended(others[2 * h], others[2 * h + 1], p)
            at = rows * (1 + 3 * h)
            fields_ref[at : at + rows, lanes] = (own_r * r + own_i * i).astype(BF16)
            fields_ref[at + rows : at + 2 * rows, lanes] = (own_i * r - own_r * i).astype(BF16)
            fields_ref[at + 2 * rows : at + 3 * rows, lanes] = (r * r + i * i).astype(BF16)
    box = range_box()
    for p in range(tiles):
        sums = dot(fields_ref[:, p * LANES : (p + 2) * LANES], box)
        own = line_box(sums[0:rows])
        for h in range(count):
            at = rows * (1 + 3 * h)
            re = line_box(sums[at : at + rows])
            im = line_box(sums[at + rows : at + 2 * rows])
            partner = line_box(sums[at + 2 * rows : at + 3 * rows])
            value = flag_ref[0, h].astype(F32) * (re * re + im * im) / (own * partner + 1e-06)
            out_ref[h, :, p * LANES : (p + 1) * LANES] = value.astype(BF16)


def split(table):
    high = table.astype(BF16)
    return high, (table - high.astype(np.float32)).astype(BF16)


def twice(table):
    zero = np.zeros_like(table)
    return np.block([[table, zero], [zero, table]])


def surface_tables():
    index = np.arange(BLK)
    angle = 2.0 * np.pi / BLK * (index[:, None] * index[None, :] % BLK)
    cosine, sine = np.cos(angle).astype(np.float32), np.sin(angle).astype(np.float32)
    signed = np.where(index < BLK // 2, index, index - BLK)
    upsampled = OVS * BLK
    lag_phase = (np.arange(LAGS) - LAGS // 2)[:, None] * signed[None, :] % upsampled
    lag_angle = 2.0 * np.pi / upsampled * lag_phase
    lag_cos, lag_sin = np.cos(lag_angle).astype(np.float32), np.sin(lag_angle).astype(np.float32)
    high, low = split(np.concatenate([cosine, -sine], axis=0))
    first = np.concatenate([high, low, high], axis=1)
    second = np.concatenate(split(np.concatenate([twice(cosine), twice(sine)], axis=1)), axis=0)
    per = LANES // LAGS
    order = np.arange(LAGS).reshape(LAGS // per, per).T.reshape(-1)
    left = np.block([[lag_cos[order], -lag_sin[order]], [lag_sin[order], lag_cos[order]]])
    third = np.concatenate(split(left), axis=1)
    spread = [twice(np.tile(table.T, (1, per))) for table in (lag_cos, -lag_sin)]
    fourth = np.concatenate(split(np.concatenate(spread, axis=0)), axis=0)
    return first, second, third, fourth


def surface_kernel(own_ref, ref_ref, first_ref, second_ref, third_ref, fourth_ref, out_ref, rows_ref, out_scr):
    size, cols = own_ref.shape
    tiles = cols // LANES
    group = (iota((LANES, LANES), 0) >> 6 == iota((LANES, LANES), 1) >> 6).astype(F32)
    sources = (own_ref, ref_ref)

    def tile_of(s, p):
        return sources[s][:, p * LANES : (p + 1) * LANES].astype(F32)

    for s in range(2):
        for p in range(tiles):
            rows_ref[s * tiles + p : s * tiles + p + 1, :] = jnp.sum(tile_of(s, p), axis=0, keepdims=True)
    mean = jnp.dot(rows_ref[...], group, precision=HIGHEST) / (BLK * BLK)
    centered = []
    for s in range(2):
        for p in range(tiles):
            value = tile_of(s, p) - mean[s * tiles + p : s * tiles + p + 1, :]
            rows_ref[s * tiles + p : s * tiles + p + 1, :] = jnp.sum(value * value, axis=0, keepdims=True)
            centered.append(value)
    energy = jnp.dot(rows_ref[...], group, precision=HIGHEST)
    scale = 1.0 / (BLK * jnp.sqrt(energy[0:tiles] * energy[tiles:] + 1e-06))

    def spectrum(value):
        high = value.astype(BF16)
        low = (value - high.astype(F32)).astype(BF16)
        f = dot(first_ref[...], jnp.concatenate([high, high, low], axis=0)).astype(BF16)
        s = dot(jnp.concatenate([f, f], axis=1), second_ref[...])
        return (
            s[0:size, 0:LANES] + s[size:, LANES:],
            s[size:, 0:LANES] - s[0:size, LANES:],
        )

    lag_rows = [[] for _ in range(LANES // LAGS)]
    for p in range(tiles):
        own_r, own_i = spectrum(centered[p])
        ref_r, ref_i = spectrum(centered[tiles + p])
        by = scale[p : p + 1, :]
        cross = jnp.concatenate(
            [(own_r * ref_r + own_i * ref_i) * by, (own_i * ref_r - own_r * ref_i) * by], axis=0
        ).astype(BF16)
        lags = dot(third_ref[...], jnp.concatenate([cross, cross], axis=0))
        for q in range(LANES // LAGS):
            part = [lags[ri * LAGS + q * 8 : ri * LAGS + q * 8 + 8] for ri in range(2)]
            lag_rows[q].append(jnp.concatenate(part, axis=1))
    lhs = jnp.concatenate([row for rows in lag_rows for row in rows], axis=0).astype(BF16)
    result = dot(jnp.concatenate([lhs, lhs], axis=1), fourth_ref[...])
    height = 8 * tiles
    quarter = iota((height, 2 * LANES), 1) % LANES // LAGS
    total = result[0:height]
    for q in range(1, LANES // LAGS):
        total = jnp.where(quarter == q, result[q * height : (q + 1) * height], total)
    for p in range(tiles):
        for jj in range(2):
            at = (2 * p + jj) * 8
            out_scr[at : at + 8, :] = total[p * 8 : p * 8 + 8, jj * LANES : (jj + 1) * LANES]
    for a in range(8):
        out_ref[:, a * LANES : (a + 1) * LANES] = out_scr[pl.ds(a, 2 * tiles, stride=8), :]


def shifted(value, axis, steps):
    count = lax.axis_size(axis)
    pairs = [(s, s - steps) for s in range(count) if 0 <= s - steps < count]
    return lax.ppermute(value, axis, pairs)


def from_root(value, axis, root):
    count = lax.axis_size(axis)
    value = jnp.where(lax.axis_index(axis) == root, value, jnp.zeros_like(value))
    if count & (count - 1):
        return lax.psum(value, axis)
    step = 1
    while step < count:
        value = jnp.maximum(value, lax.ppermute(value, axis, [(s, s ^ step) for s in range(count)]))
        step *= 2
    return value


def cost(flops, size):
    return pl.CostEstimate(flops=flops, bytes_accessed=size, transcendentals=0)


def body(slc, ref_date, int_offset, frac_offset, partners):
    own = slc[0]
    _, rows, cols = own.shape
    sds = jax.ShapeDtypeStruct
    payload = sds((2 * rows + 2 * TAPS, LANES), BF16)
    main, amp, low, high = pl.pallas_call(
        prep_kernel,
        out_shape=(sds(own.shape, BF16), sds((rows, cols), BF16), payload, payload),
        in_specs=[VMEM] * 3,
        out_specs=(VMEM,) * 4,
        cost_estimate=cost(2 * 128 * 256 * cols, 1 << 20),
        name="prepare",
    )(own, int_offset[0], frac_offset[0])
    right = shifted(low, "rng", 1)
    left = shifted(high, "rng", -1)
    two = shifted(main, "date", 2)
    one = shifted(main, "date", 1)
    edge = pl.pallas_call(
        edge_kernel,
        out_shape=sds((rows, LANES), BF16),
        in_specs=[VMEM] * 4,
        out_specs=VMEM,
        name="edges",
    )(low, high, left, right)
    mains = [one, two, shifted(two, "date", 1), shifted(two, "date", 2)]
    edges = [shifted(edge, "date", h) for h in range(1, SPAN + 1)]
    ref_amp = from_root(amp, "date", ref_date[0])
    tables = [jnp.asarray(t) for t in surface_tables()]
    surface = pl.pallas_call(
        surface_kernel,
        out_shape=sds((cols // BLK, LAGS * LAGS), F32),
        in_specs=[VMEM] * 6,
        out_specs=VMEM,
        scratch_shapes=[
            pltpu.VMEM((2 * cols // LANES, LANES), F32),
            pltpu.VMEM((8 * cols // BLK, LANES), F32),
        ],
        name="surface",
    )(amp, ref_amp, *tables)
    operands = [v for pair in zip(mains, edges) for v in pair]
    coherence = pl.pallas_call(
        lambda *refs: coherence_kernel(SPAN, *refs),
        out_shape=sds((SPAN, rows, cols), BF16),
        in_specs=[SMEM] + [VMEM] * (2 + 2 * SPAN),
        out_specs=VMEM,
        scratch_shapes=[pltpu.VMEM(((1 + 3 * SPAN) * rows, cols + LANES), BF16)],
        name="coherence",
    )(partners, main, edge, *operands)
    return (surface[None, None], coherence[None])


def solution(mesh):
    in_specs = (
        P("date", None, None, "rng"),
        P(),
        P("date", None, "rng"),
        P("date", None, "rng"),
        P("date", None),
    )
    out_specs = (P("date", None, "rng", None), P("date", None, None, "rng"))
    return jax.shard_map(body, mesh=mesh, in_specs=in_specs, out_specs=out_specs, check_vma=False)
```

```python
import jax
import jax.numpy as jnp
import numpy as np
from jax import lax
from jax.experimental import pallas as pl
from jax.experimental.pallas import tpu as pltpu
from jax.sharding import PartitionSpec as P

BLK = 64
OVS = 2
LAGS = 32
SPAN = 4
BOXA = 5
BOXR = 19
TAPS = 8
LANES = 128
PAD = 16
EDGE = 32
F32 = jnp.float32
BF16 = jnp.bfloat16
HIGHEST = lax.Precision.HIGHEST
VMEM = pl.BlockSpec(memory_space=pltpu.VMEM)
SMEM = pl.BlockSpec(memory_space=pltpu.SMEM)
PARAMS = pltpu.CompilerParams(vmem_limit_bytes=8 << 20)


def dot(a, b):
    return jnp.dot(a, b, preferred_element_type=F32)


def iota(shape, dim):
    return lax.broadcasted_iota(jnp.int32, shape, dim)


def band(table):
    top = 96
    rows = 2 * LANES - top
    step = iota((rows, LANES), 0) + top - iota((rows, LANES), 1) - (LANES - PAD - 3)
    step = step.astype(F32) - table[TAPS : TAPS + 1, :]
    out = jnp.zeros((rows, LANES), F32)
    for tap in range(TAPS):
        out = jnp.where(step == float(tap), table[tap : tap + 1, :], out)
    return jnp.concatenate([jnp.zeros((top, LANES), BF16), out.astype(BF16)], axis=0)


def prep_kernel(slc_ref, off_ref, frac_ref, res_ref, amp_ref, low_ref, high_ref):
    _, rows, cols = slc_ref.shape
    blocks = cols // BLK
    tiles = cols // LANES
    real = slc_ref[0].astype(F32)
    imag = slc_ref[1].astype(F32)
    amp_ref[...] = jnp.sqrt(real * real + imag * imag + 1e-06).astype(BF16)
    dist = iota((TAPS, blocks), 0).astype(F32) - 3.0 - frac_ref[...]
    arg = jnp.pi * dist
    sinc = jnp.where(arg == 0.0, 1.0, jnp.sin(arg) / jnp.where(arg == 0.0, 1.0, arg))
    weights = sinc * (0.5 + 0.5 * jnp.cos(arg / 4.0))
    shifts = jnp.broadcast_to(off_ref[...].astype(F32), (TAPS, blocks))
    small = jnp.concatenate([weights, shifts], axis=0).astype(BF16)
    place = (iota((blocks, cols), 1) - PAD) >> 6 == iota((blocks, cols), 0)
    table = dot(small, place.astype(BF16))
    ends = iota((blocks, 2 * LANES), 0) == jnp.where(iota((blocks, 2 * LANES), 1) < LANES, 0, blocks - 1)
    ends = dot(small, ends.astype(BF16)).astype(BF16)
    low_ref[0 : 2 * rows, :] = slc_ref[:, :, 0:LANES].reshape(2 * rows, LANES)
    low_ref[2 * rows :, :] = ends[:, 0:LANES]
    high_ref[0 : 2 * rows, :] = slc_ref[:, :, cols - LANES :].reshape(2 * rows, LANES)
    high_ref[2 * rows :, :] = ends[:, LANES:]
    for p in range(tiles):
        taps = band(table[:, p * LANES : (p + 1) * LANES])
        if p == 0:
            window, taps = slc_ref[:, :, 0:LANES], taps[LANES:]
        else:
            window = slc_ref[:, :, (p - 1) * LANES : (p + 1) * LANES]
        out = dot(window.reshape(2 * rows, window.shape[2]), taps)
        res_ref[p] = out[0:rows].astype(BF16)
        res_ref[tiles + p] = out[rows:].astype(BF16)


def edge_kernel(keep_ref, low_ref, high_ref, left_ref, right_ref, out_ref):
    rows = out_ref.shape[1]
    lane = iota((2 * TAPS, LANES), 1)
    outside = [keep_ref[0, k] == 0 for k in range(2)]
    left_ref = jnp.where(outside[0], jnp.zeros_like(left_ref), left_ref[...])
    right_ref = jnp.where(outside[1], jnp.zeros_like(right_ref), right_ref[...])

    def tile(before, after):
        table = jnp.where(lane < PAD, before[2 * rows :, :].astype(F32), after[2 * rows :, :].astype(F32))
        window = jnp.concatenate([before[0 : 2 * rows, :], after[0 : 2 * rows, :]], axis=1)
        return dot(window, band(table))

    first = tile(left_ref, low_ref)
    last = pltpu.roll(tile(high_ref, right_ref), EDGE, 1)
    lane = iota((2 * rows, LANES), 1)
    both = jnp.where(lane < EDGE, first, jnp.where(lane < 2 * EDGE, last, 0.0))
    out_ref[0] = (both[0:rows] + pltpu.roll(both[rows:], 2 * EDGE, 1)).astype(BF16)


def range_box():
    gap = iota((2 * LANES, LANES), 0) - iota((2 * LANES, LANES), 1) - PAD
    return (jnp.abs(gap) <= BOXR // 2).astype(BF16)


def line_box(field):
    rows, lanes = field.shape
    base = jnp.concatenate([field, jnp.zeros((8, lanes), F32)], axis=0)
    two = base + pltpu.roll(base, 1, 0)
    four = two + pltpu.roll(two, 2, 0)
    five = four + pltpu.roll(base, 4, 0)
    return pltpu.roll(five, rows + 8 - BOXA // 2, 0)[0:rows]


def extended(main_ref, edge_ref, p):
    tiles = main_ref.shape[0] // 2
    if 0 < p < tiles:
        return tuple(main_ref[c * tiles + p].astype(F32) for c in range(2))
    edge = edge_ref[0].astype(F32)
    lane = iota(edge.shape, 1)
    if p == 0:
        inner = [main_ref[c * tiles].astype(F32) for c in range(2)]
        outer = [edge, pltpu.roll(edge, LANES - 2 * EDGE, 1)]
    else:
        inner = [jnp.zeros(edge.shape, F32)] * 2
        outer = [pltpu.roll(edge, LANES - EDGE, 1), pltpu.roll(edge, LANES - 3 * EDGE, 1)]
    return tuple(jnp.where(lane < EDGE, o, i) for o, i in zip(outer, inner))


def pair_kernel(first, flag_ref, own_ref, own_edge_ref, main_ref, edge_ref, *refs):
    if first:
        out_ref, power_ref, fields_ref = refs
    else:
        power_ref, out_ref, fields_ref = refs
    rows, cols = out_ref.shape
    tiles = cols // LANES
    for p in range(tiles + 1):
        lanes = slice(p * LANES, (p + 1) * LANES)
        own_r, own_i = extended(own_ref, own_edge_ref, p)
        r, i = extended(main_ref, edge_ref, p)
        fields_ref[0:rows, lanes] = (own_r * r + own_i * i).astype(BF16)
        fields_ref[rows : 2 * rows, lanes] = (own_i * r - own_r * i).astype(BF16)
        fields_ref[2 * rows : 3 * rows, lanes] = (r * r + i * i).astype(BF16)
        if first:
            fields_ref[3 * rows :, lanes] = (own_r * own_r + own_i * own_i).astype(BF16)
    box = range_box()
    flag = flag_ref[0].astype(F32)
    for p in range(tiles):
        lanes = slice(p * LANES, (p + 1) * LANES)
        sums = dot(fields_ref[:, p * LANES : (p + 2) * LANES], box)
        if first:
            power_ref[:, lanes] = line_box(sums[3 * rows :])
        re = line_box(sums[0:rows])
        im = line_box(sums[rows : 2 * rows])
        partner = line_box(sums[2 * rows : 3 * rows])
        value = flag * (re * re + im * im) / (power_ref[:, lanes] * partner + 1e-06)
        out_ref[:, lanes] = value.astype(BF16)


def first_kernel(*refs):
    pair_kernel(True, *refs)


def next_kernel(*refs):
    pair_kernel(False, *refs)


def last_kernel(odd_ref, flag_ref, own_ref, own_edge_ref, main_ref, edge_ref, power_ref, *refs):
    two_ref, cross_ref, four_ref, out_ref, tail_ref, fields_ref = refs
    pair_kernel(False, flag_ref, own_ref, own_edge_ref, main_ref, edge_ref, power_ref, tail_ref, fields_ref)
    odd = odd_ref[0] == 1
    tail, cross = tail_ref[...], cross_ref[...]
    out_ref[0] = jnp.where(odd, cross, tail)
    out_ref[1] = two_ref[...]
    out_ref[2] = jnp.where(odd, tail, cross)
    out_ref[3] = four_ref[...]


def split(table):
    high = table.astype(BF16)
    return high, (table - high.astype(np.float32)).astype(BF16)


def twice(table):
    zero = np.zeros_like(table)
    return np.block([[table, zero], [zero, table]])


def surface_tables():
    index = np.arange(BLK)
    angle = 2.0 * np.pi / BLK * (index[:, None] * index[None, :] % BLK)
    cosine, sine = np.cos(angle).astype(np.float32), np.sin(angle).astype(np.float32)
    signed = np.where(index < BLK // 2, index, index - BLK)
    upsampled = OVS * BLK
    lag_phase = (np.arange(LAGS) - LAGS // 2)[:, None] * signed[None, :] % upsampled
    lag_angle = 2.0 * np.pi / upsampled * lag_phase
    lag_cos, lag_sin = np.cos(lag_angle).astype(np.float32), np.sin(lag_angle).astype(np.float32)
    high, low = split(np.concatenate([cosine, -sine], axis=0))
    first = np.concatenate([high, low, high], axis=1)
    second = np.concatenate(split(np.concatenate([twice(cosine), twice(sine)], axis=1)), axis=0)
    per = LANES // LAGS
    order = np.arange(LAGS).reshape(LAGS // per, per).T.reshape(-1)
    left = np.block([[lag_cos[order], -lag_sin[order]], [lag_sin[order], lag_cos[order]]])
    third = np.concatenate(split(left), axis=1)
    spread = [twice(np.tile(table.T, (1, per))) for table in (lag_cos, -lag_sin)]
    fourth = np.concatenate(split(np.concatenate(spread, axis=0)), axis=0)
    return first, second, third, fourth


def surface_kernel(own_ref, ref_ref, first_ref, second_ref, third_ref, fourth_ref, out_ref, rows_ref, out_scr):
    size, cols = own_ref.shape
    tiles = cols // LANES
    group = (iota((LANES, LANES), 0) >> 6 == iota((LANES, LANES), 1) >> 6).astype(F32)
    sources = (own_ref, ref_ref)

    def tile_of(s, p):
        return sources[s][:, p * LANES : (p + 1) * LANES].astype(F32)

    for s in range(2):
        for p in range(tiles):
            rows_ref[s * tiles + p : s * tiles + p + 1, :] = jnp.sum(tile_of(s, p), axis=0, keepdims=True)
    mean = jnp.dot(rows_ref[...], group, precision=HIGHEST) / (BLK * BLK)
    centered = []
    for s in range(2):
        for p in range(tiles):
            value = tile_of(s, p) - mean[s * tiles + p : s * tiles + p + 1, :]
            rows_ref[s * tiles + p : s * tiles + p + 1, :] = jnp.sum(value * value, axis=0, keepdims=True)
            centered.append(value)
    energy = jnp.dot(rows_ref[...], group, precision=HIGHEST)
    scale = 1.0 / (BLK * jnp.sqrt(energy[0:tiles] * energy[tiles:] + 1e-06))

    def spectrum(value):
        high = value.astype(BF16)
        low = (value - high.astype(F32)).astype(BF16)
        f = dot(first_ref[...], jnp.concatenate([high, high, low], axis=0)).astype(BF16)
        s = dot(jnp.concatenate([f, f], axis=1), second_ref[...])
        return (
            s[0:size, 0:LANES] + s[size:, LANES:],
            s[size:, 0:LANES] - s[0:size, LANES:],
        )

    lag_rows = [[] for _ in range(LANES // LAGS)]
    for p in range(tiles):
        own_r, own_i = spectrum(centered[p])
        ref_r, ref_i = spectrum(centered[tiles + p])
        by = scale[p : p + 1, :]
        cross = jnp.concatenate(
            [(own_r * ref_r + own_i * ref_i) * by, (own_i * ref_r - own_r * ref_i) * by], axis=0
        ).astype(BF16)
        lags = dot(third_ref[...], jnp.concatenate([cross, cross], axis=0))
        for q in range(LANES // LAGS):
            part = [lags[ri * LAGS + q * 8 : ri * LAGS + q * 8 + 8] for ri in range(2)]
            lag_rows[q].append(jnp.concatenate(part, axis=1))
    lhs = jnp.concatenate([row for rows in lag_rows for row in rows], axis=0).astype(BF16)
    result = dot(jnp.concatenate([lhs, lhs], axis=1), fourth_ref[...])
    height = 8 * tiles
    quarter = iota((height, 2 * LANES), 1) % LANES // LAGS
    total = result[0:height]
    for q in range(1, LANES // LAGS):
        total = jnp.where(quarter == q, result[q * height : (q + 1) * height], total)
    for p in range(tiles):
        for jj in range(2):
            at = (2 * p + jj) * 8
            out_scr[at : at + 8, :] = total[p * 8 : p * 8 + 8, jj * LANES : (jj + 1) * LANES]
    for a in range(8):
        out_ref[:, a * LANES : (a + 1) * LANES] = out_scr[pl.ds(a, 2 * tiles, stride=8), :]


def shifted(value, axis, steps):
    count = lax.axis_size(axis)
    return lax.ppermute(value, axis, [(s, (s - steps) % count) for s in range(count)])


def swapped(value, axis, step):
    return lax.ppermute(value, axis, [(s, s ^ step) for s in range(lax.axis_size(axis))])


def two_later(value, axis):
    count = lax.axis_size(axis)
    middle = {s: s + 2 if s % 4 > 1 else s - 2 for s in range(2, count - 2)}
    middle.update({0: 1, 1: 0, count - 2: count - 1, count - 1: count - 2})
    inner = lax.ppermute(value, axis, sorted(middle.items()))
    outer = swapped(value, axis, 2)
    return jnp.where(lax.axis_index(axis) % 4 < 2, outer, inner)


def from_root(value, axis, root):
    count = lax.axis_size(axis)
    value = jnp.where(lax.axis_index(axis) == root, value, jnp.zeros_like(value))
    if count & (count - 1):
        return lax.psum(value, axis)
    step = count // 2
    while step:
        value = jnp.maximum(value, swapped(value, axis, step))
        step //= 2
    return value


def cost(flops, size):
    return pl.CostEstimate(flops=flops, bytes_accessed=size, transcendentals=0)


def body(slc, ref_date, int_offset, frac_offset, partners):
    own = slc[0]
    _, rows, cols = own.shape
    tiles = cols // LANES
    sds = jax.ShapeDtypeStruct
    payload = sds((2 * rows + 2 * TAPS, LANES), BF16)
    main, amp, low, high = pl.pallas_call(
        prep_kernel,
        out_shape=(sds((2 * tiles, rows, LANES), BF16), sds((rows, cols), BF16), payload, payload),
        in_specs=[VMEM] * 3,
        out_specs=(VMEM,) * 4,
        compiler_params=PARAMS,
        name="prepare",
    )(own, int_offset[0], frac_offset[0])
    at = lax.axis_index("rng")
    keep = jnp.stack([at > 0, at < lax.axis_size("rng") - 1]).astype(jnp.int32)[None]
    ahead = lax.axis_index("date") + 1 + jnp.arange(SPAN, dtype=jnp.int32)
    flags = jnp.where(ahead < lax.axis_size("date"), partners[0], 0)
    odd = lax.axis_index("date") % 2
    beside = swapped(main, "date", 1)
    two = two_later(main, "date")
    cross = swapped(two, "date", 1)
    four = two_later(two, "date")
    four_cross = swapped(four, "date", 1)
    right = shifted(low, "rng", 1)
    left = shifted(high, "rng", -1)
    edge = pl.pallas_call(
        edge_kernel,
        out_shape=sds((1, rows, LANES), BF16),
        in_specs=[SMEM] + [VMEM] * 4,
        out_specs=VMEM,
        compiler_params=PARAMS,
        name="edges",
    )(keep, low, high, left, right)
    one_edge, two_edge, three_edge, four_edge = [shifted(edge, "date", h) for h in range(1, SPAN + 1)]
    ref_amp = from_root(amp, "date", ref_date[0])
    tables = [jnp.asarray(t) for t in surface_tables()]
    surface = pl.pallas_call(
        surface_kernel,
        out_shape=sds((cols // BLK, LAGS * LAGS), F32),
        in_specs=[VMEM] * 6,
        out_specs=VMEM,
        scratch_shapes=[
            pltpu.VMEM((2 * cols // LANES, LANES), F32),
            pltpu.VMEM((8 * cols // BLK, LANES), F32),
        ],
        compiler_params=PARAMS,
        name="surface",
    )(amp, ref_amp, *tables)

    def pair(kernel, name, flag, partner, partner_edge, extra, out_shape, fields, scratch=()):
        return pl.pallas_call(
            kernel,
            out_shape=out_shape,
            in_specs=[SMEM] * (2 if name == "last" else 1) + [VMEM] * (4 + len(extra)),
            out_specs=jax.tree.map(lambda _: VMEM, out_shape),
            scratch_shapes=[*scratch, pltpu.VMEM((fields * rows, cols + LANES), BF16)],
            compiler_params=PARAMS,
            name=name,
        )(*([odd[None]] if name == "last" else []), flag, main, edge, partner, partner_edge, *extra)

    field = sds((rows, cols), BF16)
    even = odd == 0
    coh_two, power = pair(
        first_kernel, "first", flags[1:2], two, two_edge, (), (field, sds((rows, cols), F32)), 4
    )
    coh_cross = pair(
        next_kernel,
        "cross",
        jnp.where(even, flags[2:3], flags[0:1]),
        cross,
        jnp.where(even, three_edge, one_edge),
        (power,),
        field,
        3,
    )
    coh_four = pair(next_kernel, "four", flags[3:4], four, four_edge, (power,), field, 3)
    coherence = pair(
        last_kernel,
        "last",
        jnp.where(even, flags[0:1], flags[2:3]),
        jnp.where(even, beside, four_cross),
        jnp.where(even, one_edge, three_edge),
        (power, coh_two, coh_cross, coh_four),
        sds((SPAN, rows, cols), BF16),
        3,
        (pltpu.VMEM((rows, cols), BF16),),
    )
    return (surface[None, None], coherence[None])


def solution(mesh):
    in_specs = (
        P("date", None, None, "rng"),
        P(),
        P("date", None, "rng"),
        P("date", None, "rng"),
        P("date", None),
    )
    out_specs = (P("date", None, "rng", None), P("date", None, None, "rng"))
    return jax.shard_map(body, mesh=mesh, in_specs=in_specs, out_specs=out_specs, check_vma=False)
```

```python
import functools

import jax
import jax.numpy as jnp
import numpy as np
from jax import lax
from jax.experimental import pallas as pl
from jax.experimental.pallas import tpu as pltpu
from jax.sharding import PartitionSpec as P

BLK = 64
OVS = 2
LAGS = 32
SPAN = 4
BOXA = 5
BOXR = 19
TAPS = 8
LANES = 128
PAD = 16
EDGE = 32
HROWS = 16
F32 = jnp.float32
BF16 = jnp.bfloat16
HIGHEST = lax.Precision.HIGHEST
VMEM = pl.BlockSpec(memory_space=pltpu.VMEM)
SMEM = pl.BlockSpec(memory_space=pltpu.SMEM)
PARAMS = pltpu.CompilerParams(vmem_limit_bytes=8 << 20)


def dot(a, b):
    return jnp.dot(a, b, preferred_element_type=F32)


def iota(shape, dim):
    return lax.broadcasted_iota(jnp.int32, shape, dim)


def band(table):
    top = 96
    rows = 2 * LANES - top
    step = iota((rows, LANES), 0) + top - iota((rows, LANES), 1) - (LANES - PAD - 3)
    step = step.astype(F32) - table[TAPS : TAPS + 1, :]
    out = jnp.zeros((rows, LANES), F32)
    for tap in range(TAPS):
        out = jnp.where(step == float(tap), table[tap : tap + 1, :], out)
    return jnp.concatenate([jnp.zeros((top, LANES), BF16), out.astype(BF16)], axis=0)


def amplitude(real, imag):
    real, imag = real.astype(F32), imag.astype(F32)
    return jnp.sqrt(real * real + imag * imag + 1e-06).astype(BF16)


EVEN, LEFT, RIGHT, PICK = 4, 5, 6, 8


def prep_kernel(
    own_hbm, off_hbm, frac_hbm, ref_hbm, partners_hbm, own_ref, cond_ref, taps_ref, low_ref, high_ref, *scratch
):
    off_ref, frac_ref, ref_ref, partners_ref, sems = scratch
    sources = (own_hbm, off_hbm, frac_hbm, ref_hbm, partners_hbm)
    targets = (own_ref, off_ref, frac_ref, ref_ref, partners_ref)
    copies = [pltpu.make_async_copy(s, t, sems.at[k]) for k, (s, t) in enumerate(zip(sources, targets))]
    for copy in copies:
        copy.start()
    for copy in copies[1:]:
        copy.wait()
    rows, cols = own_ref.shape[0] // 2, own_ref.shape[1]
    blocks = cols // BLK
    date, dates = lax.axis_index("date"), lax.axis_size("date")
    place, places = lax.axis_index("rng"), lax.axis_size("rng")
    values = [jnp.where(date + 1 + h < dates, partners_ref[0, h], 0) for h in range(SPAN)]
    values += [1 - date % 2, (place > 0).astype(jnp.int32), (place < places - 1).astype(jnp.int32), jnp.int32(0)]
    beside = date + 1 - 2 * (date % 2)
    held = [date, beside, date + 2, beside + 2, date + 4, beside + 4]
    found = [(lax.rem(h, dates) == ref_ref[0]).astype(jnp.int32) for h in held]
    values += found
    row = iota(cond_ref.shape, 0)
    cond = jnp.zeros(cond_ref.shape, jnp.int32)
    for k, value in enumerate(values):
        cond = jnp.where(row == k, value, cond)
    cond_ref[...] = cond.astype(F32)
    dist = iota((TAPS, blocks), 0).astype(F32) - 3.0 - frac_ref[...]
    arg = jnp.pi * dist
    sinc = jnp.where(arg == 0.0, 1.0, jnp.sin(arg) / jnp.where(arg == 0.0, 1.0, arg))
    weights = sinc * (0.5 + 0.5 * jnp.cos(arg / 4.0))
    shifts = jnp.broadcast_to(off_ref[...].astype(F32), (TAPS, blocks))
    small = jnp.concatenate([weights, shifts], axis=0).astype(BF16)
    block, lane = iota((blocks, LANES), 0), iota((blocks, LANES), 1)
    taps_ref[...] = dot(small, (lane == block + 1).astype(BF16)).astype(BF16)
    low_ref[2 * rows :, :] = dot(small, (block == 0).astype(BF16)).astype(BF16)
    high_ref[2 * rows :, :] = dot(small, (block == blocks - 1).astype(BF16)).astype(BF16)
    copies[0].wait()
    low_ref[0 : 2 * rows, :] = own_ref[:, 0:LANES]
    high_ref[0 : 2 * rows, :] = own_ref[:, cols - LANES :]


def join_kernel(cond_ref, own_ref, beside_ref, halo_ref, two_ref, two_halo_ref, amp_ref, both_ref, all_ref):
    rows = amp_ref.shape[0]
    mine, other = cond_ref[PICK : PICK + 1, 0:1] > 0.0, cond_ref[PICK + 1 : PICK + 2, 0:1] > 0.0
    value = jnp.where(other, beside_ref[...].astype(F32), own_ref[...].astype(F32))
    value = amplitude(value[0:rows], value[rows:])
    amp_ref[...] = jnp.where(mine | other, value.astype(F32), 0.0).astype(BF16)
    width = two_halo_ref.shape[1]
    for ref in (both_ref, all_ref):
        ref[0 : 2 * rows, :] = two_ref[...]
        ref[2 * rows : 2 * rows + HROWS, 0:width] = two_halo_ref[...]
        ref[2 * rows : 2 * rows + HROWS, width:] = jnp.zeros((HROWS, ref.shape[1] - width), BF16)
    all_ref[2 * rows + HROWS :, 0:width] = halo_ref[...]
    all_ref[2 * rows + HROWS :, width:] = jnp.zeros((HROWS, all_ref.shape[1] - width), BF16)


def halo_kernel(blocks, cond_ref, taps_ref, left_ref, right_ref, out_ref):
    left = jnp.where(cond_ref[LEFT : LEFT + 1, :] > 0.0, left_ref[...].astype(F32), 0.0)
    right = jnp.where(cond_ref[RIGHT : RIGHT + 1, :] > 0.0, right_ref[...].astype(F32), 0.0)
    rows = (left.shape[0] - HROWS) // 2
    lane = iota((2 * rows, LANES), 1)
    both = jnp.where(lane < EDGE, pltpu.roll(left[0 : 2 * rows], EDGE, 1), pltpu.roll(right[0 : 2 * rows], EDGE, 1))
    both = jnp.where(lane < 2 * EDGE, both, 0.0)
    both = (both[0:rows] + pltpu.roll(both[rows:], 2 * EDGE, 1)).astype(BF16)
    groups = rows // HROWS
    for k in range(groups):
        out_ref[:, k * LANES : (k + 1) * LANES] = both[k * HROWS : (k + 1) * HROWS]
    lane = iota((HROWS, LANES), 1)
    taps = jnp.where(lane == 0, left[2 * rows :], taps_ref[...].astype(F32))
    out_ref[:, groups * LANES : (groups + 1) * LANES] = jnp.where(
        lane == blocks + 1, right[2 * rows :], taps
    ).astype(BF16)


def resample(main_ref, halo_ref, use):
    rows, cols = main_ref.shape[0] // 2, main_ref.shape[1]
    tiles = cols // LANES
    groups = rows // HROWS
    edge = jnp.concatenate([halo_ref[:, k * LANES : (k + 1) * LANES] for k in range(groups)], axis=0).astype(F32)
    edge = [pltpu.roll(edge, LANES - EDGE, 1), pltpu.roll(edge, EDGE, 1)]
    edge = jnp.concatenate(edge, axis=0).astype(BF16)
    shape = (LANES, cols + LANES)
    place = ((iota(shape, 1) - PAD) >> 6) + 1 == iota(shape, 0)
    table = dot(halo_ref[:, groups * LANES : (groups + 1) * LANES], place.astype(BF16))
    for p in range(tiles + 1):
        if p == 0:
            window = jnp.concatenate([edge, main_ref[:, 0:LANES]], axis=1)
        elif p == tiles:
            window = jnp.concatenate([main_ref[:, cols - LANES :], edge], axis=1)
        else:
            window = main_ref[:, (p - 1) * LANES : (p + 1) * LANES]
        out = dot(window, band(table[:, p * LANES : (p + 1) * LANES])).astype(BF16)
        use(p, out[0:rows], out[rows:])


def range_box():
    gap = iota((2 * LANES, LANES), 0) - iota((2 * LANES, LANES), 1) - PAD
    return (jnp.abs(gap) <= BOXR // 2).astype(BF16)


def line_box(field):
    rows, lanes = field.shape
    base = jnp.concatenate([field, jnp.zeros((8, lanes), F32)], axis=0)
    two = base + pltpu.roll(base, 1, 0)
    four = two + pltpu.roll(two, 2, 0)
    five = four + pltpu.roll(base, 4, 0)
    return pltpu.roll(five, rows + 8 - BOXA // 2, 0)[0:rows]


def own_kernel(main_ref, halo_ref, ext_ref, power_ref, fields_ref):
    rows, cols = power_ref.shape

    def use(p, real, imag):
        lanes = slice(p * LANES, (p + 1) * LANES)
        ext_ref[0:rows, lanes] = real
        ext_ref[rows:, lanes] = imag
        real, imag = real.astype(F32), imag.astype(F32)
        fields_ref[:, lanes] = (real * real + imag * imag).astype(BF16)

    resample(main_ref, halo_ref, use)
    box = range_box()
    for p in range(cols // LANES):
        lanes = slice(p * LANES, (p + 1) * LANES)
        power_ref[:, lanes] = line_box(dot(fields_ref[:, p * LANES : (p + 2) * LANES], box))


def pair(flag, ext_ref, power_ref, main_ref, halo_ref, out_ref, fields_ref):
    rows, cols = out_ref.shape

    def use(p, real, imag):
        lanes = slice(p * LANES, (p + 1) * LANES)
        own_r, own_i = ext_ref[0:rows, lanes].astype(F32), ext_ref[rows:, lanes].astype(F32)
        r, i = real.astype(F32), imag.astype(F32)
        fields_ref[0:rows, lanes] = (own_r * r + own_i * i).astype(BF16)
        fields_ref[rows : 2 * rows, lanes] = (own_i * r - own_r * i).astype(BF16)
        fields_ref[2 * rows :, lanes] = (r * r + i * i).astype(BF16)

    resample(main_ref, halo_ref, use)
    box = range_box()
    for p in range(cols // LANES):
        lanes = slice(p * LANES, (p + 1) * LANES)
        sums = dot(fields_ref[:, p * LANES : (p + 2) * LANES], box)
        re = line_box(sums[0:rows])
        im = line_box(sums[rows : 2 * rows])
        partner = line_box(sums[2 * rows :])
        value = flag * (re * re + im * im) / (power_ref[:, lanes] * partner + 1e-06)
        out_ref[:, lanes] = value.astype(BF16)


def two_kernel(cond_ref, ext_ref, power_ref, main_ref, halo_ref, out_ref, fields_ref):
    pair(cond_ref[1:2, :], ext_ref, power_ref, main_ref, halo_ref, out_ref, fields_ref)


def joined(ref, rows):
    return ref.at[0 : 2 * rows], ref.at[2 * rows : 2 * rows + HROWS]


def four_kernel(cond_ref, ext_ref, power_ref, both_ref, out_ref, fields_ref):
    pair(cond_ref[3:4, :], ext_ref, power_ref, *joined(both_ref, out_ref.shape[0]), out_ref, fields_ref)


def cross_kernel(cond_ref, ext_ref, power_ref, both_ref, out_ref, fields_ref):
    flag = jnp.where(cond_ref[EVEN : EVEN + 1, :] > 0.0, cond_ref[2:3, :], cond_ref[0:1, :])
    pair(flag, ext_ref, power_ref, *joined(both_ref, out_ref.shape[0]), out_ref, fields_ref)


def split(table):
    high = table.astype(BF16)
    return high, (table - high.astype(np.float32)).astype(BF16)


def twice(table):
    zero = np.zeros_like(table)
    return np.block([[table, zero], [zero, table]])


def surface_tables():
    index = np.arange(BLK)
    angle = 2.0 * np.pi / BLK * (index[:, None] * index[None, :] % BLK)
    cosine, sine = np.cos(angle).astype(np.float32), np.sin(angle).astype(np.float32)
    signed = np.where(index < BLK // 2, index, index - BLK)
    upsampled = OVS * BLK
    lag_phase = (np.arange(LAGS) - LAGS // 2)[:, None] * signed[None, :] % upsampled
    lag_angle = 2.0 * np.pi / upsampled * lag_phase
    lag_cos, lag_sin = np.cos(lag_angle).astype(np.float32), np.sin(lag_angle).astype(np.float32)
    high, low = split(np.concatenate([cosine, -sine], axis=0))
    first = np.concatenate([high, low, high], axis=1)
    second = np.concatenate(split(np.concatenate([twice(cosine), twice(sine)], axis=1)), axis=0)
    per = LANES // LAGS
    order = np.arange(LAGS).reshape(LAGS // per, per).T.reshape(-1)
    left = np.block([[lag_cos[order], -lag_sin[order]], [lag_sin[order], lag_cos[order]]])
    third = np.concatenate(split(left), axis=1)
    spread = [twice(np.tile(table.T, (1, per))) for table in (lag_cos, -lag_sin)]
    fourth = np.concatenate(split(np.concatenate(spread, axis=0)), axis=0)
    return first, second, third, fourth


def spectrum(amp_ref, rows_ref, first_ref, second_ref, use):
    size, cols = amp_ref.shape
    tiles = cols // LANES
    group = (iota((LANES, LANES), 0) >> 6 == iota((LANES, LANES), 1) >> 6).astype(F32)
    values = [amp_ref[:, p * LANES : (p + 1) * LANES].astype(F32) for p in range(tiles)]
    for p, value in enumerate(values):
        rows_ref[p : p + 1, :] = jnp.sum(value, axis=0, keepdims=True)
    mean = jnp.dot(rows_ref[...], group, precision=HIGHEST) / (BLK * BLK)
    for p, value in enumerate(values):
        value = value - mean[p : p + 1, :]
        rows_ref[p : p + 1, :] = jnp.sum(value * value, axis=0, keepdims=True)
        high = value.astype(BF16)
        low = (value - high.astype(F32)).astype(BF16)
        f = dot(first_ref[...], jnp.concatenate([high, high, low], axis=0)).astype(BF16)
        s = dot(jnp.concatenate([f, f], axis=1), second_ref[...])
        use(p, s[0:size, 0:LANES] + s[size:, LANES:], s[size:, 0:LANES] - s[0:size, LANES:])
    return jnp.dot(rows_ref[...], group, precision=HIGHEST)


def spectrum_kernel(own_ref, first_ref, second_ref, spec_ref, energy_ref, amp_ref, rows_ref):
    size = amp_ref.shape[0]
    amp_ref[...] = amplitude(own_ref[0:size, :], own_ref[size:, :])

    def use(p, real, imag):
        lanes = slice(p * LANES, (p + 1) * LANES)
        spec_ref[0:size, lanes] = real
        spec_ref[size:, lanes] = imag

    energy_ref[...] = spectrum(amp_ref, rows_ref, first_ref, second_ref, use)


def last_kernel(
    cond_ref,
    ext_ref,
    power_ref,
    last_ref,
    last_halo_ref,
    coh_two_ref,
    coh_cross_ref,
    coh_four_ref,
    *refs,
):
    samples, before_ref, refs = refs[0:6], refs[6], refs[7:]
    spec_ref, energy_ref, first_ref, second_ref, third_ref, fourth_ref, coh_hbm, surface_hbm = refs[0:8]
    tail_ref, fields_ref, amp_ref, rows_ref, cross_ref, out_scr, out_ref, sems = refs[8:]
    odd = lax.axis_index("date") % 2
    copies = [
        pltpu.make_async_copy(coh_two_ref, coh_hbm.at[1], sems.at[0]),
        pltpu.make_async_copy(coh_four_ref, coh_hbm.at[3], sems.at[1]),
        pltpu.make_async_copy(coh_cross_ref, coh_hbm.at[2 - 2 * odd], sems.at[2]),
        pltpu.make_async_copy(tail_ref, coh_hbm.at[2 * odd], sems.at[3]),
        pltpu.make_async_copy(out_ref, surface_hbm, sems.at[4]),
    ]
    for copy in copies[0:3]:
        copy.start()
    flag = jnp.where(cond_ref[EVEN : EVEN + 1, :] > 0.0, cond_ref[0:1, :], cond_ref[2:3, :])
    pair(flag, ext_ref, power_ref, last_ref, last_halo_ref, tail_ref, fields_ref)
    copies[3].start()
    size, cols = amp_ref.shape
    tiles = cols // LANES
    picks = [cond_ref[PICK + k : PICK + k + 1, 0:1] > 0.0 for k in range(len(samples))]
    value = samples[0][...].astype(F32)
    for pick, ref in zip(picks[1:], samples[1:]):
        value = jnp.where(pick, ref[0 : 2 * size, :].astype(F32), value)
    found = functools.reduce(jnp.logical_or, picks)
    value = amplitude(value[0:size], value[size:]).astype(F32)
    amp_ref[...] = jnp.where(found, value, before_ref[...].astype(F32)).astype(BF16)

    def use(p, ref_r, ref_i):
        lanes = slice(p * LANES, (p + 1) * LANES)
        own_r, own_i = spec_ref[0:size, lanes], spec_ref[size:, lanes]
        cross_ref[0:size, lanes] = own_r * ref_r + own_i * ref_i
        cross_ref[size:, lanes] = own_i * ref_r - own_r * ref_i

    energy = spectrum(amp_ref, rows_ref, first_ref, second_ref, use)
    scale = 1.0 / (BLK * jnp.sqrt(energy_ref[...] * energy + 1e-06))
    lag_rows = [[] for _ in range(LANES // LAGS)]
    for p in range(tiles):
        cross = (cross_ref[:, p * LANES : (p + 1) * LANES] * scale[p : p + 1, :]).astype(BF16)
        lags = dot(third_ref[...], jnp.concatenate([cross, cross], axis=0))
        for q in range(LANES // LAGS):
            part = [lags[ri * LAGS + q * 8 : ri * LAGS + q * 8 + 8] for ri in range(2)]
            lag_rows[q].append(jnp.concatenate(part, axis=1))
    lhs = jnp.concatenate([row for rows in lag_rows for row in rows], axis=0).astype(BF16)
    result = dot(jnp.concatenate([lhs, lhs], axis=1), fourth_ref[...])
    height = 8 * tiles
    quarter = iota((height, 2 * LANES), 1) % LANES // LAGS
    total = result[0:height]
    for q in range(1, LANES // LAGS):
        total = jnp.where(quarter == q, result[q * height : (q + 1) * height], total)
    for p in range(tiles):
        for jj in range(2):
            at = (2 * p + jj) * 8
            out_scr[at : at + 8, :] = total[p * 8 : p * 8 + 8, jj * LANES : (jj + 1) * LANES]
    for a in range(8):
        out_ref[:, a * LANES : (a + 1) * LANES] = out_scr[pl.ds(a, 2 * tiles, stride=8), :]
    copies[4].start()
    for copy in copies:
        copy.wait()


def shifted(value, axis, steps):
    count = lax.axis_size(axis)
    return lax.ppermute(value, axis, [(s, (s - steps) % count) for s in range(count)])


def swapped(value, axis, step):
    return lax.ppermute(value, axis, [(s, s ^ step) for s in range(lax.axis_size(axis))])


def spread(value, axis):
    count = lax.axis_size(axis)
    step = 2
    while step < count:
        value = jnp.maximum(value, swapped(value, axis, step))
        step *= 2
    return value


def call(kernel, name, out_shape, operands, scratch=()):
    return pl.pallas_call(
        kernel,
        out_shape=out_shape,
        in_specs=[VMEM] * len(operands),
        out_specs=jax.tree.map(lambda _: VMEM, out_shape),
        scratch_shapes=[pltpu.VMEM(*s) for s in scratch],
        compiler_params=PARAMS,
        name=name,
    )(*operands)


def body(slc, ref_date, int_offset, frac_offset, partners):
    sds = jax.ShapeDtypeStruct
    _, _, rows, cols = slc.shape
    tiles = cols // LANES
    dates = lax.axis_size("date")
    even = lax.axis_index("date") % 2 == 0
    field, samples = sds((rows, cols), BF16), sds((2 * rows, cols), BF16)
    payload = sds((2 * rows + HROWS, LANES), BF16)
    own, cond, taps, low, high = pl.pallas_call(
        prep_kernel,
        out_shape=(samples, sds((16, LANES), F32), sds((HROWS, LANES), BF16), payload, payload),
        in_specs=[pl.BlockSpec(memory_space=pl.ANY)] * 5,
        out_specs=(VMEM,) * 5,
        scratch_shapes=[
            pltpu.VMEM(int_offset.shape[1:], jnp.int32),
            pltpu.VMEM(frac_offset.shape[1:], F32),
            pltpu.SMEM(ref_date.shape, jnp.int32),
            pltpu.SMEM(partners.shape, jnp.int32),
            pltpu.SemaphoreType.DMA((5,)),
        ],
        compiler_params=PARAMS,
        name="prepare",
    )(slc.reshape(2 * rows, cols), int_offset[0], frac_offset[0], ref_date, partners)
    beside = swapped(own, "date", 1)
    two = shifted(own, "date", 2)
    right = shifted(low, "rng", 1)
    left = shifted(high, "rng", -1)
    width = (rows // HROWS + 1) * LANES
    halo = call(
        functools.partial(halo_kernel, cols // BLK), "halo", sds((HROWS, width), BF16), (cond, taps, left, right)
    )
    two_halo = shifted(halo, "date", 2)
    pair_amp, both, everything = call(
        join_kernel,
        "join",
        (field, sds((2 * rows + HROWS, cols), BF16), sds((2 * rows + 2 * HROWS, cols), BF16)),
        (cond, own, beside, halo, two, two_halo),
    )
    cross = swapped(everything, "date", 1)
    four = shifted(both, "date", 2)
    before = shifted(pair_amp, "date", -2) if dates == 8 else spread(pair_amp, "date")
    across = lax.ppermute(both, "date", [(s, (s - 2) % dates ^ 1) for s in range(dates)])
    first, second, third, fourth = [jnp.asarray(t) for t in surface_tables()]
    spec, energy = call(
        spectrum_kernel,
        "spectrum",
        (sds((2 * rows, cols), F32), sds((tiles, LANES), F32)),
        (own, first, second),
        [((rows, cols), BF16), ((tiles, LANES), F32)],
    )
    fields = ((3 * rows, cols + LANES), BF16)
    ext, power = call(
        own_kernel,
        "own",
        (sds((2 * rows, cols + LANES), BF16), sds((rows, cols), F32)),
        (own, halo),
        [((rows, cols + LANES), BF16)],
    )
    coh_two = call(two_kernel, "two", field, (cond, ext, power, two, two_halo), [fields])
    coh_cross = call(cross_kernel, "cross", field, (cond, ext, power, cross), [fields])
    coh_four = call(four_kernel, "four", field, (cond, ext, power, four), [fields])
    last = jnp.where(even, beside, across[0 : 2 * rows])
    last_halo = jnp.where(even, cross[2 * rows + HROWS :], across[2 * rows :])
    operands = (
        *(cond, ext, power, last, last_halo, coh_two, coh_cross, coh_four),
        *(own, beside, two, cross, four, across, before),
        *(spec, energy, first, second, third, fourth),
    )
    lags = (cols // BLK, LAGS * LAGS)
    coherence, surface = pl.pallas_call(
        last_kernel,
        out_shape=(sds((SPAN, rows, cols), BF16), sds(lags, F32)),
        in_specs=[VMEM] * len(operands),
        out_specs=(pl.BlockSpec(memory_space=pl.ANY),) * 2,
        scratch_shapes=[
            pltpu.VMEM((rows, cols), BF16),
            pltpu.VMEM(*fields),
            pltpu.VMEM((rows, cols), BF16),
            pltpu.VMEM((tiles, LANES), F32),
            pltpu.VMEM((2 * rows, cols), F32),
            pltpu.VMEM((8 * cols // BLK, LANES), F32),
            pltpu.VMEM(lags, F32),
            pltpu.SemaphoreType.DMA((5,)),
        ],
        compiler_params=PARAMS,
        name="last",
    )(*operands)
    return (surface[None, None], coherence[None])


def solution(mesh):
    in_specs = (
        P("date", None, None, "rng"),
        P(),
        P("date", None, "rng"),
        P("date", None, "rng"),
        P("date", None),
    )
    out_specs = (P("date", None, "rng", None), P("date", None, None, "rng"))
    return jax.shard_map(body, mesh=mesh, in_specs=in_specs, out_specs=out_specs, check_vma=False)
```

```python
import functools

import jax
import jax.numpy as jnp
import numpy as np
from jax import lax
from jax.experimental import pallas as pl
from jax.experimental.pallas import tpu as pltpu
from jax.sharding import PartitionSpec as P

BLK = 64
OVS = 2
LAGS = 32
SPAN = 4
BOXA = 5
BOXR = 19
TAPS = 8
LANES = 128
PAD = 16
EDGE = 32
HROWS = 16
F32 = jnp.float32
BF16 = jnp.bfloat16
HIGHEST = lax.Precision.HIGHEST
VMEM = pl.BlockSpec(memory_space=pltpu.VMEM)
SMEM = pl.BlockSpec(memory_space=pltpu.SMEM)
PARAMS = pltpu.CompilerParams(vmem_limit_bytes=8 << 20)


def dot(a, b):
    return jnp.dot(a, b, preferred_element_type=F32)


def iota(shape, dim):
    return lax.broadcasted_iota(jnp.int32, shape, dim)


def band(table):
    top = 96
    rows = 2 * LANES - top
    step = iota((rows, LANES), 0) + top - iota((rows, LANES), 1) - (LANES - PAD - 3)
    step = step.astype(F32) - table[TAPS : TAPS + 1, :]
    out = jnp.zeros((rows, LANES), F32)
    for tap in range(TAPS):
        out = jnp.where(step == float(tap), table[tap : tap + 1, :], out)
    return jnp.concatenate([jnp.zeros((top, LANES), BF16), out.astype(BF16)], axis=0)


def amplitude(real, imag):
    real, imag = real.astype(F32), imag.astype(F32)
    return jnp.sqrt(real * real + imag * imag + 1e-06).astype(BF16)


EVEN, LEFT, RIGHT, PICK = 4, 5, 6, 8


def prep_kernel(
    own_hbm, off_hbm, frac_hbm, ref_hbm, partners_hbm, own_ref, cond_ref, taps_ref, low_ref, high_ref, *scratch
):
    off_ref, frac_ref, ref_ref, partners_ref, sems = scratch
    sources = (own_hbm, off_hbm, frac_hbm, ref_hbm, partners_hbm)
    targets = (own_ref, off_ref, frac_ref, ref_ref, partners_ref)
    copies = [pltpu.make_async_copy(s, t, sems.at[k]) for k, (s, t) in enumerate(zip(sources, targets))]
    for copy in copies:
        copy.start()
    for copy in copies[1:]:
        copy.wait()
    rows, cols = own_ref.shape[0] // 2, own_ref.shape[1]
    blocks = cols // BLK
    date, dates = lax.axis_index("date"), lax.axis_size("date")
    place, places = lax.axis_index("rng"), lax.axis_size("rng")
    values = [jnp.where(date + 1 + h < dates, partners_ref[0, h], 0) for h in range(SPAN)]
    values += [1 - date % 2, (place > 0).astype(jnp.int32), (place < places - 1).astype(jnp.int32), jnp.int32(0)]
    beside = date + 1 - 2 * (date % 2)
    held = [date, beside, date + 2, date + 4, beside + 2, beside + 4]
    found = [(lax.rem(h, dates) == ref_ref[0]).astype(jnp.int32) for h in held]
    values += found[0:4] + [(found[4] + found[5]) * int(dates == 8)]
    row = iota(cond_ref.shape, 0)
    cond = jnp.zeros(cond_ref.shape, jnp.int32)
    for k, value in enumerate(values):
        cond = jnp.where(row == k, value, cond)
    cond_ref[...] = cond.astype(F32)
    dist = iota((TAPS, blocks), 0).astype(F32) - 3.0 - frac_ref[...]
    arg = jnp.pi * dist
    sinc = jnp.where(arg == 0.0, 1.0, jnp.sin(arg) / jnp.where(arg == 0.0, 1.0, arg))
    weights = sinc * (0.5 + 0.5 * jnp.cos(arg / 4.0))
    shifts = jnp.broadcast_to(off_ref[...].astype(F32), (TAPS, blocks))
    small = jnp.concatenate([weights, shifts], axis=0).astype(BF16)
    block, lane = iota((blocks, LANES), 0), iota((blocks, LANES), 1)
    taps_ref[...] = dot(small, (lane == block + 1).astype(BF16)).astype(BF16)
    low_ref[2 * rows :, :] = dot(small, (block == 0).astype(BF16)).astype(BF16)
    high_ref[2 * rows :, :] = dot(small, (block == blocks - 1).astype(BF16)).astype(BF16)
    copies[0].wait()
    low_ref[0 : 2 * rows, :] = own_ref[:, 0:LANES]
    high_ref[0 : 2 * rows, :] = own_ref[:, cols - LANES :]


def candidate_kernel(first, cond_ref, a_ref, b_ref, amp_ref):
    rows = amp_ref.shape[0]
    at = PICK + first
    a, b = cond_ref[at : at + 1, 0:1] > 0.0, cond_ref[at + 1 : at + 2, 0:1] > 0.0
    value = jnp.where(b, b_ref[...].astype(F32), a_ref[...].astype(F32))
    value = amplitude(value[0:rows], value[rows:])
    amp_ref[...] = jnp.where(a | b, value.astype(F32), 0.0).astype(BF16)


def pass_kernel(earlier_ref, in_ref, out_ref):
    del earlier_ref
    out_ref[...] = in_ref[...]


def halo_kernel(blocks, cond_ref, taps_ref, left_ref, right_ref, out_ref):
    left = jnp.where(cond_ref[LEFT : LEFT + 1, :] > 0.0, left_ref[...].astype(F32), 0.0)
    right = jnp.where(cond_ref[RIGHT : RIGHT + 1, :] > 0.0, right_ref[...].astype(F32), 0.0)
    rows = (left.shape[0] - HROWS) // 2
    lane = iota((2 * rows, LANES), 1)
    both = jnp.where(lane < EDGE, pltpu.roll(left[0 : 2 * rows], EDGE, 1), pltpu.roll(right[0 : 2 * rows], EDGE, 1))
    both = jnp.where(lane < 2 * EDGE, both, 0.0)
    both = (both[0:rows] + pltpu.roll(both[rows:], 2 * EDGE, 1)).astype(BF16)
    groups = rows // HROWS
    for k in range(groups):
        out_ref[:, k * LANES : (k + 1) * LANES] = both[k * HROWS : (k + 1) * HROWS]
    lane = iota((HROWS, LANES), 1)
    taps = jnp.where(lane == 0, left[2 * rows :], taps_ref[...].astype(F32))
    out_ref[:, groups * LANES : (groups + 1) * LANES] = jnp.where(
        lane == blocks + 1, right[2 * rows :], taps
    ).astype(BF16)


def resample(main_ref, halo_ref, use):
    rows, cols = main_ref.shape[0] // 2, main_ref.shape[1]
    tiles = cols // LANES
    groups = rows // HROWS
    edge = jnp.concatenate([halo_ref[:, k * LANES : (k + 1) * LANES] for k in range(groups)], axis=0).astype(F32)
    edge = [pltpu.roll(edge, LANES - EDGE, 1), pltpu.roll(edge, EDGE, 1)]
    edge = jnp.concatenate(edge, axis=0).astype(BF16)
    shape = (LANES, cols + LANES)
    place = ((iota(shape, 1) - PAD) >> 6) + 1 == iota(shape, 0)
    table = dot(halo_ref[:, groups * LANES : (groups + 1) * LANES], place.astype(BF16))
    for p in range(tiles + 1):
        if p == 0:
            window = jnp.concatenate([edge, main_ref[:, 0:LANES]], axis=1)
        elif p == tiles:
            window = jnp.concatenate([main_ref[:, cols - LANES :], edge], axis=1)
        else:
            window = main_ref[:, (p - 1) * LANES : (p + 1) * LANES]
        out = dot(window, band(table[:, p * LANES : (p + 1) * LANES])).astype(BF16)
        use(p, out[0:rows], out[rows:])


def range_box():
    gap = iota((2 * LANES, LANES), 0) - iota((2 * LANES, LANES), 1) - PAD
    return (jnp.abs(gap) <= BOXR // 2).astype(BF16)


def line_box(field):
    rows, lanes = field.shape
    base = jnp.concatenate([field, jnp.zeros((8, lanes), F32)], axis=0)
    two = base + pltpu.roll(base, 1, 0)
    four = two + pltpu.roll(two, 2, 0)
    five = four + pltpu.roll(base, 4, 0)
    return pltpu.roll(five, rows + 8 - BOXA // 2, 0)[0:rows]


def keep_tile(ext_ref, p, real, imag):
    rows, lanes = real.shape[0], slice(p * LANES, (p + 1) * LANES)
    ext_ref[0:rows, lanes] = real
    ext_ref[rows:, lanes] = imag


def power_tile(fields_ref, p, real, imag):
    real, imag = real.astype(F32), imag.astype(F32)
    fields_ref[:, p * LANES : (p + 1) * LANES] = (real * real + imag * imag).astype(BF16)


def cross_tile(fields_ref, ext_ref, p, real, imag):
    rows, lanes = real.shape[0], slice(p * LANES, (p + 1) * LANES)
    own_r, own_i = ext_ref[0:rows, lanes].astype(F32), ext_ref[rows:, lanes].astype(F32)
    r, i = real.astype(F32), imag.astype(F32)
    fields_ref[0:rows, lanes] = (own_r * r + own_i * i).astype(BF16)
    fields_ref[rows : 2 * rows, lanes] = (own_i * r - own_r * i).astype(BF16)


def coherence(sums, own, partner):
    rows = own.shape[0]
    re, im = line_box(sums[0:rows]), line_box(sums[rows : 2 * rows])
    return ((re * re + im * im) / (own * partner + 1e-06)).astype(BF16)


def own_kernel(earlier_ref, main_ref, halo_ref, ext_ref, power_ref, fields_ref):
    del earlier_ref
    rows, cols = power_ref.shape

    def use(p, real, imag):
        keep_tile(ext_ref, p, real, imag)
        power_tile(fields_ref, p, real, imag)

    resample(main_ref, halo_ref, use)
    box = range_box()
    for p in range(cols // LANES):
        lanes = slice(p * LANES, (p + 1) * LANES)
        power_ref[:, lanes] = line_box(dot(fields_ref[:, p * LANES : (p + 2) * LANES], box))


def pair_kernel(own_ref, own_power_ref, main_ref, halo_ref, ext_ref, power_ref, out_ref, fields_ref):
    rows, cols = out_ref.shape

    def use(p, real, imag):
        keep_tile(ext_ref, p, real, imag)
        power_tile(fields_ref.at[2 * rows :], p, real, imag)
        cross_tile(fields_ref, own_ref, p, real, imag)

    resample(main_ref, halo_ref, use)
    box = range_box()
    for p in range(cols // LANES):
        lanes = slice(p * LANES, (p + 1) * LANES)
        sums = dot(fields_ref[:, p * LANES : (p + 2) * LANES], box)
        power = line_box(sums[2 * rows :])
        power_ref[:, lanes] = power
        out_ref[:, lanes] = coherence(sums, own_power_ref[:, lanes], power)


def again_kernel(own_ref, own_power_ref, ext_ref, power_ref, out_ref, fields_ref):
    rows, cols = out_ref.shape
    for p in range(cols // LANES + 1):
        lanes = slice(p * LANES, (p + 1) * LANES)
        cross_tile(fields_ref, own_ref, p, ext_ref[0:rows, lanes], ext_ref[rows:, lanes])
    box = range_box()
    for p in range(cols // LANES):
        lanes = slice(p * LANES, (p + 1) * LANES)
        sums = dot(fields_ref[:, p * LANES : (p + 2) * LANES], box)
        out_ref[:, lanes] = coherence(sums, own_power_ref[:, lanes], power_ref[:, lanes])


def place_kernel(cond_ref, beside_ref, two_ref, four_ref, near_ref, far_ref, out_ref):
    even = cond_ref[EVEN : EVEN + 1, 0:1] > 0.0
    near = near_ref[...].astype(F32)
    fields = [
        jnp.where(even, beside_ref[...].astype(F32), near),
        two_ref[...].astype(F32),
        jnp.where(even, near, far_ref[...].astype(F32)),
        four_ref[...].astype(F32),
    ]
    for h, value in enumerate(fields):
        out_ref[h] = (value * cond_ref[h : h + 1, 0:1]).astype(BF16)


def split(table):
    high = table.astype(BF16)
    return high, (table - high.astype(np.float32)).astype(BF16)


def twice(table):
    zero = np.zeros_like(table)
    return np.block([[table, zero], [zero, table]])


def surface_tables():
    index = np.arange(BLK)
    angle = 2.0 * np.pi / BLK * (index[:, None] * index[None, :] % BLK)
    cosine, sine = np.cos(angle).astype(np.float32), np.sin(angle).astype(np.float32)
    signed = np.where(index < BLK // 2, index, index - BLK)
    upsampled = OVS * BLK
    lag_phase = (np.arange(LAGS) - LAGS // 2)[:, None] * signed[None, :] % upsampled
    lag_angle = 2.0 * np.pi / upsampled * lag_phase
    lag_cos, lag_sin = np.cos(lag_angle).astype(np.float32), np.sin(lag_angle).astype(np.float32)
    high, low = split(np.concatenate([cosine, -sine], axis=0))
    first = np.concatenate([high, low, high], axis=1)
    second = np.concatenate(split(np.concatenate([twice(cosine), twice(sine)], axis=1)), axis=0)
    per = LANES // LAGS
    order = np.arange(LAGS).reshape(LAGS // per, per).T.reshape(-1)
    left = np.block([[lag_cos[order], -lag_sin[order]], [lag_sin[order], lag_cos[order]]])
    third = np.concatenate(split(left), axis=1)
    spread = [twice(np.tile(table.T, (1, per))) for table in (lag_cos, -lag_sin)]
    fourth = np.concatenate(split(np.concatenate(spread, axis=0)), axis=0)
    return first, second, third, fourth


def spectrum(amp_ref, rows_ref, first_ref, second_ref, use):
    size, cols = amp_ref.shape
    tiles = cols // LANES
    group = (iota((LANES, LANES), 0) >> 6 == iota((LANES, LANES), 1) >> 6).astype(F32)
    values = [amp_ref[:, p * LANES : (p + 1) * LANES].astype(F32) for p in range(tiles)]
    for p, value in enumerate(values):
        rows_ref[p : p + 1, :] = jnp.sum(value, axis=0, keepdims=True)
    mean = jnp.dot(rows_ref[...], group, precision=HIGHEST) / (BLK * BLK)
    for p, value in enumerate(values):
        value = value - mean[p : p + 1, :]
        rows_ref[p : p + 1, :] = jnp.sum(value * value, axis=0, keepdims=True)
        high = value.astype(BF16)
        low = (value - high.astype(F32)).astype(BF16)
        f = dot(first_ref[...], jnp.concatenate([high, high, low], axis=0)).astype(BF16)
        s = dot(jnp.concatenate([f, f], axis=1), second_ref[...])
        use(p, s[0:size, 0:LANES] + s[size:, LANES:], s[size:, 0:LANES] - s[0:size, LANES:])
    return jnp.dot(rows_ref[...], group, precision=HIGHEST)


def spectrum_kernel(own_ref, first_ref, second_ref, third_ref, fourth_ref, spec_ref, energy_ref, amp_ref, rows_ref):
    del third_ref, fourth_ref
    size = amp_ref.shape[0]
    amp_ref[...] = amplitude(own_ref[0:size, :], own_ref[size:, :])

    def use(p, real, imag):
        lanes = slice(p * LANES, (p + 1) * LANES)
        spec_ref[0:size, lanes] = real
        spec_ref[size:, lanes] = imag

    energy_ref[...] = spectrum(amp_ref, rows_ref, first_ref, second_ref, use)


def surface_kernel(cond_ref, *refs):
    samples, across_ref, before_ref, refs = refs[0:4], refs[4], refs[5], refs[6:]
    spec_ref, energy_ref, first_ref, second_ref, third_ref, fourth_ref, out_ref = refs[0:7]
    amp_ref, rows_ref, cross_ref, out_scr = refs[7:]
    size, cols = amp_ref.shape
    tiles = cols // LANES
    picks = [cond_ref[PICK + k : PICK + k + 1, 0:1] > 0.0 for k in range(len(samples) + 1)]
    value = samples[0][...].astype(F32)
    for pick, ref in zip(picks[1:4], samples[1:]):
        value = jnp.where(pick, ref[...].astype(F32), value)
    found = functools.reduce(jnp.logical_or, picks[0:4])
    value = amplitude(value[0:size], value[size:]).astype(F32)
    other = jnp.where(picks[4], across_ref[...].astype(F32), before_ref[...].astype(F32))
    amp_ref[...] = jnp.where(found, value, other).astype(BF16)

    def use(p, ref_r, ref_i):
        lanes = slice(p * LANES, (p + 1) * LANES)
        own_r, own_i = spec_ref[0:size, lanes], spec_ref[size:, lanes]
        cross_ref[0:size, lanes] = own_r * ref_r + own_i * ref_i
        cross_ref[size:, lanes] = own_i * ref_r - own_r * ref_i

    energy = spectrum(amp_ref, rows_ref, first_ref, second_ref, use)
    scale = 1.0 / (BLK * jnp.sqrt(energy_ref[...] * energy + 1e-06))
    lag_rows = [[] for _ in range(LANES // LAGS)]
    for p in range(tiles):
        cross = (cross_ref[:, p * LANES : (p + 1) * LANES] * scale[p : p + 1, :]).astype(BF16)
        lags = dot(third_ref[...], jnp.concatenate([cross, cross], axis=0))
        for q in range(LANES // LAGS):
            part = [lags[ri * LAGS + q * 8 : ri * LAGS + q * 8 + 8] for ri in range(2)]
            lag_rows[q].append(jnp.concatenate(part, axis=1))
    lhs = jnp.concatenate([row for rows in lag_rows for row in rows], axis=0).astype(BF16)
    result = dot(jnp.concatenate([lhs, lhs], axis=1), fourth_ref[...])
    height = 8 * tiles
    quarter = iota((height, 2 * LANES), 1) % LANES // LAGS
    total = result[0:height]
    for q in range(1, LANES // LAGS):
        total = jnp.where(quarter == q, result[q * height : (q + 1) * height], total)
    for p in range(tiles):
        for jj in range(2):
            at = (2 * p + jj) * 8
            out_scr[at : at + 8, :] = total[p * 8 : p * 8 + 8, jj * LANES : (jj + 1) * LANES]
    for a in range(8):
        out_ref[:, a * LANES : (a + 1) * LANES] = out_scr[pl.ds(a, 2 * tiles, stride=8), :]


def shifted(value, axis, steps):
    count = lax.axis_size(axis)
    return lax.ppermute(value, axis, [(s, (s - steps) % count) for s in range(count)])


def swapped(value, axis, step):
    return lax.ppermute(value, axis, [(s, s ^ step) for s in range(lax.axis_size(axis))])


def spread(value, axis):
    count = lax.axis_size(axis)
    step = 2
    while step < count:
        value = jnp.maximum(value, swapped(value, axis, step))
        step *= 2
    return value


def call(kernel, name, out_shape, operands, scratch=()):
    return pl.pallas_call(
        kernel,
        out_shape=out_shape,
        in_specs=[VMEM] * len(operands),
        out_specs=jax.tree.map(lambda _: VMEM, out_shape),
        scratch_shapes=[pltpu.VMEM(*s) for s in scratch],
        compiler_params=PARAMS,
        name=name,
    )(*operands)


def body(slc, ref_date, int_offset, frac_offset, partners):
    sds = jax.ShapeDtypeStruct
    _, _, rows, cols = slc.shape
    tiles = cols // LANES
    dates = lax.axis_size("date")
    even = lax.axis_index("date") % 2 == 0
    field, samples = sds((rows, cols), BF16), sds((2 * rows, cols), BF16)
    payload = sds((2 * rows + HROWS, LANES), BF16)
    own, cond, taps, low, high = pl.pallas_call(
        prep_kernel,
        out_shape=(samples, sds((16, LANES), F32), sds((HROWS, LANES), BF16), payload, payload),
        in_specs=[pl.BlockSpec(memory_space=pltpu.HBM)] * 5,
        out_specs=(VMEM,) * 5,
        scratch_shapes=[
            pltpu.VMEM(int_offset.shape[1:], jnp.int32),
            pltpu.VMEM(frac_offset.shape[1:], F32),
            pltpu.SMEM(ref_date.shape, jnp.int32),
            pltpu.SMEM(partners.shape, jnp.int32),
            pltpu.SemaphoreType.DMA((5,)),
        ],
        compiler_params=PARAMS,
        name="prepare",
    )(slc.reshape(2 * rows, cols), int_offset[0], frac_offset[0], ref_date, partners)
    beside = swapped(slc.reshape(2 * rows, cols), "date", 1)
    two = shifted(slc.reshape(2 * rows, cols), "date", 2)
    right = shifted(low, "rng", 1)
    left = shifted(high, "rng", -1)
    width = (rows // HROWS + 1) * LANES
    halo = call(
        functools.partial(halo_kernel, cols // BLK), "halo", sds((HROWS, width), BF16), (cond, taps, left, right)
    )
    two = call(pass_kernel, "pass", samples, (halo, two))
    four = shifted(two, "date", 2)
    beside_halo = swapped(halo, "date", 1)
    two_halo = shifted(halo, "date", 2)
    four_halo = shifted(halo, "date", 4)
    amp = call(functools.partial(candidate_kernel, 0), "candidate", field, (cond, own, beside))
    before = shifted(amp, "date", -2) if dates == 8 else spread(amp, "date")
    later = call(functools.partial(candidate_kernel, 2), "later", field, (cond, two, four))
    across = swapped(later, "date", 1)
    first, second, third, fourth = [jnp.asarray(t) for t in surface_tables()]
    spec, energy = call(
        spectrum_kernel,
        "spectrum",
        (sds((2 * rows, cols), F32), sds((tiles, LANES), F32)),
        (own, first, second, third, fourth),
        [((rows, cols), BF16), ((tiles, LANES), F32)],
    )
    resampled = (sds((2 * rows, cols + LANES), BF16), sds((rows, cols), F32))
    scratch = [[((k * rows, cols + LANES), BF16)] for k in range(4)]
    own_ext = call(own_kernel, "own", resampled, (amp, own, halo), scratch[1])
    *beside_ext, coh_beside = call(
        pair_kernel, "beside", (*resampled, field), (*own_ext, beside, beside_halo), scratch[3]
    )
    *two_ext, coh_near = call(pair_kernel, "near", (*resampled, field), (*beside_ext, two, two_halo), scratch[3])
    near = swapped(coh_near, "date", 1)
    coh_two = call(again_kernel, "two", field, (*own_ext, *two_ext), scratch[2])
    *four_ext, coh_far = call(pair_kernel, "far", (*resampled, field), (*beside_ext, four, four_halo), scratch[3])
    far = swapped(coh_far, "date", 1)
    coh_four = call(again_kernel, "four", field, (*own_ext, *four_ext), scratch[2])
    surface = call(
        surface_kernel,
        "surface",
        sds((cols // BLK, LAGS * LAGS), F32),
        (cond, own, beside, two, four, across, before, spec, energy, first, second, third, fourth),
        [
            ((rows, cols), BF16),
            ((tiles, LANES), F32),
            ((2 * rows, cols), F32),
            ((8 * cols // BLK, LANES), F32),
        ],
    )
    fields = call(
        place_kernel,
        "place",
        sds((SPAN, rows, cols), BF16),
        (cond, coh_beside, coh_two, coh_four, near, far),
    )
    return (surface[None, None], fields[None])


def solution(mesh):
    in_specs = (
        P("date", None, None, "rng"),
        P(),
        P("date", None, "rng"),
        P("date", None, "rng"),
        P("date", None),
    )
    out_specs = (P("date", None, "rng", None), P("date", None, None, "rng"))
    return jax.shard_map(body, mesh=mesh, in_specs=in_specs, out_specs=out_specs, check_vma=False)
```

```python
import functools

import jax
import jax.numpy as jnp
import numpy as np
from jax import lax
from jax.experimental import pallas as pl
from jax.experimental.pallas import tpu as pltpu
from jax.sharding import PartitionSpec as P

BLK = 64
OVS = 2
LAGS = 32
SPAN = 4
BOXA = 5
BOXR = 19
TAPS = 8
LANES = 128
PAD = 16
EDGE = 32
HROWS = 16
F32 = jnp.float32
BF16 = jnp.bfloat16
HIGHEST = lax.Precision.HIGHEST
VMEM = pl.BlockSpec(memory_space=pltpu.VMEM)
SMEM = pl.BlockSpec(memory_space=pltpu.SMEM)
PARAMS = pltpu.CompilerParams(vmem_limit_bytes=8 << 20)


def dot(a, b):
    return jnp.dot(a, b, preferred_element_type=F32)


def iota(shape, dim):
    return lax.broadcasted_iota(jnp.int32, shape, dim)


def band(table):
    top = 96
    rows = 2 * LANES - top
    step = iota((rows, LANES), 0) + top - iota((rows, LANES), 1) - (LANES - PAD - 3)
    step = step.astype(F32) - table[TAPS : TAPS + 1, :]
    out = jnp.zeros((rows, LANES), F32)
    for tap in range(TAPS):
        out = jnp.where(step == float(tap), table[tap : tap + 1, :], out)
    return jnp.concatenate([jnp.zeros((top, LANES), BF16), out.astype(BF16)], axis=0)


def amplitude(real, imag):
    real, imag = real.astype(F32), imag.astype(F32)
    return jnp.sqrt(real * real + imag * imag + 1e-06).astype(BF16)


EVEN, LEFT, RIGHT, PICK = 4, 5, 6, 8


def prep_kernel(
    own_hbm, off_hbm, frac_hbm, partners_hbm, ref_ref, own_ref, cond_ref, taps_ref, low_ref, high_ref, *scratch
):
    off_ref, frac_ref, partners_ref, sems = scratch
    sources = (own_hbm, off_hbm, frac_hbm, partners_hbm)
    targets = (own_ref.at[0 : own_hbm.shape[0]], off_ref, frac_ref, partners_ref)
    copies = [pltpu.make_async_copy(s, t, sems.at[k]) for k, (s, t) in enumerate(zip(sources, targets))]
    for copy in copies:
        copy.start()
    for copy in copies[1:]:
        copy.wait()
    rows, cols = own_hbm.shape[0] // 2, own_ref.shape[1]
    blocks = cols // BLK
    date, dates = lax.axis_index("date"), lax.axis_size("date")
    place, places = lax.axis_index("rng"), lax.axis_size("rng")
    values = [jnp.where(date + 1 + h < dates, partners_ref[0, h], 0) for h in range(SPAN)]
    values += [1 - date % 2, (place > 0).astype(jnp.int32), (place < places - 1).astype(jnp.int32), jnp.int32(0)]
    beside = date + 1 - 2 * (date % 2)
    held = [date, beside, date + 2, date + 4, beside + 2, beside + 4]
    found = [(lax.rem(h, dates) == ref_ref[0]).astype(jnp.int32) for h in held]
    values += found[0:4] + [(found[4] + found[5]) * int(dates == 8)]
    row = iota(cond_ref.shape, 0)
    cond = jnp.zeros(cond_ref.shape, jnp.int32)
    for k, value in enumerate(values):
        cond = jnp.where(row == k, value, cond)
    cond_ref[...] = cond.astype(F32)
    dist = iota((TAPS, blocks), 0).astype(F32) - 3.0 - frac_ref[...]
    arg = jnp.pi * dist
    sinc = jnp.where(arg == 0.0, 1.0, jnp.sin(arg) / jnp.where(arg == 0.0, 1.0, arg))
    weights = sinc * (0.5 + 0.5 * jnp.cos(arg / 4.0))
    shifts = jnp.broadcast_to(off_ref[...].astype(F32), (TAPS, blocks))
    small = jnp.concatenate([weights, shifts], axis=0).astype(BF16)
    block, lane = iota((blocks, LANES), 0), iota((blocks, LANES), 1)
    taps_ref[...] = dot(small, (lane == block + 1).astype(BF16)).astype(BF16)
    low_ref[2 * rows :, :] = dot(small, (block == 0).astype(BF16)).astype(BF16)
    high_ref[2 * rows :, :] = dot(small, (block == blocks - 1).astype(BF16)).astype(BF16)
    copies[0].wait()
    low_ref[0 : 2 * rows, :] = own_ref[0 : 2 * rows, 0:LANES]
    high_ref[0 : 2 * rows, :] = own_ref[0 : 2 * rows, cols - LANES :]


def candidate_kernel(first, cond_ref, a_ref, b_ref, amp_ref):
    rows = amp_ref.shape[0]
    at = PICK + first
    a, b = cond_ref[at : at + 1, 0:1] > 0.0, cond_ref[at + 1 : at + 2, 0:1] > 0.0
    value = jnp.where(b, b_ref[0 : 2 * rows, :].astype(F32), a_ref[0 : 2 * rows, :].astype(F32))
    value = amplitude(value[0:rows], value[rows:])
    amp_ref[...] = jnp.where(a | b, value.astype(F32), 0.0).astype(BF16)


def join_kernel(halo_ref, main_ref, both_ref):
    rows, width = main_ref.shape[0], halo_ref.shape[1]
    both_ref[0:rows, :] = main_ref[...]
    both_ref[rows:, 0:width] = halo_ref[...]
    both_ref[rows:, width:] = jnp.zeros((HROWS, both_ref.shape[1] - width), BF16)


def halo_kernel(blocks, cond_ref, taps_ref, left_ref, right_ref, out_ref):
    left = jnp.where(cond_ref[LEFT : LEFT + 1, :] > 0.0, left_ref[...].astype(F32), 0.0)
    right = jnp.where(cond_ref[RIGHT : RIGHT + 1, :] > 0.0, right_ref[...].astype(F32), 0.0)
    rows = (left.shape[0] - HROWS) // 2
    lane = iota((2 * rows, LANES), 1)
    both = jnp.where(lane < EDGE, pltpu.roll(left[0 : 2 * rows], EDGE, 1), pltpu.roll(right[0 : 2 * rows], EDGE, 1))
    both = jnp.where(lane < 2 * EDGE, both, 0.0)
    both = (both[0:rows] + pltpu.roll(both[rows:], 2 * EDGE, 1)).astype(BF16)
    groups = rows // HROWS
    for k in range(groups):
        out_ref[:, k * LANES : (k + 1) * LANES] = both[k * HROWS : (k + 1) * HROWS]
    lane = iota((HROWS, LANES), 1)
    taps = jnp.where(lane == 0, left[2 * rows :], taps_ref[...].astype(F32))
    out_ref[:, groups * LANES : (groups + 1) * LANES] = jnp.where(
        lane == blocks + 1, right[2 * rows :], taps
    ).astype(BF16)


def resample(main_ref, halo_ref, use):
    rows, cols = main_ref.shape[0] // (2 * HROWS) * HROWS, main_ref.shape[1]
    rows -= rows % BLK
    main_ref, halo_ref = main_ref.at[0 : 2 * rows], halo_ref.at[halo_ref.shape[0] - HROWS :]
    tiles = cols // LANES
    groups = rows // HROWS
    edge = jnp.concatenate([halo_ref[:, k * LANES : (k + 1) * LANES] for k in range(groups)], axis=0).astype(F32)
    edge = [pltpu.roll(edge, LANES - EDGE, 1), pltpu.roll(edge, EDGE, 1)]
    edge = jnp.concatenate(edge, axis=0).astype(BF16)
    shape = (LANES, cols + LANES)
    place = ((iota(shape, 1) - PAD) >> 6) + 1 == iota(shape, 0)
    table = dot(halo_ref[:, groups * LANES : (groups + 1) * LANES], place.astype(BF16))
    for p in range(tiles + 1):
        if p == 0:
            window = jnp.concatenate([edge, main_ref[:, 0:LANES]], axis=1)
        elif p == tiles:
            window = jnp.concatenate([main_ref[:, cols - LANES :], edge], axis=1)
        else:
            window = main_ref[:, (p - 1) * LANES : (p + 1) * LANES]
        out = dot(window, band(table[:, p * LANES : (p + 1) * LANES])).astype(BF16)
        use(p, out[0:rows], out[rows:])


def range_box():
    gap = iota((2 * LANES, LANES), 0) - iota((2 * LANES, LANES), 1) - PAD
    return (jnp.abs(gap) <= BOXR // 2).astype(BF16)


def line_box(field):
    rows, lanes = field.shape
    base = jnp.concatenate([field, jnp.zeros((8, lanes), F32)], axis=0)
    two = base + pltpu.roll(base, 1, 0)
    four = two + pltpu.roll(two, 2, 0)
    five = four + pltpu.roll(base, 4, 0)
    return pltpu.roll(five, rows + 8 - BOXA // 2, 0)[0:rows]


def keep_tile(ext_ref, p, real, imag):
    rows, lanes = real.shape[0], slice(p * LANES, (p + 1) * LANES)
    ext_ref[0:rows, lanes] = real
    ext_ref[rows:, lanes] = imag


def power_tile(fields_ref, p, real, imag):
    real, imag = real.astype(F32), imag.astype(F32)
    fields_ref[:, p * LANES : (p + 1) * LANES] = (real * real + imag * imag).astype(BF16)


def cross_tile(fields_ref, ext_ref, p, real, imag):
    rows, lanes = real.shape[0], slice(p * LANES, (p + 1) * LANES)
    own_r, own_i = ext_ref[0:rows, lanes].astype(F32), ext_ref[rows:, lanes].astype(F32)
    r, i = real.astype(F32), imag.astype(F32)
    fields_ref[0:rows, lanes] = (own_r * r + own_i * i).astype(BF16)
    fields_ref[rows : 2 * rows, lanes] = (own_i * r - own_r * i).astype(BF16)


def coherence(sums, own, partner):
    rows = own.shape[0]
    re, im = line_box(sums[0:rows]), line_box(sums[rows : 2 * rows])
    return ((re * re + im * im) / (own * partner + 1e-06)).astype(BF16)


def own_kernel(earlier_ref, main_ref, halo_ref, ext_ref, power_ref, fields_ref):
    del earlier_ref
    rows, cols = power_ref.shape

    def use(p, real, imag):
        keep_tile(ext_ref, p, real, imag)
        power_tile(fields_ref, p, real, imag)

    resample(main_ref, halo_ref, use)
    box = range_box()
    for p in range(cols // LANES):
        lanes = slice(p * LANES, (p + 1) * LANES)
        power_ref[:, lanes] = line_box(dot(fields_ref[:, p * LANES : (p + 2) * LANES], box))


def pair_kernel(own_ref, own_power_ref, main_ref, halo_ref, ext_ref, power_ref, out_ref, fields_ref):
    rows, cols = out_ref.shape

    def use(p, real, imag):
        keep_tile(ext_ref, p, real, imag)
        power_tile(fields_ref.at[2 * rows :], p, real, imag)
        cross_tile(fields_ref, own_ref, p, real, imag)

    resample(main_ref, halo_ref, use)
    box = range_box()
    for p in range(cols // LANES):
        lanes = slice(p * LANES, (p + 1) * LANES)
        sums = dot(fields_ref[:, p * LANES : (p + 2) * LANES], box)
        power = line_box(sums[2 * rows :])
        power_ref[:, lanes] = power
        out_ref[:, lanes] = coherence(sums, own_power_ref[:, lanes], power)


def beside_kernel(earlier_ref, *refs):
    del earlier_ref
    pair_kernel(*refs)


def again_kernel(own_ref, own_power_ref, ext_ref, power_ref, out_ref, fields_ref):
    rows, cols = out_ref.shape
    for p in range(cols // LANES + 1):
        lanes = slice(p * LANES, (p + 1) * LANES)
        cross_tile(fields_ref, own_ref, p, ext_ref[0:rows, lanes], ext_ref[rows:, lanes])
    box = range_box()
    for p in range(cols // LANES):
        lanes = slice(p * LANES, (p + 1) * LANES)
        sums = dot(fields_ref[:, p * LANES : (p + 2) * LANES], box)
        out_ref[:, lanes] = coherence(sums, own_power_ref[:, lanes], power_ref[:, lanes])


def place_kernel(
    cond_ref, surface_ref, beside_ref, two_ref, four_ref, near_ref, far_ref, surface_hbm, out_hbm, out_ref, sems
):
    copies = [pltpu.make_async_copy(surface_ref, surface_hbm, sems.at[SPAN])]
    copies += [pltpu.make_async_copy(out_ref.at[h], out_hbm.at[h], sems.at[h]) for h in range(SPAN)]
    copies[0].start()
    even = cond_ref[EVEN : EVEN + 1, 0:1] > 0.0
    near = near_ref[...].astype(F32)
    fields = [
        lambda: jnp.where(even, beside_ref[...].astype(F32), near),
        lambda: two_ref[...].astype(F32),
        lambda: jnp.where(even, near, far_ref[...].astype(F32)),
        lambda: four_ref[...].astype(F32),
    ]
    for h, value in enumerate(fields):
        out_ref[h] = (value() * cond_ref[h : h + 1, 0:1]).astype(BF16)
        copies[1 + h].start()
    for copy in copies:
        copy.wait()


def split(table):
    high = table.astype(BF16)
    return high, (table - high.astype(np.float32)).astype(BF16)


def twice(table):
    zero = np.zeros_like(table)
    return np.block([[table, zero], [zero, table]])


def surface_tables():
    index = np.arange(BLK)
    angle = 2.0 * np.pi / BLK * (index[:, None] * index[None, :] % BLK)
    cosine, sine = np.cos(angle).astype(np.float32), np.sin(angle).astype(np.float32)
    signed = np.where(index < BLK // 2, index, index - BLK)
    upsampled = OVS * BLK
    lag_phase = (np.arange(LAGS) - LAGS // 2)[:, None] * signed[None, :] % upsampled
    lag_angle = 2.0 * np.pi / upsampled * lag_phase
    lag_cos, lag_sin = np.cos(lag_angle).astype(np.float32), np.sin(lag_angle).astype(np.float32)
    high, low = split(np.concatenate([cosine, -sine], axis=0))
    first = np.concatenate([high, low, high], axis=1)
    second = np.concatenate(split(np.concatenate([twice(cosine), twice(sine)], axis=1)), axis=0)
    per = LANES // LAGS
    order = np.arange(LAGS).reshape(LAGS // per, per).T.reshape(-1)
    left = np.block([[lag_cos[order], -lag_sin[order]], [lag_sin[order], lag_cos[order]]])
    third = np.concatenate(split(left), axis=1)
    spread = [twice(np.tile(table.T, (1, per))) for table in (lag_cos, -lag_sin)]
    fourth = np.concatenate(split(np.concatenate(spread, axis=0)), axis=0)
    return first, second, third, fourth


def spectrum(amp_ref, rows_ref, first_ref, second_ref, use):
    size, cols = amp_ref.shape
    tiles = cols // LANES
    group = (iota((LANES, LANES), 0) >> 6 == iota((LANES, LANES), 1) >> 6).astype(F32)
    values = [amp_ref[:, p * LANES : (p + 1) * LANES].astype(F32) for p in range(tiles)]
    for p, value in enumerate(values):
        rows_ref[p : p + 1, :] = jnp.sum(value, axis=0, keepdims=True)
    mean = jnp.dot(rows_ref[...], group, precision=HIGHEST) / (BLK * BLK)
    parts = [[], []]
    for p, value in enumerate(values):
        value = value - mean[p : p + 1, :]
        rows_ref[p : p + 1, :] = jnp.sum(value * value, axis=0, keepdims=True)
        parts[0].append(value.astype(BF16))
        parts[1].append((value - parts[0][p].astype(F32)).astype(BF16))
    high, low = (jnp.concatenate(part, axis=1) for part in parts)
    f = dot(first_ref[...], jnp.concatenate([high, high, low], axis=0)).astype(BF16)
    f = jnp.concatenate([f[:, p * LANES : (p + 1) * LANES] for p in range(tiles)], axis=0)
    s = dot(jnp.concatenate([f, f], axis=1), second_ref[...])
    for p in range(tiles):
        at = 2 * size * p
        top, bottom = s[at : at + size], s[at + size : at + 2 * size]
        use(p, top[:, 0:LANES] + bottom[:, LANES:], bottom[:, 0:LANES] - top[:, LANES:])
    return jnp.dot(rows_ref[...], group, precision=HIGHEST)


def spectrum_kernel(own_ref, first_ref, second_ref, third_ref, fourth_ref, spec_ref, energy_ref, amp_ref, rows_ref):
    del third_ref, fourth_ref
    size = amp_ref.shape[0]
    amp_ref[...] = amplitude(own_ref[0:size, :], own_ref[size : 2 * size, :])

    def use(p, real, imag):
        lanes = slice(p * LANES, (p + 1) * LANES)
        spec_ref[0:size, lanes] = real
        spec_ref[size:, lanes] = imag

    energy_ref[...] = spectrum(amp_ref, rows_ref, first_ref, second_ref, use)


def surface_kernel(cond_ref, *refs):
    samples, across_ref, before_ref, refs = refs[0:4], refs[4], refs[5], refs[6:]
    spec_ref, energy_ref, first_ref, second_ref, third_ref, fourth_ref, out_ref = refs[0:7]
    amp_ref, rows_ref, cross_ref, out_scr = refs[7:]
    size, cols = amp_ref.shape
    tiles = cols // LANES
    picks = [cond_ref[PICK + k : PICK + k + 1, 0:1] > 0.0 for k in range(len(samples) + 1)]
    value = samples[0][0 : 2 * size, :].astype(F32)
    for pick, ref in zip(picks[1:4], samples[1:]):
        value = jnp.where(pick, ref[0 : 2 * size, :].astype(F32), value)
    found = functools.reduce(jnp.logical_or, picks[0:4])
    value = amplitude(value[0:size], value[size:]).astype(F32)
    other = jnp.where(picks[4], across_ref[...].astype(F32), before_ref[...].astype(F32))
    amp_ref[...] = jnp.where(found, value, other).astype(BF16)

    def use(p, ref_r, ref_i):
        lanes = slice(p * LANES, (p + 1) * LANES)
        own_r, own_i = spec_ref[0:size, lanes], spec_ref[size:, lanes]
        cross_ref[0:size, lanes] = own_r * ref_r + own_i * ref_i
        cross_ref[size:, lanes] = own_i * ref_r - own_r * ref_i

    energy = spectrum(amp_ref, rows_ref, first_ref, second_ref, use)
    scale = 1.0 / (BLK * jnp.sqrt(energy_ref[...] * energy + 1e-06))
    lag_rows = [[] for _ in range(LANES // LAGS)]
    cross = [cross_ref[:, p * LANES : (p + 1) * LANES] * scale[p : p + 1, :] for p in range(tiles)]
    cross = jnp.concatenate([value.astype(BF16) for value in cross], axis=1)
    lags = dot(third_ref[...], jnp.concatenate([cross, cross], axis=0))
    for p in range(tiles):
        for q in range(LANES // LAGS):
            at = [ri * LAGS + q * 8 for ri in range(2)]
            part = [lags[k : k + 8, p * LANES : (p + 1) * LANES] for k in at]
            lag_rows[q].append(jnp.concatenate(part, axis=1))
    lhs = jnp.concatenate([row for rows in lag_rows for row in rows], axis=0).astype(BF16)
    result = dot(jnp.concatenate([lhs, lhs], axis=1), fourth_ref[...])
    height = 8 * tiles
    quarter = iota((height, 2 * LANES), 1) % LANES // LAGS
    total = result[0:height]
    for q in range(1, LANES // LAGS):
        total = jnp.where(quarter == q, result[q * height : (q + 1) * height], total)
    for p in range(tiles):
        for jj in range(2):
            at = (2 * p + jj) * 8
            out_scr[at : at + 8, :] = total[p * 8 : p * 8 + 8, jj * LANES : (jj + 1) * LANES]
    for a in range(8):
        out_ref[:, a * LANES : (a + 1) * LANES] = out_scr[pl.ds(a, 2 * tiles, stride=8), :]


def shifted(value, axis, steps):
    count = lax.axis_size(axis)
    return lax.ppermute(value, axis, [(s, (s - steps) % count) for s in range(count)])


def swapped(value, axis, step):
    return lax.ppermute(value, axis, [(s, s ^ step) for s in range(lax.axis_size(axis))])


def spread(value, axis):
    count = lax.axis_size(axis)
    step = 2
    while step < count:
        value = jnp.maximum(value, swapped(value, axis, step))
        step *= 2
    return value


def call(kernel, name, out_shape, operands, scratch=()):
    return pl.pallas_call(
        kernel,
        out_shape=out_shape,
        in_specs=[VMEM] * len(operands),
        out_specs=jax.tree.map(lambda _: VMEM, out_shape),
        scratch_shapes=[pltpu.VMEM(*s) for s in scratch],
        compiler_params=PARAMS,
        name=name,
    )(*operands)


def body(slc, ref_date, int_offset, frac_offset, partners):
    sds = jax.ShapeDtypeStruct
    _, _, rows, cols = slc.shape
    tiles = cols // LANES
    dates = lax.axis_size("date")
    even = lax.axis_index("date") % 2 == 0
    field, samples = sds((rows, cols), BF16), sds((2 * rows, cols), BF16)
    payload = sds((2 * rows + HROWS, LANES), BF16)
    inputs = (slc.reshape(2 * rows, cols), int_offset[0], frac_offset[0], partners)
    inputs = [pltpu.with_memory_space_constraint(v, pltpu.HBM) for v in inputs]
    own, cond, taps, low, high = pl.pallas_call(
        prep_kernel,
        out_shape=(sds((2 * rows + 32, cols), BF16), sds((16, LANES), F32), sds((HROWS, LANES), BF16), payload, payload),
        in_specs=[pl.BlockSpec(memory_space=pltpu.HBM)] * 4 + [SMEM],
        out_specs=(VMEM,) * 5,
        scratch_shapes=[
            pltpu.VMEM(int_offset.shape[1:], jnp.int32),
            pltpu.VMEM(frac_offset.shape[1:], F32),
            pltpu.SMEM(partners.shape, jnp.int32),
            pltpu.SemaphoreType.DMA((4,)),
        ],
        compiler_params=PARAMS,
        name="prepare",
    )(*inputs, ref_date)
    beside = swapped(own, "date", 1)
    two = shifted(slc.reshape(2 * rows, cols), "date", 2)
    right = shifted(low, "rng", 1)
    left = shifted(high, "rng", -1)
    width = (rows // HROWS + 1) * LANES
    halo = call(
        functools.partial(halo_kernel, cols // BLK), "halo", sds((HROWS, width), BF16), (cond, taps, left, right)
    )
    joined = sds((2 * rows + HROWS, cols), BF16)
    four = shifted(call(join_kernel, "join", joined, (halo, two)), "date", 2)
    beside_halo = swapped(halo, "date", 1)
    four_halo = shifted(halo, "date", 4)
    amp = call(functools.partial(candidate_kernel, 0), "candidate", field, (cond, own, beside))
    before = shifted(amp, "date", -2) if dates == 8 else spread(amp, "date")
    later = call(functools.partial(candidate_kernel, 2), "later", field, (cond, two, four))
    across = swapped(later, "date", 1)
    first, second, third, fourth = [jnp.asarray(t) for t in surface_tables()]
    spec, energy = call(
        spectrum_kernel,
        "spectrum",
        (sds((2 * rows, cols), F32), sds((tiles, LANES), F32)),
        (own, first, second, third, fourth),
        [((rows, cols), BF16), ((tiles, LANES), F32)],
    )
    resampled = (sds((2 * rows, cols + LANES), BF16), sds((rows, cols), F32))
    scratch = [[((k * rows, cols + LANES), BF16)] for k in range(4)]
    own_ext = call(own_kernel, "own", resampled, (amp, own, halo), scratch[1])
    *beside_ext, coh_beside = call(
        beside_kernel, "beside", (*resampled, field), (energy, *own_ext, beside, beside_halo), scratch[3]
    )
    *two_ext, coh_near = call(pair_kernel, "near", (*resampled, field), (*beside_ext, two, four), scratch[3])
    near = swapped(coh_near, "date", 1)
    coh_two = call(again_kernel, "two", field, (*own_ext, *two_ext), scratch[2])
    *four_ext, coh_far = call(pair_kernel, "far", (*resampled, field), (*beside_ext, four, four_halo), scratch[3])
    far = swapped(coh_far, "date", 1)
    coh_four = call(again_kernel, "four", field, (*own_ext, *four_ext), scratch[2])
    surface = call(
        surface_kernel,
        "surface",
        sds((cols // BLK, LAGS * LAGS), F32),
        (cond, own, beside, two, four, across, before, spec, energy, first, second, third, fourth),
        [
            ((rows, cols), BF16),
            ((tiles, LANES), F32),
            ((2 * rows, cols), F32),
            ((8 * cols // BLK, LANES), F32),
        ],
    )
    operands = (cond, surface, coh_beside, coh_two, coh_four, near, far)
    surface, fields = pl.pallas_call(
        place_kernel,
        out_shape=(sds(surface.shape, F32), sds((SPAN, rows, cols), BF16)),
        in_specs=[VMEM] * len(operands),
        out_specs=(pl.BlockSpec(memory_space=pl.ANY),) * 2,
        scratch_shapes=[pltpu.VMEM((SPAN, rows, cols), BF16), pltpu.SemaphoreType.DMA((SPAN + 1,))],
        compiler_params=PARAMS,
        name="place",
    )(*operands)
    return (surface[None, None], fields[None])


def solution(mesh):
    in_specs = (
        P("date", None, None, "rng"),
        P(),
        P("date", None, "rng"),
        P("date", None, "rng"),
        P("date", None),
    )
    out_specs = (P("date", None, "rng", None), P("date", None, None, "rng"))
    return jax.shard_map(body, mesh=mesh, in_specs=in_specs, out_specs=out_specs, check_vma=False)
```

```python
import functools

import jax
import jax.numpy as jnp
import numpy as np
from jax import lax
from jax.experimental import pallas as pl
from jax.experimental.pallas import tpu as pltpu
from jax.sharding import PartitionSpec as P

BLK = 64
OVS = 2
LAGS = 32
SPAN = 4
BOXA = 5
BOXR = 19
TAPS = 8
LANES = 128
PAD = 16
EDGE = 32
HROWS = 16
F32 = jnp.float32
BF16 = jnp.bfloat16
HIGHEST = lax.Precision.HIGHEST
VMEM = pl.BlockSpec(memory_space=pltpu.VMEM)
SMEM = pl.BlockSpec(memory_space=pltpu.SMEM)
PARAMS = pltpu.CompilerParams(vmem_limit_bytes=8 << 20)


def dot(a, b):
    return jnp.dot(a, b, preferred_element_type=F32)


def iota(shape, dim):
    return lax.broadcasted_iota(jnp.int32, shape, dim)


def band(table):
    top = 96
    rows = 2 * LANES - top
    step = iota((rows, LANES), 0) + top - iota((rows, LANES), 1) - (LANES - PAD - 3)
    table = table.astype(BF16)
    step = step.astype(F32).astype(BF16) - table[TAPS : TAPS + 1, :]
    out = jnp.zeros((rows, LANES), BF16)
    for tap in range(TAPS):
        out = jnp.where(step == jnp.asarray(tap, BF16), table[tap : tap + 1, :], out)
    return jnp.concatenate([jnp.zeros((top, LANES), BF16), out], axis=0)


def amplitude(real, imag):
    real, imag = real.astype(F32), imag.astype(F32)
    return jnp.sqrt(real * real + imag * imag + 1e-06).astype(BF16)


EVEN, LEFT, RIGHT, PICK = 4, 5, 6, 8


def prep_kernel(
    own_hbm, off_hbm, frac_hbm, partners_hbm, ref_ref, own_ref, cond_ref, taps_ref, low_ref, high_ref, *scratch
):
    off_ref, frac_ref, partners_ref, sems = scratch
    sources = (own_hbm, off_hbm, frac_hbm, partners_hbm)
    targets = (own_ref.at[0 : own_hbm.shape[0]], off_ref, frac_ref, partners_ref)
    copies = [pltpu.make_async_copy(s, t, sems.at[k]) for k, (s, t) in enumerate(zip(sources, targets))]
    for copy in copies:
        copy.start()
    for copy in copies[1:]:
        copy.wait()
    rows, cols = own_hbm.shape[0] // 2, own_ref.shape[1]
    blocks = cols // BLK
    date, dates = lax.axis_index("date"), lax.axis_size("date")
    place, places = lax.axis_index("rng"), lax.axis_size("rng")
    values = [jnp.where(date + 1 + h < dates, partners_ref[0, h], 0) for h in range(SPAN)]
    values += [1 - date % 2, (place > 0).astype(jnp.int32), (place < places - 1).astype(jnp.int32), jnp.int32(0)]
    beside = date + 1 - 2 * (date % 2)
    held = [date, beside, date + 2, date + 4, beside + 2, beside + 4]
    found = [(lax.rem(h, dates) == ref_ref[0]).astype(jnp.int32) for h in held]
    values += found[0:4] + [(found[4] + found[5]) * int(dates == 8)]
    row = iota(cond_ref.shape, 0)
    cond = jnp.zeros(cond_ref.shape, jnp.int32)
    for k, value in enumerate(values):
        cond = jnp.where(row == k, value, cond)
    cond_ref[...] = cond.astype(F32)
    dist = iota((TAPS, blocks), 0).astype(F32) - 3.0 - frac_ref[...]
    arg = jnp.pi * dist
    sinc = jnp.where(arg == 0.0, 1.0, jnp.sin(arg) / jnp.where(arg == 0.0, 1.0, arg))
    weights = sinc * (0.5 + 0.5 * jnp.cos(arg / 4.0))
    shifts = jnp.broadcast_to(off_ref[...].astype(F32), (TAPS, blocks))
    small = jnp.concatenate([weights, shifts], axis=0).astype(BF16)
    block, lane = iota((blocks, LANES), 0), iota((blocks, LANES), 1)
    taps_ref[...] = dot(small, (lane == block + 1).astype(BF16)).astype(BF16)
    low_ref[2 * rows :, :] = dot(small, (block == 0).astype(BF16)).astype(BF16)
    high_ref[2 * rows :, :] = dot(small, (block == blocks - 1).astype(BF16)).astype(BF16)
    copies[0].wait()
    low_ref[0 : 2 * rows, :] = own_ref[0 : 2 * rows, 0:LANES]
    high_ref[0 : 2 * rows, :] = own_ref[0 : 2 * rows, cols - LANES :]


def candidate_kernel(picks, cond_ref, a_ref, b_ref, amp_ref):
    rows = amp_ref.shape[0]
    a, b = (cond_ref[PICK + k : PICK + k + 1, 0:1] > 0.0 for k in picks)
    value = jnp.where(b, b_ref[0 : 2 * rows, :].astype(F32), a_ref[0 : 2 * rows, :].astype(F32))
    value = amplitude(value[0:rows], value[rows:])
    amp_ref[...] = jnp.where(a | b, value.astype(F32), 0.0).astype(BF16)


def join_kernel(halo_ref, main_ref, both_ref):
    rows, width = main_ref.shape[0], halo_ref.shape[1]
    both_ref[0:rows, :] = main_ref[...]
    both_ref[rows:, 0:width] = halo_ref[...]
    both_ref[rows:, width:] = jnp.zeros((HROWS, both_ref.shape[1] - width), BF16)


def halo_kernel(blocks, cond_ref, taps_ref, left_ref, right_ref, out_ref):
    left = jnp.where(cond_ref[LEFT : LEFT + 1, :] > 0.0, left_ref[...].astype(F32), 0.0)
    right = jnp.where(cond_ref[RIGHT : RIGHT + 1, :] > 0.0, right_ref[...].astype(F32), 0.0)
    rows = (left.shape[0] - HROWS) // 2
    lane = iota((2 * rows, LANES), 1)
    both = jnp.where(lane < EDGE, pltpu.roll(left[0 : 2 * rows], EDGE, 1), pltpu.roll(right[0 : 2 * rows], EDGE, 1))
    both = jnp.where(lane < 2 * EDGE, both, 0.0)
    both = (both[0:rows] + pltpu.roll(both[rows:], 2 * EDGE, 1)).astype(BF16)
    groups = rows // HROWS
    for k in range(groups):
        out_ref[:, k * LANES : (k + 1) * LANES] = both[k * HROWS : (k + 1) * HROWS]
    lane = iota((HROWS, LANES), 1)
    taps = jnp.where(lane == 0, left[2 * rows :], taps_ref[...].astype(F32))
    out_ref[:, groups * LANES : (groups + 1) * LANES] = jnp.where(
        lane == blocks + 1, right[2 * rows :], taps
    ).astype(BF16)


def resample(main_ref, halo_ref, use):
    rows, cols = main_ref.shape[0] // (2 * HROWS) * HROWS, main_ref.shape[1]
    rows -= rows % BLK
    main_ref, halo_ref = main_ref.at[0 : 2 * rows], halo_ref.at[halo_ref.shape[0] - HROWS :]
    tiles = cols // LANES
    groups = rows // HROWS
    edge = jnp.concatenate([halo_ref[:, k * LANES : (k + 1) * LANES] for k in range(groups)], axis=0).astype(F32)
    edge = [pltpu.roll(edge, LANES - EDGE, 1), pltpu.roll(edge, EDGE, 1)]
    edge = jnp.concatenate(edge, axis=0).astype(BF16)
    shape = (LANES, cols + LANES)
    place = ((iota(shape, 1) - PAD) >> 6) + 1 == iota(shape, 0)
    table = dot(halo_ref[:, groups * LANES : (groups + 1) * LANES], place.astype(BF16))
    for p in range(tiles + 1):
        if p == 0:
            window = jnp.concatenate([edge, main_ref[:, 0:LANES]], axis=1)
        elif p == tiles:
            window = jnp.concatenate([main_ref[:, cols - LANES :], edge], axis=1)
        else:
            window = main_ref[:, (p - 1) * LANES : (p + 1) * LANES]
        out = dot(window, band(table[:, p * LANES : (p + 1) * LANES])).astype(BF16)
        use(p, out[0:rows], out[rows:])


def range_box():
    gap = iota((2 * LANES, LANES), 0) - iota((2 * LANES, LANES), 1) - PAD
    return (jnp.abs(gap) <= BOXR // 2).astype(BF16)


def line_box(field):
    rows, lanes = field.shape
    base = jnp.concatenate([field, jnp.zeros((8, lanes), F32)], axis=0)
    two = base + pltpu.roll(base, 1, 0)
    four = two + pltpu.roll(two, rows + 8 - BOXA // 2, 0)
    return (four + pltpu.roll(base, BOXA // 2, 0))[0:rows]


def keep_tile(ext_ref, p, real, imag):
    rows, lanes = real.shape[0], slice(p * LANES, (p + 1) * LANES)
    ext_ref[0:rows, lanes] = real
    ext_ref[rows:, lanes] = imag


def power_tile(fields_ref, p, real, imag):
    real, imag = real.astype(F32), imag.astype(F32)
    fields_ref[:, p * LANES : (p + 1) * LANES] = (real * real + imag * imag).astype(BF16)


def cross_tile(fields_ref, ext_ref, p, real, imag):
    rows, lanes = real.shape[0], slice(p * LANES, (p + 1) * LANES)
    own_r, own_i = ext_ref[0:rows, lanes].astype(F32), ext_ref[rows:, lanes].astype(F32)
    r, i = real.astype(F32), imag.astype(F32)
    fields_ref[0:rows, lanes] = (own_r * r + own_i * i).astype(BF16)
    fields_ref[rows : 2 * rows, lanes] = (own_i * r - own_r * i).astype(BF16)


def coherence(sums, own, partner):
    rows = own.shape[0]
    re, im = line_box(sums[0:rows]), line_box(sums[rows : 2 * rows])
    return ((re * re + im * im) / (own * partner + 1e-06)).astype(BF16)


def late_candidate_kernel(picks, earlier_ref, *refs):
    del earlier_ref
    candidate_kernel(picks, *refs)


def own_kernel(earlier_ref, main_ref, halo_ref, ext_ref, power_ref, fields_ref):
    del earlier_ref
    rows, cols = power_ref.shape

    def use(p, real, imag):
        keep_tile(ext_ref, p, real, imag)
        power_tile(fields_ref, p, real, imag)

    resample(main_ref, halo_ref, use)
    box = range_box()
    for p in range(cols // LANES):
        lanes = slice(p * LANES, (p + 1) * LANES)
        power_ref[:, lanes] = line_box(dot(fields_ref[:, p * LANES : (p + 2) * LANES], box))


def pair_kernel(own_ref, own_power_ref, main_ref, halo_ref, ext_ref, power_ref, out_ref, fields_ref):
    rows, cols = out_ref.shape

    def use(p, real, imag):
        keep_tile(ext_ref, p, real, imag)
        power_tile(fields_ref.at[2 * rows :], p, real, imag)
        cross_tile(fields_ref, own_ref, p, real, imag)

    resample(main_ref, halo_ref, use)
    box = range_box()
    for p in range(cols // LANES):
        lanes = slice(p * LANES, (p + 1) * LANES)
        sums = dot(fields_ref[:, p * LANES : (p + 2) * LANES], box)
        power = line_box(sums[2 * rows :])
        power_ref[:, lanes] = power
        out_ref[:, lanes] = coherence(sums, own_power_ref[:, lanes], power)


def beside_kernel(earlier_ref, *refs):
    del earlier_ref
    pair_kernel(*refs)


def again_kernel(own_ref, own_power_ref, ext_ref, power_ref, out_ref, fields_ref):
    rows, cols = out_ref.shape
    for p in range(cols // LANES + 1):
        lanes = slice(p * LANES, (p + 1) * LANES)
        cross_tile(fields_ref, own_ref, p, ext_ref[0:rows, lanes], ext_ref[rows:, lanes])
    box = range_box()
    for p in range(cols // LANES):
        lanes = slice(p * LANES, (p + 1) * LANES)
        sums = dot(fields_ref[:, p * LANES : (p + 2) * LANES], box)
        out_ref[:, lanes] = coherence(sums, own_power_ref[:, lanes], power_ref[:, lanes])


def place_kernel(
    cond_ref, surface_ref, beside_ref, two_ref, four_ref, near_ref, far_ref, surface_hbm, out_hbm, out_ref, sems
):
    copies = [pltpu.make_async_copy(surface_ref, surface_hbm, sems.at[SPAN])]
    copies += [pltpu.make_async_copy(out_ref.at[h], out_hbm.at[h], sems.at[h]) for h in range(SPAN)]
    copies[0].start()
    even = cond_ref[EVEN : EVEN + 1, 0:1] > 0.0
    near = near_ref[...].astype(F32)
    fields = [
        lambda: jnp.where(even, beside_ref[...].astype(F32), near),
        lambda: two_ref[...].astype(F32),
        lambda: jnp.where(even, near, far_ref[...].astype(F32)),
        lambda: four_ref[...].astype(F32),
    ]
    for h, value in enumerate(fields):
        out_ref[h] = (value() * cond_ref[h : h + 1, 0:1]).astype(BF16)
        copies[1 + h].start()
    for copy in copies:
        copy.wait()


def split(table):
    high = table.astype(BF16)
    return high, (table - high.astype(np.float32)).astype(BF16)


def twice(table):
    zero = np.zeros_like(table)
    return np.block([[table, zero], [zero, table]])


def surface_tables():
    index = np.arange(BLK)
    angle = 2.0 * np.pi / BLK * (index[:, None] * index[None, :] % BLK)
    cosine, sine = np.cos(angle).astype(np.float32), np.sin(angle).astype(np.float32)
    signed = np.where(index < BLK // 2, index, index - BLK)
    upsampled = OVS * BLK
    lag_phase = (np.arange(LAGS) - LAGS // 2)[:, None] * signed[None, :] % upsampled
    lag_angle = 2.0 * np.pi / upsampled * lag_phase
    lag_cos, lag_sin = np.cos(lag_angle).astype(np.float32), np.sin(lag_angle).astype(np.float32)
    high, low = split(np.concatenate([cosine, -sine], axis=0))
    first = np.concatenate([high, low, high], axis=1)
    second = np.concatenate(split(np.concatenate([twice(cosine), twice(sine)], axis=1)), axis=0)
    per = LANES // LAGS
    order = np.arange(LAGS).reshape(LAGS // per, per).T.reshape(-1)
    left = np.block([[lag_cos[order], -lag_sin[order]], [lag_sin[order], lag_cos[order]]])
    third = np.concatenate(split(left), axis=1)
    spread = [twice(np.tile(table.T, (1, per))) for table in (lag_cos, -lag_sin)]
    fourth = np.concatenate(split(np.concatenate(spread, axis=0)), axis=0)
    return first, second, third, fourth


def spectrum(amp_ref, rows_ref, first_ref, second_ref, use):
    size, cols = amp_ref.shape
    tiles = cols // LANES
    group = (iota((LANES, LANES), 0) >> 6 == iota((LANES, LANES), 1) >> 6).astype(F32)
    values = [amp_ref[:, p * LANES : (p + 1) * LANES].astype(F32) for p in range(tiles)]
    for p, value in enumerate(values):
        rows_ref[p : p + 1, :] = jnp.sum(value, axis=0, keepdims=True)
    mean = jnp.dot(rows_ref[...], group, precision=HIGHEST) / (BLK * BLK)
    parts = [[], []]
    for p, value in enumerate(values):
        value = value - mean[p : p + 1, :]
        rows_ref[p : p + 1, :] = jnp.sum(value * value, axis=0, keepdims=True)
        parts[0].append(value.astype(BF16))
        parts[1].append((value - parts[0][p].astype(F32)).astype(BF16))
    high, low = (jnp.concatenate(part, axis=1) for part in parts)
    f = dot(first_ref[...], jnp.concatenate([high, high, low], axis=0)).astype(BF16)
    f = jnp.concatenate([f[:, p * LANES : (p + 1) * LANES] for p in range(tiles)], axis=0)
    s = dot(jnp.concatenate([f, f], axis=1), second_ref[...])
    for p in range(tiles):
        at = 2 * size * p
        top, bottom = s[at : at + size], s[at + size : at + 2 * size]
        use(p, top[:, 0:LANES] + bottom[:, LANES:], bottom[:, 0:LANES] - top[:, LANES:])
    return jnp.dot(rows_ref[...], group, precision=HIGHEST)


def spectrum_kernel(own_ref, first_ref, second_ref, third_ref, fourth_ref, spec_ref, energy_ref, amp_ref, rows_ref):
    del third_ref, fourth_ref
    size = amp_ref.shape[0]
    amp_ref[...] = amplitude(own_ref[0:size, :], own_ref[size : 2 * size, :])

    def use(p, real, imag):
        lanes = slice(p * LANES, (p + 1) * LANES)
        spec_ref[0:size, lanes] = real
        spec_ref[size:, lanes] = imag

    energy_ref[...] = spectrum(amp_ref, rows_ref, first_ref, second_ref, use)


def surface_kernel(cond_ref, *refs):
    samples, across_ref, before_ref, refs = refs[0:4], refs[4], refs[5], refs[6:]
    spec_ref, energy_ref, first_ref, second_ref, third_ref, fourth_ref, out_ref = refs[0:7]
    amp_ref, rows_ref, cross_ref, out_scr = refs[7:]
    size, cols = amp_ref.shape
    tiles = cols // LANES
    picks = [cond_ref[PICK + k : PICK + k + 1, 0:1] > 0.0 for k in range(len(samples) + 1)]
    value = samples[0][0 : 2 * size, :].astype(F32)
    for pick, ref in zip(picks[1:4], samples[1:]):
        value = jnp.where(pick, ref[0 : 2 * size, :].astype(F32), value)
    found = functools.reduce(jnp.logical_or, picks[0:4])
    value = amplitude(value[0:size], value[size:]).astype(F32)
    other = jnp.where(picks[4], across_ref[...].astype(F32), before_ref[...].astype(F32))
    amp_ref[...] = jnp.where(found, value, other).astype(BF16)

    def use(p, ref_r, ref_i):
        lanes = slice(p * LANES, (p + 1) * LANES)
        own_r, own_i = spec_ref[0:size, lanes], spec_ref[size:, lanes]
        cross_ref[0:size, lanes] = own_r * ref_r + own_i * ref_i
        cross_ref[size:, lanes] = own_i * ref_r - own_r * ref_i

    energy = spectrum(amp_ref, rows_ref, first_ref, second_ref, use)
    scale = 1.0 / (BLK * jnp.sqrt(energy_ref[...] * energy + 1e-06))
    lag_rows = [[] for _ in range(LANES // LAGS)]
    cross = [cross_ref[:, p * LANES : (p + 1) * LANES] * scale[p : p + 1, :] for p in range(tiles)]
    cross = jnp.concatenate([value.astype(BF16) for value in cross], axis=1)
    lags = dot(third_ref[...], jnp.concatenate([cross, cross], axis=0))
    for p in range(tiles):
        for q in range(LANES // LAGS):
            at = [ri * LAGS + q * 8 for ri in range(2)]
            part = [lags[k : k + 8, p * LANES : (p + 1) * LANES] for k in at]
            lag_rows[q].append(jnp.concatenate(part, axis=1))
    lhs = jnp.concatenate([row for rows in lag_rows for row in rows], axis=0).astype(BF16)
    result = dot(jnp.concatenate([lhs, lhs], axis=1), fourth_ref[...])
    height = 8 * tiles
    quarter = iota((height, 2 * LANES), 1) % LANES // LAGS
    total = result[0:height]
    for q in range(1, LANES // LAGS):
        total = jnp.where(quarter == q, result[q * height : (q + 1) * height], total)
    for p in range(tiles):
        for jj in range(2):
            at = (2 * p + jj) * 8
            out_scr[at : at + 8, :] = total[p * 8 : p * 8 + 8, jj * LANES : (jj + 1) * LANES]
    for a in range(8):
        out_ref[:, a * LANES : (a + 1) * LANES] = out_scr[pl.ds(a, 2 * tiles, stride=8), :]


def shifted(value, axis, steps):
    count = lax.axis_size(axis)
    return lax.ppermute(value, axis, [(s, (s - steps) % count) for s in range(count)])


def swapped(value, axis, step):
    return lax.ppermute(value, axis, [(s, s ^ step) for s in range(lax.axis_size(axis))])


def spread(value, axis):
    count = lax.axis_size(axis)
    step = 2
    while step < count:
        value = jnp.maximum(value, swapped(value, axis, step))
        step *= 2
    return value


def call(kernel, name, out_shape, operands, scratch=()):
    return pl.pallas_call(
        kernel,
        out_shape=out_shape,
        in_specs=[VMEM] * len(operands),
        out_specs=jax.tree.map(lambda _: VMEM, out_shape),
        scratch_shapes=[pltpu.VMEM(*s) for s in scratch],
        compiler_params=PARAMS,
        name=name,
    )(*operands)


def body(slc, ref_date, int_offset, frac_offset, partners):
    sds = jax.ShapeDtypeStruct
    _, _, rows, cols = slc.shape
    tiles = cols // LANES
    dates = lax.axis_size("date")
    even = lax.axis_index("date") % 2 == 0
    field, samples = sds((rows, cols), BF16), sds((2 * rows, cols), BF16)
    payload = sds((2 * rows + HROWS, LANES), BF16)
    inputs = (slc.reshape(2 * rows, cols), int_offset[0], frac_offset[0], partners)
    inputs = [pltpu.with_memory_space_constraint(v, pltpu.HBM) for v in inputs]
    own, cond, taps, low, high = pl.pallas_call(
        prep_kernel,
        out_shape=(sds((2 * rows + 16, cols), BF16), sds((16, LANES), F32), sds((HROWS, LANES), BF16), payload, payload),
        in_specs=[pl.BlockSpec(memory_space=pltpu.HBM)] * 4 + [SMEM],
        out_specs=(VMEM,) * 5,
        scratch_shapes=[
            pltpu.VMEM(int_offset.shape[1:], jnp.int32),
            pltpu.VMEM(frac_offset.shape[1:], F32),
            pltpu.SMEM(partners.shape, jnp.int32),
            pltpu.SemaphoreType.DMA((4,)),
        ],
        compiler_params=PARAMS,
        name="prepare",
    )(*inputs, ref_date)
    beside = swapped(own, "date", 1)
    two = shifted(slc.reshape(2 * rows, cols), "date", 2)
    right = shifted(low, "rng", 1)
    left = shifted(high, "rng", -1)
    width = (rows // HROWS + 1) * LANES
    halo = call(
        functools.partial(halo_kernel, cols // BLK), "halo", sds((HROWS, width), BF16), (cond, taps, left, right)
    )
    joined = sds((2 * rows + HROWS, cols), BF16)
    four = shifted(call(join_kernel, "join", joined, (halo, two)), "date", 2)
    later = call(functools.partial(candidate_kernel, (0, 2)), "later", field, (cond, own, two))
    across = lax.ppermute(later, "date", [(s, (s - 2) % dates ^ 1) for s in range(dates)])
    beside_halo = swapped(halo, "date", 1)
    four_halo = shifted(halo, "date", 4)
    first, second, third, fourth = [jnp.asarray(t) for t in surface_tables()]
    spec, energy = call(
        spectrum_kernel,
        "spectrum",
        (sds((2 * rows, cols), F32), sds((tiles, LANES), F32)),
        (own, first, second, third, fourth),
        [((rows, cols), BF16), ((tiles, LANES), F32)],
    )
    resampled = (sds((2 * rows, cols + LANES), BF16), sds((rows, cols), F32))
    scratch = [[((k * rows, cols + LANES), BF16)] for k in range(4)]
    own_ext = call(own_kernel, "own", resampled, (energy, own, halo), scratch[1])
    *beside_ext, coh_beside = call(
        beside_kernel, "beside", (*resampled, field), (energy, *own_ext, beside, beside_halo), scratch[3]
    )
    amp = call(functools.partial(late_candidate_kernel, (0, 1)), "candidate", field, (coh_beside, cond, own, beside))
    before = shifted(amp, "date", -2) if dates == 8 else spread(amp, "date")
    *two_ext, coh_near = call(pair_kernel, "near", (*resampled, field), (*beside_ext, two, four), scratch[3])
    near = swapped(coh_near, "date", 1)
    coh_two = call(again_kernel, "two", field, (*own_ext, *two_ext), scratch[2])
    *four_ext, coh_far = call(pair_kernel, "far", (*resampled, field), (*beside_ext, four, four_halo), scratch[3])
    far = swapped(coh_far, "date", 1)
    coh_four = call(again_kernel, "four", field, (*own_ext, *four_ext), scratch[2])
    surface = call(
        surface_kernel,
        "surface",
        sds((cols // BLK, LAGS * LAGS), F32),
        (cond, own, beside, two, four, across, before, spec, energy, first, second, third, fourth),
        [
            ((rows, cols), BF16),
            ((tiles, LANES), F32),
            ((2 * rows, cols), F32),
            ((8 * cols // BLK, LANES), F32),
        ],
    )
    operands = (cond, surface, coh_beside, coh_two, coh_four, near, far)
    surface, fields = pl.pallas_call(
        place_kernel,
        out_shape=(sds(surface.shape, F32), sds((SPAN, rows, cols), BF16)),
        in_specs=[VMEM] * len(operands),
        out_specs=(pl.BlockSpec(memory_space=pl.ANY),) * 2,
        scratch_shapes=[pltpu.VMEM((SPAN, rows, cols), BF16), pltpu.SemaphoreType.DMA((SPAN + 1,))],
        compiler_params=PARAMS,
        name="place",
    )(*operands)
    return (surface[None, None], fields[None])


def solution(mesh):
    in_specs = (
        P("date", None, None, "rng"),
        P(),
        P("date", None, "rng"),
        P("date", None, "rng"),
        P("date", None),
    )
    out_specs = (P("date", None, "rng", None), P("date", None, None, "rng"))
    return jax.shard_map(body, mesh=mesh, in_specs=in_specs, out_specs=out_specs, check_vma=False)
```

```python
import functools

import jax
import jax.numpy as jnp
import numpy as np
from jax import lax
from jax.experimental import pallas as pl
from jax.experimental.pallas import tpu as pltpu
from jax.sharding import PartitionSpec as P

BLK = 64
OVS = 2
LAGS = 32
SPAN = 4
BOXA = 5
BOXR = 19
TAPS = 8
LANES = 128
PAD = 16
EDGE = 32
HROWS = 16
F32 = jnp.float32
BF16 = jnp.bfloat16
HIGHEST = lax.Precision.HIGHEST
VMEM = pl.BlockSpec(memory_space=pltpu.VMEM)
SMEM = pl.BlockSpec(memory_space=pltpu.SMEM)
PARAMS = pltpu.CompilerParams(vmem_limit_bytes=8 << 20)


def dot(a, b):
    return jnp.dot(a, b, preferred_element_type=F32)


def iota(shape, dim):
    return lax.broadcasted_iota(jnp.int32, shape, dim)


def band(table):
    top = 96
    rows = 2 * LANES - top
    step = iota((rows, LANES), 0) + top - iota((rows, LANES), 1) - (LANES - PAD - 3)
    table = table.astype(BF16)
    step = step.astype(F32).astype(BF16) - table[TAPS : TAPS + 1, :]
    out = jnp.zeros((rows, LANES), BF16)
    for tap in range(TAPS):
        out = jnp.where(step == jnp.asarray(tap, BF16), table[tap : tap + 1, :], out)
    return jnp.concatenate([jnp.zeros((top, LANES), BF16), out], axis=0)


def amplitude(real, imag):
    real, imag = real.astype(F32), imag.astype(F32)
    return jnp.sqrt(real * real + imag * imag + 1e-06).astype(BF16)


EVEN, LEFT, RIGHT, PICK = 4, 5, 6, 8


def prep_kernel(
    own_hbm, off_hbm, frac_hbm, partners_hbm, ref_ref, own_ref, cond_ref, taps_ref, low_ref, high_ref, *scratch
):
    off_ref, frac_ref, partners_ref, sems = scratch
    sources = (own_hbm, off_hbm, frac_hbm, partners_hbm)
    targets = (own_ref.at[0 : own_hbm.shape[0]], off_ref, frac_ref, partners_ref)
    copies = [pltpu.make_async_copy(s, t, sems.at[k]) for k, (s, t) in enumerate(zip(sources, targets))]
    for copy in copies:
        copy.start()
    for copy in copies[1:]:
        copy.wait()
    rows, cols = own_hbm.shape[0] // 2, own_ref.shape[1]
    blocks = cols // BLK
    date, dates = lax.axis_index("date"), lax.axis_size("date")
    place, places = lax.axis_index("rng"), lax.axis_size("rng")
    values = [jnp.where(date + 1 + h < dates, partners_ref[0, h], 0) for h in range(SPAN)]
    values += [1 - date % 2, (place > 0).astype(jnp.int32), (place < places - 1).astype(jnp.int32), jnp.int32(0)]
    beside = date + 1 - 2 * (date % 2)
    held = [date, beside, date + 2, date + 4, beside + 2, beside + 4]
    found = [(lax.rem(h, dates) == ref_ref[0]).astype(jnp.int32) for h in held]
    values += found[0:4] + [(found[4] + found[5]) * int(dates == 8)]
    row = iota(cond_ref.shape, 0)
    cond = jnp.zeros(cond_ref.shape, jnp.int32)
    for k, value in enumerate(values):
        cond = jnp.where(row == k, value, cond)
    cond_ref[...] = cond.astype(F32)
    dist = iota((TAPS, blocks), 0).astype(F32) - 3.0 - frac_ref[...]
    arg = jnp.pi * dist
    sinc = jnp.where(arg == 0.0, 1.0, jnp.sin(arg) / jnp.where(arg == 0.0, 1.0, arg))
    weights = sinc * (0.5 + 0.5 * jnp.cos(arg / 4.0))
    shifts = jnp.broadcast_to(off_ref[...].astype(F32), (TAPS, blocks))
    small = jnp.concatenate([weights, shifts], axis=0).astype(BF16)
    block, lane = iota((blocks, LANES), 0), iota((blocks, LANES), 1)
    taps_ref[...] = dot(small, (lane == block + 1).astype(BF16)).astype(BF16)
    low_ref[2 * rows :, :] = dot(small, (block == 0).astype(BF16)).astype(BF16)
    high_ref[2 * rows :, :] = dot(small, (block == blocks - 1).astype(BF16)).astype(BF16)
    copies[0].wait()
    low_ref[0 : 2 * rows, :] = own_ref[0 : 2 * rows, 0:LANES]
    high_ref[0 : 2 * rows, :] = own_ref[0 : 2 * rows, cols - LANES :]


def candidate_kernel(picks, cond_ref, a_ref, b_ref, amp_ref):
    rows = amp_ref.shape[0]
    a, b = (cond_ref[PICK + k : PICK + k + 1, 0:1] > 0.0 for k in picks)
    value = jnp.where(b, b_ref[0 : 2 * rows, :].astype(F32), a_ref[0 : 2 * rows, :].astype(F32))
    value = amplitude(value[0:rows], value[rows:])
    amp_ref[...] = jnp.where(a | b, value.astype(F32), 0.0).astype(BF16)


def join_kernel(halo_ref, main_ref, both_ref):
    rows, width = main_ref.shape[0], halo_ref.shape[1]
    both_ref[0:rows, :] = main_ref[...]
    both_ref[rows:, 0:width] = halo_ref[...]
    both_ref[rows:, width:] = jnp.zeros((HROWS, both_ref.shape[1] - width), BF16)


def halo_kernel(blocks, cond_ref, taps_ref, left_ref, right_ref, out_ref):
    left = jnp.where(cond_ref[LEFT : LEFT + 1, :] > 0.0, left_ref[...].astype(F32), 0.0)
    right = jnp.where(cond_ref[RIGHT : RIGHT + 1, :] > 0.0, right_ref[...].astype(F32), 0.0)
    rows = (left.shape[0] - HROWS) // 2
    lane = iota((2 * rows, LANES), 1)
    both = jnp.where(lane < EDGE, pltpu.roll(left[0 : 2 * rows], EDGE, 1), pltpu.roll(right[0 : 2 * rows], EDGE, 1))
    both = jnp.where(lane < 2 * EDGE, both, 0.0)
    both = (both[0:rows] + pltpu.roll(both[rows:], 2 * EDGE, 1)).astype(BF16)
    groups = rows // HROWS
    for k in range(groups):
        out_ref[:, k * LANES : (k + 1) * LANES] = both[k * HROWS : (k + 1) * HROWS]
    lane = iota((HROWS, LANES), 1)
    taps = jnp.where(lane == 0, left[2 * rows :], taps_ref[...].astype(F32))
    out_ref[:, groups * LANES : (groups + 1) * LANES] = jnp.where(
        lane == blocks + 1, right[2 * rows :], taps
    ).astype(BF16)


def resample(main_ref, halo_ref, use):
    rows, cols = main_ref.shape[0] // (2 * HROWS) * HROWS, main_ref.shape[1]
    rows -= rows % BLK
    main_ref, halo_ref = main_ref.at[0 : 2 * rows], halo_ref.at[halo_ref.shape[0] - HROWS :]
    tiles = cols // LANES
    groups = rows // HROWS
    edge = jnp.concatenate([halo_ref[:, k * LANES : (k + 1) * LANES] for k in range(groups)], axis=0).astype(F32)
    edge = [pltpu.roll(edge, LANES - EDGE, 1), pltpu.roll(edge, EDGE, 1)]
    edge = jnp.concatenate(edge, axis=0).astype(BF16)
    shape = (LANES, cols + LANES)
    place = ((iota(shape, 1) - PAD) >> 6) + 1 == iota(shape, 0)
    table = dot(halo_ref[:, groups * LANES : (groups + 1) * LANES], place.astype(BF16))
    for p in range(tiles + 1):
        if p == 0:
            window = jnp.concatenate([edge, main_ref[:, 0:LANES]], axis=1)
        elif p == tiles:
            window = jnp.concatenate([main_ref[:, cols - LANES :], edge], axis=1)
        else:
            window = main_ref[:, (p - 1) * LANES : (p + 1) * LANES]
        out = dot(window, band(table[:, p * LANES : (p + 1) * LANES])).astype(BF16)
        use(p, out[0:rows], out[rows:])


def range_box():
    gap = iota((2 * LANES, LANES), 0) - iota((2 * LANES, LANES), 1) - PAD
    return (jnp.abs(gap) <= BOXR // 2).astype(BF16)


def line_box(field):
    rows, lanes = field.shape
    base = jnp.concatenate([field, jnp.zeros((8, lanes), F32)], axis=0)
    two = base + pltpu.roll(base, 1, 0)
    four = two + pltpu.roll(two, rows + 8 - BOXA // 2, 0)
    return (four + pltpu.roll(base, BOXA // 2, 0))[0:rows]


def keep_tile(ext_ref, p, real, imag):
    rows, lanes = real.shape[0], slice(p * LANES, (p + 1) * LANES)
    ext_ref[0:rows, lanes] = real
    ext_ref[rows:, lanes] = imag


def power_tile(fields_ref, p, real, imag):
    real, imag = real.astype(F32), imag.astype(F32)
    fields_ref[:, p * LANES : (p + 1) * LANES] = (real * real + imag * imag).astype(BF16)


def cross_tile(fields_ref, ext_ref, p, real, imag):
    rows, lanes = real.shape[0], slice(p * LANES, (p + 1) * LANES)
    own_r, own_i = ext_ref[0:rows, lanes].astype(F32), ext_ref[rows:, lanes].astype(F32)
    r, i = real.astype(F32), imag.astype(F32)
    fields_ref[0:rows, lanes] = (own_r * r + own_i * i).astype(BF16)
    fields_ref[rows : 2 * rows, lanes] = (own_i * r - own_r * i).astype(BF16)


def coherence(sums, own, partner):
    rows = own.shape[0]
    re, im = line_box(sums[0:rows]), line_box(sums[rows : 2 * rows])
    return ((re * re + im * im) / (own * partner + 1e-06)).astype(BF16)


def late_candidate_kernel(picks, earlier_ref, *refs):
    del earlier_ref
    candidate_kernel(picks, *refs)


def own_kernel(earlier_ref, main_ref, halo_ref, ext_ref, power_ref, fields_ref):
    del earlier_ref
    rows, cols = power_ref.shape

    def use(p, real, imag):
        keep_tile(ext_ref, p, real, imag)
        power_tile(fields_ref, p, real, imag)

    resample(main_ref, halo_ref, use)
    box = range_box()
    for p in range(cols // LANES):
        lanes = slice(p * LANES, (p + 1) * LANES)
        power_ref[:, lanes] = line_box(dot(fields_ref[:, p * LANES : (p + 2) * LANES], box))


def pair_kernel(own_ref, own_power_ref, main_ref, halo_ref, ext_ref, power_ref, out_ref, fields_ref):
    rows, cols = out_ref.shape

    def use(p, real, imag):
        keep_tile(ext_ref, p, real, imag)
        power_tile(fields_ref.at[2 * rows :], p, real, imag)
        cross_tile(fields_ref, own_ref, p, real, imag)

    resample(main_ref, halo_ref, use)
    box = range_box()
    for p in range(cols // LANES):
        lanes = slice(p * LANES, (p + 1) * LANES)
        sums = dot(fields_ref[:, p * LANES : (p + 2) * LANES], box)
        power = line_box(sums[2 * rows :])
        power_ref[:, lanes] = power
        out_ref[:, lanes] = coherence(sums, own_power_ref[:, lanes], power)


def beside_kernel(earlier_ref, *refs):
    del earlier_ref
    pair_kernel(*refs)


def again_kernel(own_ref, own_power_ref, ext_ref, power_ref, out_ref, fields_ref):
    rows, cols = out_ref.shape
    for p in range(cols // LANES + 1):
        lanes = slice(p * LANES, (p + 1) * LANES)
        cross_tile(fields_ref, own_ref, p, ext_ref[0:rows, lanes], ext_ref[rows:, lanes])
    box = range_box()
    for p in range(cols // LANES):
        lanes = slice(p * LANES, (p + 1) * LANES)
        sums = dot(fields_ref[:, p * LANES : (p + 2) * LANES], box)
        out_ref[:, lanes] = coherence(sums, own_power_ref[:, lanes], power_ref[:, lanes])


def place_kernel(
    cond_ref, surface_ref, beside_ref, two_ref, four_ref, near_ref, far_ref, surface_hbm, out_hbm, out_ref, sems
):
    copies = [pltpu.make_async_copy(surface_ref, surface_hbm, sems.at[SPAN])]
    copies += [pltpu.make_async_copy(out_ref.at[h], out_hbm.at[h], sems.at[h]) for h in range(SPAN)]
    copies[0].start()
    even = cond_ref[EVEN : EVEN + 1, 0:1] > 0.0
    near = near_ref[...].astype(F32)
    fields = [
        lambda: jnp.where(even, beside_ref[...].astype(F32), near),
        lambda: two_ref[...].astype(F32),
        lambda: jnp.where(even, near, far_ref[...].astype(F32)),
        lambda: four_ref[...].astype(F32),
    ]
    for h, value in enumerate(fields):
        out_ref[h] = (value() * cond_ref[h : h + 1, 0:1]).astype(BF16)
        copies[1 + h].start()
    for copy in copies:
        copy.wait()


def split(table):
    high = table.astype(BF16)
    return high, (table - high.astype(np.float32)).astype(BF16)


def twice(table):
    zero = np.zeros_like(table)
    return np.block([[table, zero], [zero, table]])


def surface_tables():
    index = np.arange(BLK)
    angle = 2.0 * np.pi / BLK * (index[:, None] * index[None, :] % BLK)
    cosine, sine = np.cos(angle).astype(np.float32), np.sin(angle).astype(np.float32)
    signed = np.where(index < BLK // 2, index, index - BLK)
    upsampled = OVS * BLK
    lag_phase = (np.arange(LAGS) - LAGS // 2)[:, None] * signed[None, :] % upsampled
    lag_angle = 2.0 * np.pi / upsampled * lag_phase
    lag_cos, lag_sin = np.cos(lag_angle).astype(np.float32), np.sin(lag_angle).astype(np.float32)
    high, low = split(np.concatenate([cosine, -sine], axis=0))
    first = np.concatenate([high, low, high], axis=1)
    second = np.concatenate(split(np.concatenate([twice(cosine), twice(sine)], axis=1)), axis=0)
    per = LANES // LAGS
    order = np.arange(LAGS).reshape(LAGS // per, per).T.reshape(-1)
    left = np.block([[lag_cos[order], -lag_sin[order]], [lag_sin[order], lag_cos[order]]])
    third = np.concatenate(split(left), axis=1)
    spread = [twice(np.tile(table.T, (1, per))) for table in (lag_cos, -lag_sin)]
    fourth = np.concatenate(split(np.concatenate(spread, axis=0)), axis=0)
    return first, second, third, fourth


def spectrum(amp_ref, rows_ref, first_ref, second_ref, use):
    size, cols = amp_ref.shape
    tiles = cols // LANES
    group = (iota((LANES, LANES), 0) >> 6 == iota((LANES, LANES), 1) >> 6).astype(F32)
    values = [amp_ref[:, p * LANES : (p + 1) * LANES].astype(F32) for p in range(tiles)]
    for p, value in enumerate(values):
        rows_ref[p : p + 1, :] = jnp.sum(value, axis=0, keepdims=True)
    mean = jnp.dot(rows_ref[...], group, precision=HIGHEST) / (BLK * BLK)
    parts = [[], []]
    for p, value in enumerate(values):
        value = value - mean[p : p + 1, :]
        rows_ref[p : p + 1, :] = jnp.sum(value * value, axis=0, keepdims=True)
        parts[0].append(value.astype(BF16))
        parts[1].append((value - parts[0][p].astype(F32)).astype(BF16))
    high, low = (jnp.concatenate(part, axis=1) for part in parts)
    f = dot(first_ref[...], jnp.concatenate([high, high, low], axis=0)).astype(BF16)
    f = jnp.concatenate([f[:, p * LANES : (p + 1) * LANES] for p in range(tiles)], axis=0)
    s = dot(jnp.concatenate([f, f], axis=1), second_ref[...])
    for p in range(tiles):
        at = 2 * size * p
        top, bottom = s[at : at + size], s[at + size : at + 2 * size]
        use(p, top[:, 0:LANES] + bottom[:, LANES:], bottom[:, 0:LANES] - top[:, LANES:])
    return jnp.dot(rows_ref[...], group, precision=HIGHEST)


def spectrum_kernel(own_ref, first_ref, second_ref, third_ref, fourth_ref, spec_ref, energy_ref, amp_ref, rows_ref):
    del third_ref, fourth_ref
    size = amp_ref.shape[0]
    amp_ref[...] = amplitude(own_ref[0:size, :], own_ref[size : 2 * size, :])

    def use(p, real, imag):
        lanes = slice(p * LANES, (p + 1) * LANES)
        spec_ref[0:size, lanes] = real
        spec_ref[size:, lanes] = imag

    energy_ref[...] = spectrum(amp_ref, rows_ref, first_ref, second_ref, use)


def surface_kernel(cond_ref, *refs):
    samples, across_ref, before_ref, refs = refs[0:4], refs[4], refs[5], refs[6:]
    spec_ref, energy_ref, first_ref, second_ref, third_ref, fourth_ref, out_ref = refs[0:7]
    amp_ref, rows_ref, cross_ref, out_scr = refs[7:]
    size, cols = amp_ref.shape
    tiles = cols // LANES
    picks = [cond_ref[PICK + k : PICK + k + 1, 0:1] > 0.0 for k in range(len(samples) + 1)]
    value = samples[0][0 : 2 * size, :].astype(F32)
    for pick, ref in zip(picks[1:4], samples[1:]):
        value = jnp.where(pick, ref[0 : 2 * size, :].astype(F32), value)
    found = functools.reduce(jnp.logical_or, picks[0:4])
    value = amplitude(value[0:size], value[size:]).astype(F32)
    other = jnp.where(picks[4], across_ref[...].astype(F32), before_ref[...].astype(F32))
    amp_ref[...] = jnp.where(found, value, other).astype(BF16)

    def use(p, ref_r, ref_i):
        lanes = slice(p * LANES, (p + 1) * LANES)
        own_r, own_i = spec_ref[0:size, lanes], spec_ref[size:, lanes]
        cross_ref[0:size, lanes] = own_r * ref_r + own_i * ref_i
        cross_ref[size:, lanes] = own_i * ref_r - own_r * ref_i

    energy = spectrum(amp_ref, rows_ref, first_ref, second_ref, use)
    scale = 1.0 / (BLK * jnp.sqrt(energy_ref[...] * energy + 1e-06))
    lag_rows = [[] for _ in range(LANES // LAGS)]
    cross = [cross_ref[:, p * LANES : (p + 1) * LANES] * scale[p : p + 1, :] for p in range(tiles)]
    cross = jnp.concatenate([value.astype(BF16) for value in cross], axis=1)
    lags = dot(third_ref[...], jnp.concatenate([cross, cross], axis=0))
    for p in range(tiles):
        for q in range(LANES // LAGS):
            at = [ri * LAGS + q * 8 for ri in range(2)]
            part = [lags[k : k + 8, p * LANES : (p + 1) * LANES] for k in at]
            lag_rows[q].append(jnp.concatenate(part, axis=1))
    lhs = jnp.concatenate([row for rows in lag_rows for row in rows], axis=0).astype(BF16)
    result = dot(jnp.concatenate([lhs, lhs], axis=1), fourth_ref[...])
    height = 8 * tiles
    quarter = iota((height, 2 * LANES), 1) % LANES // LAGS
    total = result[0:height]
    for q in range(1, LANES // LAGS):
        total = jnp.where(quarter == q, result[q * height : (q + 1) * height], total)
    for p in range(tiles):
        for jj in range(2):
            at = (2 * p + jj) * 8
            out_scr[at : at + 8, :] = total[p * 8 : p * 8 + 8, jj * LANES : (jj + 1) * LANES]
    for a in range(8):
        out_ref[:, a * LANES : (a + 1) * LANES] = out_scr[pl.ds(a, 2 * tiles, stride=8), :]


def shifted(value, axis, steps):
    count = lax.axis_size(axis)
    return lax.ppermute(value, axis, [(s, (s - steps) % count) for s in range(count)])


def swapped(value, axis, step):
    return lax.ppermute(value, axis, [(s, s ^ step) for s in range(lax.axis_size(axis))])


def spread(value, axis):
    count = lax.axis_size(axis)
    step = 2
    while step < count:
        value = jnp.maximum(value, swapped(value, axis, step))
        step *= 2
    return value


def call(kernel, name, out_shape, operands, scratch=()):
    return pl.pallas_call(
        kernel,
        out_shape=out_shape,
        in_specs=[VMEM] * len(operands),
        out_specs=jax.tree.map(lambda _: VMEM, out_shape),
        scratch_shapes=[pltpu.VMEM(*s) for s in scratch],
        compiler_params=PARAMS,
        name=name,
    )(*operands)


def body(slc, ref_date, int_offset, frac_offset, partners):
    sds = jax.ShapeDtypeStruct
    _, _, rows, cols = slc.shape
    tiles = cols // LANES
    dates = lax.axis_size("date")
    even = lax.axis_index("date") % 2 == 0
    field, samples = sds((rows, cols), BF16), sds((2 * rows, cols), BF16)
    payload = sds((2 * rows + HROWS, LANES), BF16)
    inputs = (slc.reshape(2 * rows, cols), int_offset[0], frac_offset[0], partners)
    inputs = [pltpu.with_memory_space_constraint(v, pltpu.HBM) for v in inputs]
    own, cond, taps, low, high = pl.pallas_call(
        prep_kernel,
        out_shape=(sds((2 * rows + 16, cols), BF16), sds((16, LANES), F32), sds((HROWS, LANES), BF16), payload, payload),
        in_specs=[pl.BlockSpec(memory_space=pltpu.HBM)] * 4 + [SMEM],
        out_specs=(VMEM,) * 5,
        scratch_shapes=[
            pltpu.VMEM(int_offset.shape[1:], jnp.int32),
            pltpu.VMEM(frac_offset.shape[1:], F32),
            pltpu.SMEM(partners.shape, jnp.int32),
            pltpu.SemaphoreType.DMA((4,)),
        ],
        compiler_params=PARAMS,
        name="prepare",
    )(*inputs, ref_date)
    beside = swapped(own, "date", 1)
    two = shifted(slc.reshape(2 * rows, cols), "date", 2)
    right = shifted(low, "rng", 1)
    left = shifted(high, "rng", -1)
    width = (rows // HROWS + 1) * LANES
    halo = call(
        functools.partial(halo_kernel, cols // BLK), "halo", sds((HROWS, width), BF16), (cond, taps, left, right)
    )
    joined = sds((2 * rows + HROWS, cols), BF16)
    four = shifted(call(join_kernel, "join", joined, (halo, two)), "date", 2)
    later = call(functools.partial(candidate_kernel, (0, 2)), "later", field, (cond, own, two))
    across = lax.ppermute(later, "date", [(s, (s - 2) % dates ^ 1) for s in range(dates)])
    beside_halo = swapped(halo, "date", 1)
    four_halo = shifted(halo, "date", 4)
    first, second, third, fourth = [jnp.asarray(t) for t in surface_tables()]
    spec, energy = call(
        spectrum_kernel,
        "spectrum",
        (sds((2 * rows, cols), F32), sds((tiles, LANES), F32)),
        (own, first, second, third, fourth),
        [((rows, cols), BF16), ((tiles, LANES), F32)],
    )
    resampled = (sds((2 * rows, cols + LANES), BF16), sds((rows, cols), F32))
    scratch = [[((k * rows, cols + LANES), BF16)] for k in range(4)]
    own_ext = call(own_kernel, "own", resampled, (energy, own, halo), scratch[1])
    *beside_ext, coh_beside = call(
        beside_kernel, "beside", (*resampled, field), (energy, *own_ext, beside, beside_halo), scratch[3]
    )
    amp = call(functools.partial(late_candidate_kernel, (0, 1)), "candidate", field, (coh_beside, cond, own, beside))
    before = shifted(amp, "date", -2) if dates == 8 else spread(amp, "date")
    *two_ext, coh_near = call(pair_kernel, "near", (*resampled, field), (*beside_ext, two, four), scratch[3])
    near = swapped(coh_near, "date", 1)
    coh_two = call(again_kernel, "two", field, (*own_ext, *two_ext), scratch[2])
    *four_ext, coh_far = call(pair_kernel, "far", (*resampled, field), (*beside_ext, four, four_halo), scratch[3])
    far = swapped(coh_far, "date", 1)
    coh_four = call(again_kernel, "four", field, (*own_ext, *four_ext), scratch[2])
    surface = call(
        surface_kernel,
        "surface",
        sds((cols // BLK, LAGS * LAGS), F32),
        (cond, own, beside, two, four, across, before, spec, energy, first, second, third, fourth),
        [
            ((rows, cols), BF16),
            ((tiles, LANES), F32),
            ((2 * rows, cols), F32),
            ((8 * cols // BLK + 8, LANES), F32),
        ],
    )
    operands = (cond, surface, coh_beside, coh_two, coh_four, near, far)
    surface, fields = pl.pallas_call(
        place_kernel,
        out_shape=(sds(surface.shape, F32), sds((SPAN, rows, cols), BF16)),
        in_specs=[VMEM] * len(operands),
        out_specs=(pl.BlockSpec(memory_space=pl.ANY),) * 2,
        scratch_shapes=[pltpu.VMEM((SPAN, rows, cols), BF16), pltpu.SemaphoreType.DMA((SPAN + 1,))],
        compiler_params=PARAMS,
        name="place",
    )(*operands)
    return (surface[None, None], fields[None])


def solution(mesh):
    in_specs = (
        P("date", None, None, "rng"),
        P(),
        P("date", None, "rng"),
        P("date", None, "rng"),
        P("date", None),
    )
    out_specs = (P("date", None, "rng", None), P("date", None, None, "rng"))
    return jax.shard_map(body, mesh=mesh, in_specs=in_specs, out_specs=out_specs, check_vma=False)
```

```python
import functools

import jax
import jax.numpy as jnp
import numpy as np
from jax import lax
from jax.experimental import pallas as pl
from jax.experimental.pallas import tpu as pltpu
from jax.sharding import PartitionSpec as P

BLK = 64
OVS = 2
LAGS = 32
SPAN = 4
BOXA = 5
BOXR = 19
TAPS = 8
LANES = 128
PAD = 16
EDGE = 32
HROWS = 16
F32 = jnp.float32
BF16 = jnp.bfloat16
HIGHEST = lax.Precision.HIGHEST
VMEM = pl.BlockSpec(memory_space=pltpu.VMEM)
SMEM = pl.BlockSpec(memory_space=pltpu.SMEM)
PARAMS = pltpu.CompilerParams(vmem_limit_bytes=8 << 20)


def dot(a, b):
    return jnp.dot(a, b, preferred_element_type=F32)


def iota(shape, dim):
    return lax.broadcasted_iota(jnp.int32, shape, dim)


def band(table):
    top = 96
    rows = 2 * LANES - top
    step = iota((rows, LANES), 0) + top - iota((rows, LANES), 1) - (LANES - PAD - 3)
    table = table.astype(BF16)
    step = step.astype(F32).astype(BF16) - table[TAPS : TAPS + 1, :]
    out = jnp.zeros((rows, LANES), BF16)
    for tap in range(TAPS):
        out = jnp.where(step == jnp.asarray(tap, BF16), table[tap : tap + 1, :], out)
    return jnp.concatenate([jnp.zeros((top, LANES), BF16), out], axis=0)


def amplitude(real, imag):
    real, imag = real.astype(F32), imag.astype(F32)
    return jnp.sqrt(real * real + imag * imag + 1e-06).astype(BF16)


EVEN, LEFT, RIGHT, PICK = 4, 5, 6, 8


def prep_kernel(
    own_hbm, off_hbm, frac_hbm, partners_hbm, ref_ref, own_ref, cond_ref, taps_ref, low_ref, high_ref, *scratch
):
    off_ref, frac_ref, partners_ref, sems = scratch
    sources = (own_hbm, off_hbm, frac_hbm, partners_hbm)
    targets = (own_ref.at[0 : own_hbm.shape[0]], off_ref, frac_ref, partners_ref)
    copies = [pltpu.make_async_copy(s, t, sems.at[k]) for k, (s, t) in enumerate(zip(sources, targets))]
    for copy in copies:
        copy.start()
    for copy in copies[1:]:
        copy.wait()
    rows, cols = own_hbm.shape[0] // 2, own_ref.shape[1]
    blocks = cols // BLK
    date, dates = lax.axis_index("date"), lax.axis_size("date")
    place, places = lax.axis_index("rng"), lax.axis_size("rng")
    values = [jnp.where(date + 1 + h < dates, partners_ref[0, h], 0) for h in range(SPAN)]
    values += [1 - date % 2, (place > 0).astype(jnp.int32), (place < places - 1).astype(jnp.int32), jnp.int32(0)]
    beside = date + 1 - 2 * (date % 2)
    held = [date, beside, date + 2, date + 4, beside + 2, beside + 4]
    found = [(lax.rem(h, dates) == ref_ref[0]).astype(jnp.int32) for h in held]
    values += found[0:4] + [(found[4] + found[5]) * int(dates == 8)]
    row = iota(cond_ref.shape, 0)
    cond = jnp.zeros(cond_ref.shape, jnp.int32)
    for k, value in enumerate(values):
        cond = jnp.where(row == k, value, cond)
    cond_ref[...] = cond.astype(F32)
    dist = iota((TAPS, blocks), 0).astype(F32) - 3.0 - frac_ref[...]
    arg = jnp.pi * dist
    sinc = jnp.where(arg == 0.0, 1.0, jnp.sin(arg) / jnp.where(arg == 0.0, 1.0, arg))
    weights = sinc * (0.5 + 0.5 * jnp.cos(arg / 4.0))
    shifts = jnp.broadcast_to(off_ref[...].astype(F32), (TAPS, blocks))
    small = jnp.concatenate([weights, shifts], axis=0).astype(BF16)
    block, lane = iota((blocks, LANES), 0), iota((blocks, LANES), 1)
    taps_ref[...] = dot(small, (lane == block + 1).astype(BF16)).astype(BF16)
    low_ref[2 * rows :, :] = dot(small, (block == 0).astype(BF16)).astype(BF16)
    high_ref[2 * rows :, :] = dot(small, (block == blocks - 1).astype(BF16)).astype(BF16)
    copies[0].wait()
    low_ref[0 : 2 * rows, :] = own_ref[0 : 2 * rows, 0:LANES]
    high_ref[0 : 2 * rows, :] = own_ref[0 : 2 * rows, cols - LANES :]


def candidate_kernel(picks, cond_ref, a_ref, b_ref, amp_ref):
    rows = amp_ref.shape[0]
    a, b = (cond_ref[PICK + k : PICK + k + 1, 0:1] > 0.0 for k in picks)
    value = jnp.where(b, b_ref[0 : 2 * rows, :].astype(F32), a_ref[0 : 2 * rows, :].astype(F32))
    value = amplitude(value[0:rows], value[rows:])
    amp_ref[...] = jnp.where(a | b, value.astype(F32), 0.0).astype(BF16)


def join_kernel(halo_ref, main_ref, both_ref):
    rows, width = main_ref.shape[0], halo_ref.shape[1]
    both_ref[0:rows, :] = main_ref[...]
    both_ref[rows:, 0:width] = halo_ref[...]
    both_ref[rows:, width:] = jnp.zeros((HROWS, both_ref.shape[1] - width), BF16)


def halo_kernel(blocks, cond_ref, taps_ref, left_ref, right_ref, out_ref):
    left = jnp.where(cond_ref[LEFT : LEFT + 1, :] > 0.0, left_ref[...].astype(F32), 0.0)
    right = jnp.where(cond_ref[RIGHT : RIGHT + 1, :] > 0.0, right_ref[...].astype(F32), 0.0)
    rows = (left.shape[0] - HROWS) // 2
    lane = iota((2 * rows, LANES), 1)
    both = jnp.where(lane < EDGE, pltpu.roll(left[0 : 2 * rows], EDGE, 1), pltpu.roll(right[0 : 2 * rows], EDGE, 1))
    both = jnp.where(lane < 2 * EDGE, both, 0.0)
    both = (both[0:rows] + pltpu.roll(both[rows:], 2 * EDGE, 1)).astype(BF16)
    groups = rows // HROWS
    for k in range(groups):
        out_ref[:, k * LANES : (k + 1) * LANES] = both[k * HROWS : (k + 1) * HROWS]
    lane = iota((HROWS, LANES), 1)
    taps = jnp.where(lane == 0, left[2 * rows :], taps_ref[...].astype(F32))
    out_ref[:, groups * LANES : (groups + 1) * LANES] = jnp.where(
        lane == blocks + 1, right[2 * rows :], taps
    ).astype(BF16)


def resample(main_ref, halo_ref, use):
    rows, cols = main_ref.shape[0] // (2 * HROWS) * HROWS, main_ref.shape[1]
    rows -= rows % BLK
    main_ref, halo_ref = main_ref.at[0 : 2 * rows], halo_ref.at[halo_ref.shape[0] - HROWS :]
    tiles = cols // LANES
    groups = rows // HROWS
    edge = jnp.concatenate([halo_ref[:, k * LANES : (k + 1) * LANES] for k in range(groups)], axis=0).astype(F32)
    edge = [pltpu.roll(edge, LANES - EDGE, 1), pltpu.roll(edge, EDGE, 1)]
    edge = jnp.concatenate(edge, axis=0).astype(BF16)
    shape = (LANES, cols + LANES)
    place = ((iota(shape, 1) - PAD) >> 6) + 1 == iota(shape, 0)
    table = dot(halo_ref[:, groups * LANES : (groups + 1) * LANES], place.astype(BF16))
    for p in range(tiles + 1):
        if p == 0:
            window = jnp.concatenate([edge, main_ref[:, 0:LANES]], axis=1)
        elif p == tiles:
            window = jnp.concatenate([main_ref[:, cols - LANES :], edge], axis=1)
        else:
            window = main_ref[:, (p - 1) * LANES : (p + 1) * LANES]
        out = dot(window, band(table[:, p * LANES : (p + 1) * LANES])).astype(BF16)
        use(p, out[0:rows], out[rows:])


def range_box():
    gap = iota((2 * LANES, LANES), 0) - iota((2 * LANES, LANES), 1) - PAD
    return (jnp.abs(gap) <= BOXR // 2).astype(BF16)


def line_box(field):
    rows, lanes = field.shape
    base = jnp.concatenate([field, jnp.zeros((8, lanes), F32)], axis=0)
    two = base + pltpu.roll(base, 1, 0)
    four = two + pltpu.roll(two, rows + 8 - BOXA // 2, 0)
    return (four + pltpu.roll(base, BOXA // 2, 0))[0:rows]


def keep_tile(ext_ref, p, real, imag):
    rows, lanes = real.shape[0], slice(p * LANES, (p + 1) * LANES)
    ext_ref[0:rows, lanes] = real
    ext_ref[rows:, lanes] = imag


def power_tile(fields_ref, p, real, imag):
    real, imag = real.astype(F32), imag.astype(F32)
    fields_ref[:, p * LANES : (p + 1) * LANES] = (real * real + imag * imag).astype(BF16)


def cross_tile(fields_ref, ext_ref, p, real, imag):
    rows, lanes = real.shape[0], slice(p * LANES, (p + 1) * LANES)
    own_r, own_i = ext_ref[0:rows, lanes].astype(F32), ext_ref[rows:, lanes].astype(F32)
    r, i = real.astype(F32), imag.astype(F32)
    fields_ref[0:rows, lanes] = (own_r * r + own_i * i).astype(BF16)
    fields_ref[rows : 2 * rows, lanes] = (own_i * r - own_r * i).astype(BF16)


def coherence(sums, own, partner):
    rows = own.shape[0]
    re, im = line_box(sums[0:rows]), line_box(sums[rows : 2 * rows])
    return ((re * re + im * im) / (own * partner + 1e-06)).astype(BF16)


def late_candidate_kernel(picks, earlier_ref, *refs):
    del earlier_ref
    candidate_kernel(picks, *refs)


def own_kernel(earlier_ref, main_ref, halo_ref, ext_ref, power_ref, fields_ref):
    del earlier_ref
    rows, cols = power_ref.shape

    def use(p, real, imag):
        keep_tile(ext_ref, p, real, imag)
        power_tile(fields_ref, p, real, imag)

    resample(main_ref, halo_ref, use)
    box = range_box()
    for p in range(cols // LANES):
        lanes = slice(p * LANES, (p + 1) * LANES)
        power_ref[:, lanes] = line_box(dot(fields_ref[:, p * LANES : (p + 2) * LANES], box))


def pair_kernel(own_ref, own_power_ref, main_ref, halo_ref, ext_ref, power_ref, out_ref, fields_ref):
    rows, cols = out_ref.shape

    def use(p, real, imag):
        keep_tile(ext_ref, p, real, imag)
        power_tile(fields_ref.at[2 * rows :], p, real, imag)
        cross_tile(fields_ref, own_ref, p, real, imag)

    resample(main_ref, halo_ref, use)
    box = range_box()
    for p in range(cols // LANES):
        lanes = slice(p * LANES, (p + 1) * LANES)
        sums = dot(fields_ref[:, p * LANES : (p + 2) * LANES], box)
        power = line_box(sums[2 * rows :])
        power_ref[:, lanes] = power
        out_ref[:, lanes] = coherence(sums, own_power_ref[:, lanes], power)


def beside_kernel(earlier_ref, *refs):
    del earlier_ref
    pair_kernel(*refs)


def again_kernel(h, cond_ref, own_ref, own_power_ref, ext_ref, power_ref, out_ref, fields_ref):
    rows, cols = out_ref.shape
    for p in range(cols // LANES + 1):
        lanes = slice(p * LANES, (p + 1) * LANES)
        cross_tile(fields_ref, own_ref, p, ext_ref[0:rows, lanes], ext_ref[rows:, lanes])
    box = range_box()
    for p in range(cols // LANES):
        lanes = slice(p * LANES, (p + 1) * LANES)
        sums = dot(fields_ref[:, p * LANES : (p + 2) * LANES], box)
        value = coherence(sums, own_power_ref[:, lanes], power_ref[:, lanes]).astype(F32)
        out_ref[:, lanes] = (value * cond_ref[h : h + 1, :]).astype(BF16)


def one_kernel(cond_ref, beside_ref, near_ref, out_ref):
    even = cond_ref[EVEN : EVEN + 1, 0:1] > 0.0
    value = jnp.where(even, beside_ref[...].astype(F32), near_ref[...].astype(F32))
    out_ref[...] = (value * cond_ref[0:1, 0:1]).astype(BF16)


def place_kernel(
    cond_ref, surface_ref, one_ref, two_ref, four_ref, near_ref, far_ref, surface_hbm, out_hbm, three_ref, sems
):
    sources = (one_ref, two_ref, three_ref, four_ref)
    copies = [pltpu.make_async_copy(ref, out_hbm.at[h], sems.at[h]) for h, ref in enumerate(sources)]
    copies.append(pltpu.make_async_copy(surface_ref, surface_hbm, sems.at[SPAN]))
    even = cond_ref[EVEN : EVEN + 1, 0:1] > 0.0
    value = jnp.where(even, near_ref[...].astype(F32), far_ref[...].astype(F32))
    for h in (0, 1, 3, 4):
        copies[h].start()
    three_ref[...] = (value * cond_ref[2:3, 0:1]).astype(BF16)
    copies[2].start()
    for copy in copies:
        copy.wait()


def split(table):
    high = table.astype(BF16)
    return high, (table - high.astype(np.float32)).astype(BF16)


def twice(table):
    zero = np.zeros_like(table)
    return np.block([[table, zero], [zero, table]])


def surface_tables():
    index = np.arange(BLK)
    angle = 2.0 * np.pi / BLK * (index[:, None] * index[None, :] % BLK)
    cosine, sine = np.cos(angle).astype(np.float32), np.sin(angle).astype(np.float32)
    signed = np.where(index < BLK // 2, index, index - BLK)
    upsampled = OVS * BLK
    lag_phase = (np.arange(LAGS) - LAGS // 2)[:, None] * signed[None, :] % upsampled
    lag_angle = 2.0 * np.pi / upsampled * lag_phase
    lag_cos, lag_sin = np.cos(lag_angle).astype(np.float32), np.sin(lag_angle).astype(np.float32)
    high, low = split(np.concatenate([cosine, -sine], axis=0))
    first = np.concatenate([high, low, high], axis=1)
    second = np.concatenate(split(np.concatenate([twice(cosine), twice(sine)], axis=1)), axis=0)
    per = LANES // LAGS
    order = np.arange(LAGS).reshape(LAGS // per, per).T.reshape(-1)
    left = np.block([[lag_cos[order], -lag_sin[order]], [lag_sin[order], lag_cos[order]]])
    third = np.concatenate(split(left), axis=1)
    spread = [twice(np.tile(table.T, (1, per))) for table in (lag_cos, -lag_sin)]
    fourth = np.concatenate(split(np.concatenate(spread, axis=0)), axis=0)
    return first, second, third, fourth


def spectrum(amp_ref, rows_ref, first_ref, second_ref, use):
    size, cols = amp_ref.shape
    tiles = cols // LANES
    group = (iota((LANES, LANES), 0) >> 6 == iota((LANES, LANES), 1) >> 6).astype(F32)
    values = [amp_ref[:, p * LANES : (p + 1) * LANES].astype(F32) for p in range(tiles)]
    for p, value in enumerate(values):
        rows_ref[p : p + 1, :] = jnp.sum(value, axis=0, keepdims=True)
    mean = jnp.dot(rows_ref[...], group, precision=HIGHEST) / (BLK * BLK)
    parts = [[], []]
    for p, value in enumerate(values):
        value = value - mean[p : p + 1, :]
        rows_ref[p : p + 1, :] = jnp.sum(value * value, axis=0, keepdims=True)
        parts[0].append(value.astype(BF16))
        parts[1].append((value - parts[0][p].astype(F32)).astype(BF16))
    high, low = (jnp.concatenate(part, axis=1) for part in parts)
    f = dot(first_ref[...], jnp.concatenate([high, high, low], axis=0)).astype(BF16)
    f = jnp.concatenate([f[:, p * LANES : (p + 1) * LANES] for p in range(tiles)], axis=0)
    s = dot(jnp.concatenate([f, f], axis=1), second_ref[...])
    for p in range(tiles):
        at = 2 * size * p
        top, bottom = s[at : at + size], s[at + size : at + 2 * size]
        use(p, top[:, 0:LANES] + bottom[:, LANES:], bottom[:, 0:LANES] - top[:, LANES:])
    return jnp.dot(rows_ref[...], group, precision=HIGHEST)


def spectrum_kernel(own_ref, first_ref, second_ref, third_ref, fourth_ref, spec_ref, energy_ref, amp_ref, rows_ref):
    del third_ref, fourth_ref
    size = amp_ref.shape[0]
    amp_ref[...] = amplitude(own_ref[0:size, :], own_ref[size : 2 * size, :])

    def use(p, real, imag):
        lanes = slice(p * LANES, (p + 1) * LANES)
        spec_ref[0:size, lanes] = real
        spec_ref[size:, lanes] = imag

    energy_ref[...] = spectrum(amp_ref, rows_ref, first_ref, second_ref, use)


def surface_kernel(cond_ref, *refs):
    samples, across_ref, before_ref, refs = refs[0:4], refs[4], refs[5], refs[6:]
    spec_ref, energy_ref, first_ref, second_ref, third_ref, fourth_ref, out_ref = refs[0:7]
    amp_ref, rows_ref, cross_ref, out_scr = refs[7:]
    size, cols = amp_ref.shape
    tiles = cols // LANES
    picks = [cond_ref[PICK + k : PICK + k + 1, 0:1] > 0.0 for k in range(len(samples) + 1)]
    value = samples[0][0 : 2 * size, :].astype(F32)
    for pick, ref in zip(picks[1:4], samples[1:]):
        value = jnp.where(pick, ref[0 : 2 * size, :].astype(F32), value)
    found = functools.reduce(jnp.logical_or, picks[0:4])
    value = amplitude(value[0:size], value[size:]).astype(F32)
    other = jnp.where(picks[4], across_ref[...].astype(F32), before_ref[...].astype(F32))
    amp_ref[...] = jnp.where(found, value, other).astype(BF16)

    def use(p, ref_r, ref_i):
        lanes = slice(p * LANES, (p + 1) * LANES)
        own_r, own_i = spec_ref[0:size, lanes], spec_ref[size:, lanes]
        cross_ref[0:size, lanes] = own_r * ref_r + own_i * ref_i
        cross_ref[size:, lanes] = own_i * ref_r - own_r * ref_i

    energy = spectrum(amp_ref, rows_ref, first_ref, second_ref, use)
    scale = 1.0 / (BLK * jnp.sqrt(energy_ref[...] * energy + 1e-06))
    lag_rows = [[] for _ in range(LANES // LAGS)]
    cross = [cross_ref[:, p * LANES : (p + 1) * LANES] * scale[p : p + 1, :] for p in range(tiles)]
    cross = jnp.concatenate([value.astype(BF16) for value in cross], axis=1)
    lags = dot(third_ref[...], jnp.concatenate([cross, cross], axis=0))
    for p in range(tiles):
        for q in range(LANES // LAGS):
            at = [ri * LAGS + q * 8 for ri in range(2)]
            part = [lags[k : k + 8, p * LANES : (p + 1) * LANES] for k in at]
            lag_rows[q].append(jnp.concatenate(part, axis=1))
    lhs = jnp.concatenate([row for rows in lag_rows for row in rows], axis=0).astype(BF16)
    result = dot(jnp.concatenate([lhs, lhs], axis=1), fourth_ref[...])
    height = 8 * tiles
    quarter = iota((height, 2 * LANES), 1) % LANES // LAGS
    total = result[0:height]
    for q in range(1, LANES // LAGS):
        total = jnp.where(quarter == q, result[q * height : (q + 1) * height], total)
    for p in range(tiles):
        for jj in range(2):
            at = (2 * p + jj) * 8
            out_scr[at : at + 8, :] = total[p * 8 : p * 8 + 8, jj * LANES : (jj + 1) * LANES]
    for a in range(8):
        out_ref[:, a * LANES : (a + 1) * LANES] = out_scr[pl.ds(a, 2 * tiles, stride=8), :]


def shifted(value, axis, steps):
    count = lax.axis_size(axis)
    return lax.ppermute(value, axis, [(s, (s - steps) % count) for s in range(count)])


def swapped(value, axis, step):
    return lax.ppermute(value, axis, [(s, s ^ step) for s in range(lax.axis_size(axis))])


def spread(value, axis):
    count = lax.axis_size(axis)
    step = 2
    while step < count:
        value = jnp.maximum(value, swapped(value, axis, step))
        step *= 2
    return value


def call(kernel, name, out_shape, operands, scratch=()):
    return pl.pallas_call(
        kernel,
        out_shape=out_shape,
        in_specs=[VMEM] * len(operands),
        out_specs=jax.tree.map(lambda _: VMEM, out_shape),
        scratch_shapes=[pltpu.VMEM(*s) for s in scratch],
        compiler_params=PARAMS,
        name=name,
    )(*operands)


def body(slc, ref_date, int_offset, frac_offset, partners):
    sds = jax.ShapeDtypeStruct
    _, _, rows, cols = slc.shape
    tiles = cols // LANES
    dates = lax.axis_size("date")
    even = lax.axis_index("date") % 2 == 0
    field, samples = sds((rows, cols), BF16), sds((2 * rows, cols), BF16)
    payload = sds((2 * rows + HROWS, LANES), BF16)
    inputs = (slc.reshape(2 * rows, cols), int_offset[0], frac_offset[0], partners)
    inputs = [pltpu.with_memory_space_constraint(v, pltpu.HBM) for v in inputs]
    own, cond, taps, low, high = pl.pallas_call(
        prep_kernel,
        out_shape=(sds((2 * rows + 16, cols), BF16), sds((16, LANES), F32), sds((HROWS, LANES), BF16), payload, payload),
        in_specs=[pl.BlockSpec(memory_space=pltpu.HBM)] * 4 + [SMEM],
        out_specs=(VMEM,) * 5,
        scratch_shapes=[
            pltpu.VMEM(int_offset.shape[1:], jnp.int32),
            pltpu.VMEM(frac_offset.shape[1:], F32),
            pltpu.SMEM(partners.shape, jnp.int32),
            pltpu.SemaphoreType.DMA((4,)),
        ],
        compiler_params=PARAMS,
        name="prepare",
    )(*inputs, ref_date)
    beside = swapped(own, "date", 1)
    two = shifted(slc.reshape(2 * rows, cols), "date", 2)
    right = shifted(low, "rng", 1)
    left = shifted(high, "rng", -1)
    width = (rows // HROWS + 1) * LANES
    halo = call(
        functools.partial(halo_kernel, cols // BLK), "halo", sds((HROWS, width), BF16), (cond, taps, left, right)
    )
    joined = sds((2 * rows + HROWS, cols), BF16)
    four = shifted(call(join_kernel, "join", joined, (halo, two)), "date", 2)
    later = call(functools.partial(candidate_kernel, (0, 2)), "later", field, (cond, own, two))
    across = lax.ppermute(later, "date", [(s, (s - 2) % dates ^ 1) for s in range(dates)])
    amp = call(functools.partial(late_candidate_kernel, (0, 1)), "candidate", field, (later, cond, own, beside))
    before = shifted(amp, "date", -2) if dates == 8 else spread(amp, "date")
    beside_halo = swapped(halo, "date", 1)
    four_halo = shifted(halo, "date", 4)
    first, second, third, fourth = [jnp.asarray(t) for t in surface_tables()]
    spec, energy = call(
        spectrum_kernel,
        "spectrum",
        (sds((2 * rows, cols), F32), sds((tiles, LANES), F32)),
        (own, first, second, third, fourth),
        [((rows, cols), BF16), ((tiles, LANES), F32)],
    )
    resampled = (sds((2 * rows, cols + LANES), BF16), sds((rows, cols), F32))
    scratch = [[((k * rows, cols + LANES), BF16)] for k in range(4)]
    own_ext = call(own_kernel, "own", resampled, (energy, own, halo), scratch[1])
    *beside_ext, coh_beside = call(
        beside_kernel, "beside", (*resampled, field), (amp, *own_ext, beside, beside_halo), scratch[3]
    )
    *two_ext, coh_near = call(pair_kernel, "near", (*resampled, field), (*beside_ext, two, four), scratch[3])
    near = swapped(coh_near, "date", 1)
    coh_two = call(functools.partial(again_kernel, 1), "two", field, (cond, *own_ext, *two_ext), scratch[2])
    *four_ext, coh_far = call(pair_kernel, "far", (*resampled, field), (*beside_ext, four, four_halo), scratch[3])
    far = swapped(coh_far, "date", 1)
    coh_four = call(functools.partial(again_kernel, 3), "four", field, (cond, *own_ext, *four_ext), scratch[2])
    surface = call(
        surface_kernel,
        "surface",
        sds((cols // BLK, LAGS * LAGS), F32),
        (cond, own, beside, two, four, across, before, spec, energy, first, second, third, fourth),
        [
            ((rows, cols), BF16),
            ((tiles, LANES), F32),
            ((2 * rows, cols), F32),
            ((8 * cols // BLK + 8, LANES), F32),
        ],
    )
    coh_one = call(one_kernel, "one", field, (cond, coh_beside, near))
    operands = (cond, surface, coh_one, coh_two, coh_four, near, far)
    surface, fields = pl.pallas_call(
        place_kernel,
        out_shape=(sds(surface.shape, F32), sds((SPAN, rows, cols), BF16)),
        in_specs=[VMEM] * len(operands),
        out_specs=(pl.BlockSpec(memory_space=pl.ANY),) * 2,
        scratch_shapes=[pltpu.VMEM((rows, cols), BF16), pltpu.SemaphoreType.DMA((SPAN + 1,))],
        compiler_params=PARAMS,
        name="place",
    )(*operands)
    return (surface[None, None], fields[None])


def solution(mesh):
    in_specs = (
        P("date", None, None, "rng"),
        P(),
        P("date", None, "rng"),
        P("date", None, "rng"),
        P("date", None),
    )
    out_specs = (P("date", None, "rng", None), P("date", None, None, "rng"))
    return jax.shard_map(body, mesh=mesh, in_specs=in_specs, out_specs=out_specs, check_vma=False)
```

```python
import functools

import jax
import jax.numpy as jnp
import numpy as np
from jax import lax
from jax.experimental import pallas as pl
from jax.experimental.pallas import tpu as pltpu
from jax.sharding import PartitionSpec as P

BLK = 64
OVS = 2
LAGS = 32
SPAN = 4
BOXA = 5
BOXR = 19
TAPS = 8
LANES = 128
PAD = 16
EDGE = 32
HROWS = 16
F32 = jnp.float32
BF16 = jnp.bfloat16
HIGHEST = lax.Precision.HIGHEST
VMEM = pl.BlockSpec(memory_space=pltpu.VMEM)
SMEM = pl.BlockSpec(memory_space=pltpu.SMEM)
PARAMS = pltpu.CompilerParams(vmem_limit_bytes=8 << 20)


def dot(a, b):
    return jnp.dot(a, b, preferred_element_type=F32)


def iota(shape, dim):
    return lax.broadcasted_iota(jnp.int32, shape, dim)


def band(table):
    top = 96
    rows = 2 * LANES - top
    step = iota((rows, LANES), 0) + top - iota((rows, LANES), 1) - (LANES - PAD - 3)
    table = table.astype(BF16)
    step = step.astype(F32).astype(BF16) - table[TAPS : TAPS + 1, :]
    out = jnp.zeros((rows, LANES), BF16)
    for tap in range(TAPS):
        out = jnp.where(step == jnp.asarray(tap, BF16), table[tap : tap + 1, :], out)
    return jnp.concatenate([jnp.zeros((top, LANES), BF16), out], axis=0)


def amplitude(real, imag):
    real, imag = real.astype(F32), imag.astype(F32)
    return jnp.sqrt(real * real + imag * imag + 1e-06).astype(BF16)


EVEN, LEFT, RIGHT, PICK = 4, 5, 6, 8


def prep_kernel(
    own_hbm, off_hbm, frac_hbm, partners_hbm, own_ref, cond_ref, taps_ref, low_ref, high_ref, *scratch
):
    off_ref, frac_ref, partners_ref, sems = scratch
    sources = (own_hbm, off_hbm, frac_hbm, partners_hbm)
    targets = (own_ref.at[0 : own_hbm.shape[0]], off_ref, frac_ref, partners_ref)
    copies = [pltpu.make_async_copy(s, t, sems.at[k]) for k, (s, t) in enumerate(zip(sources, targets))]
    for copy in copies:
        copy.start()
    for copy in copies[1:]:
        copy.wait()
    rows, cols = own_hbm.shape[0] // 2, own_ref.shape[1]
    blocks = cols // BLK
    date, dates = lax.axis_index("date"), lax.axis_size("date")
    place, places = lax.axis_index("rng"), lax.axis_size("rng")
    values = [jnp.where(date + 1 + h < dates, partners_ref[0, h], 0) for h in range(SPAN)]
    values += [1 - date % 2, (place > 0).astype(jnp.int32), (place < places - 1).astype(jnp.int32), jnp.int32(0)]
    row = iota(cond_ref.shape, 0)
    cond = jnp.zeros(cond_ref.shape, jnp.int32)
    for k, value in enumerate(values):
        cond = jnp.where(row == k, value, cond)
    cond_ref[...] = cond.astype(F32)
    dist = iota((TAPS, blocks), 0).astype(F32) - 3.0 - frac_ref[...]
    arg = jnp.pi * dist
    sinc = jnp.where(arg == 0.0, 1.0, jnp.sin(arg) / jnp.where(arg == 0.0, 1.0, arg))
    weights = sinc * (0.5 + 0.5 * jnp.cos(arg / 4.0))
    shifts = jnp.broadcast_to(off_ref[...].astype(F32), (TAPS, blocks))
    small = jnp.concatenate([weights, shifts], axis=0).astype(BF16)
    block, lane = iota((blocks, LANES), 0), iota((blocks, LANES), 1)
    taps_ref[...] = dot(small, (lane == block + 1).astype(BF16)).astype(BF16)
    low_ref[2 * rows :, :] = dot(small, (block == 0).astype(BF16)).astype(BF16)
    high_ref[2 * rows :, :] = dot(small, (block == blocks - 1).astype(BF16)).astype(BF16)
    copies[0].wait()
    low_ref[0 : 2 * rows, :] = own_ref[0 : 2 * rows, 0:LANES]
    high_ref[0 : 2 * rows, :] = own_ref[0 : 2 * rows, cols - LANES :]


def candidate_kernel(picks, cond_ref, a_ref, b_ref, amp_ref):
    rows = amp_ref.shape[0]
    a, b = (cond_ref[PICK + k : PICK + k + 1, 0:1] > 0.0 for k in picks)
    value = jnp.where(b, b_ref[0 : 2 * rows, :].astype(F32), a_ref[0 : 2 * rows, :].astype(F32))
    value = amplitude(value[0:rows], value[rows:])
    amp_ref[...] = jnp.where(a | b, value.astype(F32), 0.0).astype(BF16)


def join_kernel(halo_ref, main_ref, both_ref):
    rows, width = main_ref.shape[0], halo_ref.shape[1]
    both_ref[0:rows, :] = main_ref[...]
    both_ref[rows:, 0:width] = halo_ref[...]
    both_ref[rows:, width:] = jnp.zeros((HROWS, both_ref.shape[1] - width), BF16)


def halo_kernel(blocks, ref_ref, cond_ref, taps_ref, left_ref, right_ref, out_ref, all_ref):
    date, dates = lax.axis_index("date"), lax.axis_size("date")
    beside = date + 1 - 2 * (date % 2)
    held = [date, beside, date + 2, date + 4, beside + 2, beside + 4]
    found = [(lax.rem(h, dates) == ref_ref[0]).astype(jnp.int32) for h in held]
    values = found[0:4] + [(found[4] + found[5]) * int(dates == 8)]
    row = iota(cond_ref.shape, 0)
    cond = cond_ref[...]
    for k, value in enumerate(values):
        cond = jnp.where(row == PICK + k, value.astype(F32), cond)
    all_ref[...] = cond
    left = jnp.where(cond_ref[LEFT : LEFT + 1, :] > 0.0, left_ref[...].astype(F32), 0.0)
    right = jnp.where(cond_ref[RIGHT : RIGHT + 1, :] > 0.0, right_ref[...].astype(F32), 0.0)
    rows = (left.shape[0] - HROWS) // 2
    lane = iota((2 * rows, LANES), 1)
    both = jnp.where(lane < EDGE, pltpu.roll(left[0 : 2 * rows], EDGE, 1), pltpu.roll(right[0 : 2 * rows], EDGE, 1))
    both = jnp.where(lane < 2 * EDGE, both, 0.0)
    both = (both[0:rows] + pltpu.roll(both[rows:], 2 * EDGE, 1)).astype(BF16)
    groups = rows // HROWS
    for k in range(groups):
        out_ref[:, k * LANES : (k + 1) * LANES] = both[k * HROWS : (k + 1) * HROWS]
    lane = iota((HROWS, LANES), 1)
    taps = jnp.where(lane == 0, left[2 * rows :], taps_ref[...].astype(F32))
    out_ref[:, groups * LANES : (groups + 1) * LANES] = jnp.where(
        lane == blocks + 1, right[2 * rows :], taps
    ).astype(BF16)


def resample(main_ref, halo_ref, use):
    rows, cols = main_ref.shape[0] // (2 * HROWS) * HROWS, main_ref.shape[1]
    rows -= rows % BLK
    main_ref, halo_ref = main_ref.at[0 : 2 * rows], halo_ref.at[halo_ref.shape[0] - HROWS :]
    tiles = cols // LANES
    groups = rows // HROWS
    edge = jnp.concatenate([halo_ref[:, k * LANES : (k + 1) * LANES] for k in range(groups)], axis=0).astype(F32)
    edge = [pltpu.roll(edge, LANES - EDGE, 1), pltpu.roll(edge, EDGE, 1)]
    edge = jnp.concatenate(edge, axis=0).astype(BF16)
    shape = (LANES, cols + LANES)
    place = ((iota(shape, 1) - PAD) >> 6) + 1 == iota(shape, 0)
    table = dot(halo_ref[:, groups * LANES : (groups + 1) * LANES], place.astype(BF16))
    for p in range(tiles + 1):
        if p == 0:
            window = jnp.concatenate([edge, main_ref[:, 0:LANES]], axis=1)
        elif p == tiles:
            window = jnp.concatenate([main_ref[:, cols - LANES :], edge], axis=1)
        else:
            window = main_ref[:, (p - 1) * LANES : (p + 1) * LANES]
        out = dot(window, band(table[:, p * LANES : (p + 1) * LANES])).astype(BF16)
        use(p, out[0:rows], out[rows:])


def range_box():
    gap = iota((2 * LANES, LANES), 0) - iota((2 * LANES, LANES), 1) - PAD
    return (jnp.abs(gap) <= BOXR // 2).astype(BF16)


def line_box(field):
    rows, lanes = field.shape
    base = jnp.concatenate([field, jnp.zeros((8, lanes), F32)], axis=0)
    two = base + pltpu.roll(base, 1, 0)
    four = two + pltpu.roll(two, rows + 8 - BOXA // 2, 0)
    return (four + pltpu.roll(base, BOXA // 2, 0))[0:rows]


def keep_tile(ext_ref, p, real, imag):
    rows, lanes = real.shape[0], slice(p * LANES, (p + 1) * LANES)
    ext_ref[0:rows, lanes] = real
    ext_ref[rows:, lanes] = imag


def power_tile(fields_ref, p, real, imag):
    real, imag = real.astype(F32), imag.astype(F32)
    fields_ref[:, p * LANES : (p + 1) * LANES] = (real * real + imag * imag).astype(BF16)


def cross_tile(fields_ref, ext_ref, p, real, imag):
    rows, lanes = real.shape[0], slice(p * LANES, (p + 1) * LANES)
    own_r, own_i = ext_ref[0:rows, lanes].astype(F32), ext_ref[rows:, lanes].astype(F32)
    r, i = real.astype(F32), imag.astype(F32)
    fields_ref[0:rows, lanes] = (own_r * r + own_i * i).astype(BF16)
    fields_ref[rows : 2 * rows, lanes] = (own_i * r - own_r * i).astype(BF16)


def coherence(sums, own, partner):
    rows = own.shape[0]
    re, im = line_box(sums[0:rows]), line_box(sums[rows : 2 * rows])
    return ((re * re + im * im) / (own * partner + 1e-06)).astype(BF16)


def late_candidate_kernel(picks, earlier_ref, *refs):
    del earlier_ref
    candidate_kernel(picks, *refs)


def own_kernel(earlier_ref, main_ref, halo_ref, ext_ref, power_ref, fields_ref):
    del earlier_ref
    rows, cols = power_ref.shape

    def use(p, real, imag):
        keep_tile(ext_ref, p, real, imag)
        power_tile(fields_ref, p, real, imag)

    resample(main_ref, halo_ref, use)
    box = range_box()
    for p in range(cols // LANES):
        lanes = slice(p * LANES, (p + 1) * LANES)
        power_ref[:, lanes] = line_box(dot(fields_ref[:, p * LANES : (p + 2) * LANES], box))


def pair_kernel(own_ref, own_power_ref, main_ref, halo_ref, ext_ref, power_ref, out_ref, fields_ref):
    rows, cols = out_ref.shape

    def use(p, real, imag):
        keep_tile(ext_ref, p, real, imag)
        power_tile(fields_ref.at[2 * rows :], p, real, imag)
        cross_tile(fields_ref, own_ref, p, real, imag)

    resample(main_ref, halo_ref, use)
    box = range_box()
    for p in range(cols // LANES):
        lanes = slice(p * LANES, (p + 1) * LANES)
        sums = dot(fields_ref[:, p * LANES : (p + 2) * LANES], box)
        power = line_box(sums[2 * rows :])
        power_ref[:, lanes] = power
        out_ref[:, lanes] = coherence(sums, own_power_ref[:, lanes], power)


def beside_kernel(earlier_ref, *refs):
    del earlier_ref
    pair_kernel(*refs)


def again_kernel(h, cond_ref, own_ref, own_power_ref, ext_ref, power_ref, out_ref, fields_ref):
    rows, cols = out_ref.shape
    for p in range(cols // LANES + 1):
        lanes = slice(p * LANES, (p + 1) * LANES)
        cross_tile(fields_ref, own_ref, p, ext_ref[0:rows, lanes], ext_ref[rows:, lanes])
    box = range_box()
    for p in range(cols // LANES):
        lanes = slice(p * LANES, (p + 1) * LANES)
        sums = dot(fields_ref[:, p * LANES : (p + 2) * LANES], box)
        value = coherence(sums, own_power_ref[:, lanes], power_ref[:, lanes]).astype(F32)
        out_ref[:, lanes] = (value * cond_ref[h : h + 1, :]).astype(BF16)


def one_kernel(cond_ref, beside_ref, near_ref, out_ref):
    even = cond_ref[EVEN : EVEN + 1, 0:1] > 0.0
    value = jnp.where(even, beside_ref[...].astype(F32), near_ref[...].astype(F32))
    out_ref[...] = (value * cond_ref[0:1, 0:1]).astype(BF16)


def place_kernel(
    cond_ref, surface_ref, one_ref, two_ref, four_ref, near_ref, far_ref, surface_hbm, out_hbm, three_ref, sems
):
    sources = (one_ref, two_ref, three_ref, four_ref)
    copies = [pltpu.make_async_copy(ref, out_hbm.at[h], sems.at[h]) for h, ref in enumerate(sources)]
    copies.append(pltpu.make_async_copy(surface_ref, surface_hbm, sems.at[SPAN]))
    even = cond_ref[EVEN : EVEN + 1, 0:1] > 0.0
    value = jnp.where(even, near_ref[...].astype(F32), far_ref[...].astype(F32))
    for h in (0, 1, 3, 4):
        copies[h].start()
    three_ref[...] = (value * cond_ref[2:3, 0:1]).astype(BF16)
    copies[2].start()
    for copy in copies:
        copy.wait()


def split(table):
    high = table.astype(BF16)
    return high, (table - high.astype(np.float32)).astype(BF16)


def twice(table):
    zero = np.zeros_like(table)
    return np.block([[table, zero], [zero, table]])


def surface_tables():
    index = np.arange(BLK)
    angle = 2.0 * np.pi / BLK * (index[:, None] * index[None, :] % BLK)
    cosine, sine = np.cos(angle).astype(np.float32), np.sin(angle).astype(np.float32)
    signed = np.where(index < BLK // 2, index, index - BLK)
    upsampled = OVS * BLK
    lag_phase = (np.arange(LAGS) - LAGS // 2)[:, None] * signed[None, :] % upsampled
    lag_angle = 2.0 * np.pi / upsampled * lag_phase
    lag_cos, lag_sin = np.cos(lag_angle).astype(np.float32), np.sin(lag_angle).astype(np.float32)
    high, low = split(np.concatenate([cosine, -sine], axis=0))
    first = np.concatenate([high, low, high], axis=1)
    second = np.concatenate(split(np.concatenate([twice(cosine), twice(sine)], axis=1)), axis=0)
    per = LANES // LAGS
    order = np.arange(LAGS).reshape(LAGS // per, per).T.reshape(-1)
    left = np.block([[lag_cos[order], -lag_sin[order]], [lag_sin[order], lag_cos[order]]])
    third = np.concatenate(split(left), axis=1)
    spread = [twice(np.tile(table.T, (1, per))) for table in (lag_cos, -lag_sin)]
    fourth = np.concatenate(split(np.concatenate(spread, axis=0)), axis=0)
    return first, second, third, fourth


def spectrum(amp_ref, rows_ref, first_ref, second_ref, use):
    size, cols = amp_ref.shape
    tiles = cols // LANES
    group = (iota((LANES, LANES), 0) >> 6 == iota((LANES, LANES), 1) >> 6).astype(F32)
    values = [amp_ref[:, p * LANES : (p + 1) * LANES].astype(F32) for p in range(tiles)]
    for p, value in enumerate(values):
        rows_ref[p : p + 1, :] = jnp.sum(value, axis=0, keepdims=True)
    mean = jnp.dot(rows_ref[...], group, precision=HIGHEST) / (BLK * BLK)
    parts = [[], []]
    for p, value in enumerate(values):
        value = value - mean[p : p + 1, :]
        rows_ref[p : p + 1, :] = jnp.sum(value * value, axis=0, keepdims=True)
        parts[0].append(value.astype(BF16))
        parts[1].append((value - parts[0][p].astype(F32)).astype(BF16))
    high, low = (jnp.concatenate(part, axis=1) for part in parts)
    f = dot(first_ref[...], jnp.concatenate([high, high, low], axis=0)).astype(BF16)
    f = jnp.concatenate([f[:, p * LANES : (p + 1) * LANES] for p in range(tiles)], axis=0)
    s = dot(jnp.concatenate([f, f], axis=1), second_ref[...])
    for p in range(tiles):
        at = 2 * size * p
        top, bottom = s[at : at + size], s[at + size : at + 2 * size]
        use(p, top[:, 0:LANES] + bottom[:, LANES:], bottom[:, 0:LANES] - top[:, LANES:])
    return jnp.dot(rows_ref[...], group, precision=HIGHEST)


def spectrum_kernel(own_ref, first_ref, second_ref, third_ref, fourth_ref, spec_ref, energy_ref, amp_ref, rows_ref):
    del third_ref, fourth_ref
    size = amp_ref.shape[0]
    amp_ref[...] = amplitude(own_ref[0:size, :], own_ref[size : 2 * size, :])

    def use(p, real, imag):
        lanes = slice(p * LANES, (p + 1) * LANES)
        spec_ref[0:size, lanes] = real
        spec_ref[size:, lanes] = imag

    energy_ref[...] = spectrum(amp_ref, rows_ref, first_ref, second_ref, use)


def surface_kernel(cond_ref, *refs):
    samples, across_ref, before_ref, refs = refs[0:4], refs[4], refs[5], refs[6:]
    spec_ref, energy_ref, first_ref, second_ref, third_ref, fourth_ref, out_ref = refs[0:7]
    amp_ref, rows_ref, cross_ref, out_scr = refs[7:]
    size, cols = amp_ref.shape
    tiles = cols // LANES
    picks = [cond_ref[PICK + k : PICK + k + 1, 0:1] > 0.0 for k in range(len(samples) + 1)]
    value = samples[0][0 : 2 * size, :].astype(F32)
    for pick, ref in zip(picks[1:4], samples[1:]):
        value = jnp.where(pick, ref[0 : 2 * size, :].astype(F32), value)
    found = functools.reduce(jnp.logical_or, picks[0:4])
    value = amplitude(value[0:size], value[size:]).astype(F32)
    other = jnp.where(picks[4], across_ref[...].astype(F32), before_ref[...].astype(F32))
    amp_ref[...] = jnp.where(found, value, other).astype(BF16)

    def use(p, ref_r, ref_i):
        lanes = slice(p * LANES, (p + 1) * LANES)
        own_r, own_i = spec_ref[0:size, lanes], spec_ref[size:, lanes]
        cross_ref[0:size, lanes] = own_r * ref_r + own_i * ref_i
        cross_ref[size:, lanes] = own_i * ref_r - own_r * ref_i

    energy = spectrum(amp_ref, rows_ref, first_ref, second_ref, use)
    scale = 1.0 / (BLK * jnp.sqrt(energy_ref[...] * energy + 1e-06))
    lag_rows = [[] for _ in range(LANES // LAGS)]
    cross = [cross_ref[:, p * LANES : (p + 1) * LANES] * scale[p : p + 1, :] for p in range(tiles)]
    cross = jnp.concatenate([value.astype(BF16) for value in cross], axis=1)
    lags = dot(third_ref[...], jnp.concatenate([cross, cross], axis=0))
    for p in range(tiles):
        for q in range(LANES // LAGS):
            at = [ri * LAGS + q * 8 for ri in range(2)]
            part = [lags[k : k + 8, p * LANES : (p + 1) * LANES] for k in at]
            lag_rows[q].append(jnp.concatenate(part, axis=1))
    lhs = jnp.concatenate([row for rows in lag_rows for row in rows], axis=0).astype(BF16)
    result = dot(jnp.concatenate([lhs, lhs], axis=1), fourth_ref[...])
    height = 8 * tiles
    quarter = iota((height, 2 * LANES), 1) % LANES // LAGS
    total = result[0:height]
    for q in range(1, LANES // LAGS):
        total = jnp.where(quarter == q, result[q * height : (q + 1) * height], total)
    for p in range(tiles):
        for jj in range(2):
            at = (2 * p + jj) * 8
            out_scr[at : at + 8, :] = total[p * 8 : p * 8 + 8, jj * LANES : (jj + 1) * LANES]
    for a in range(8):
        out_ref[:, a * LANES : (a + 1) * LANES] = out_scr[pl.ds(a, 2 * tiles, stride=8), :]


def shifted(value, axis, steps):
    count = lax.axis_size(axis)
    return lax.ppermute(value, axis, [(s, (s - steps) % count) for s in range(count)])


def swapped(value, axis, step):
    return lax.ppermute(value, axis, [(s, s ^ step) for s in range(lax.axis_size(axis))])


def spread(value, axis):
    count = lax.axis_size(axis)
    step = 2
    while step < count:
        value = jnp.maximum(value, swapped(value, axis, step))
        step *= 2
    return value


def call(kernel, name, out_shape, operands, scratch=(), smem=0):
    return pl.pallas_call(
        kernel,
        out_shape=out_shape,
        in_specs=[SMEM] * smem + [VMEM] * (len(operands) - smem),
        out_specs=jax.tree.map(lambda _: VMEM, out_shape),
        scratch_shapes=[pltpu.VMEM(*s) for s in scratch],
        compiler_params=PARAMS,
        name=name,
    )(*operands)


def body(slc, ref_date, int_offset, frac_offset, partners):
    sds = jax.ShapeDtypeStruct
    _, _, rows, cols = slc.shape
    tiles = cols // LANES
    dates = lax.axis_size("date")
    even = lax.axis_index("date") % 2 == 0
    field, samples = sds((rows, cols), BF16), sds((2 * rows, cols), BF16)
    payload = sds((2 * rows + HROWS, LANES), BF16)
    inputs = (slc.reshape(2 * rows, cols), int_offset[0], frac_offset[0], partners)
    inputs = [pltpu.with_memory_space_constraint(v, pltpu.HBM) for v in inputs]
    own, cond, taps, low, high = pl.pallas_call(
        prep_kernel,
        out_shape=(sds((2 * rows + 16, cols), BF16), sds((16, LANES), F32), sds((HROWS, LANES), BF16), payload, payload),
        in_specs=[pl.BlockSpec(memory_space=pltpu.HBM)] * 4,
        out_specs=(VMEM,) * 5,
        scratch_shapes=[
            pltpu.VMEM(int_offset.shape[1:], jnp.int32),
            pltpu.VMEM(frac_offset.shape[1:], F32),
            pltpu.SMEM(partners.shape, jnp.int32),
            pltpu.SemaphoreType.DMA((4,)),
        ],
        compiler_params=PARAMS,
        name="prepare",
    )(*inputs)
    beside = swapped(own, "date", 1)
    two = shifted(slc.reshape(2 * rows, cols), "date", 2)
    right = shifted(low, "rng", 1)
    left = shifted(high, "rng", -1)
    width = (rows // HROWS + 1) * LANES
    halo, cond = call(
        functools.partial(halo_kernel, cols // BLK),
        "halo",
        (sds((HROWS, width), BF16), sds(cond.shape, F32)),
        (ref_date, cond, taps, left, right),
        smem=1,
    )
    joined = sds((2 * rows + HROWS, cols), BF16)
    four = shifted(call(join_kernel, "join", joined, (halo, two)), "date", 2)
    later = call(functools.partial(candidate_kernel, (0, 2)), "later", field, (cond, own, two))
    across = lax.ppermute(later, "date", [(s, (s - 2) % dates ^ 1) for s in range(dates)])
    beside_halo = swapped(halo, "date", 1)
    four_halo = shifted(halo, "date", 4)
    first, second, third, fourth = [jnp.asarray(t) for t in surface_tables()]
    spec, energy = call(
        spectrum_kernel,
        "spectrum",
        (sds((2 * rows, cols), F32), sds((tiles, LANES), F32)),
        (own, first, second, third, fourth),
        [((rows, cols), BF16), ((tiles, LANES), F32)],
    )
    resampled = (sds((2 * rows, cols + LANES), BF16), sds((rows, cols), F32))
    scratch = [[((k * rows, cols + LANES), BF16)] for k in range(4)]
    own_ext = call(own_kernel, "own", resampled, (energy, own, halo), scratch[1])
    *beside_ext, coh_beside = call(
        beside_kernel, "beside", (*resampled, field), (energy, *own_ext, beside, beside_halo), scratch[3]
    )
    amp = call(functools.partial(late_candidate_kernel, (0, 1)), "candidate", field, (coh_beside, cond, own, beside))
    before = shifted(amp, "date", -2) if dates == 8 else spread(amp, "date")
    *two_ext, coh_near = call(pair_kernel, "near", (*resampled, field), (*beside_ext, two, four), scratch[3])
    near = swapped(coh_near, "date", 1)
    coh_two = call(functools.partial(again_kernel, 1), "two", field, (cond, *own_ext, *two_ext), scratch[2])
    *four_ext, coh_far = call(pair_kernel, "far", (*resampled, field), (*beside_ext, four, four_halo), scratch[3])
    far = swapped(coh_far, "date", 1)
    coh_four = call(functools.partial(again_kernel, 3), "four", field, (cond, *own_ext, *four_ext), scratch[2])
    surface = call(
        surface_kernel,
        "surface",
        sds((cols // BLK, LAGS * LAGS), F32),
        (cond, own, beside, two, four, across, before, spec, energy, first, second, third, fourth),
        [
            ((rows, cols), BF16),
            ((tiles, LANES), F32),
            ((2 * rows, cols), F32),
            ((8 * cols // BLK + 8, LANES), F32),
        ],
    )
    coh_one = call(one_kernel, "one", field, (cond, coh_beside, near))
    operands = (cond, surface, coh_one, coh_two, coh_four, near, far)
    surface, fields = pl.pallas_call(
        place_kernel,
        out_shape=(sds(surface.shape, F32), sds((SPAN, rows, cols), BF16)),
        in_specs=[VMEM] * len(operands),
        out_specs=(pl.BlockSpec(memory_space=pl.ANY),) * 2,
        scratch_shapes=[pltpu.VMEM((rows, cols), BF16), pltpu.SemaphoreType.DMA((SPAN + 1,))],
        compiler_params=PARAMS,
        name="place",
    )(*operands)
    return (surface[None, None], fields[None])


def solution(mesh):
    in_specs = (
        P("date", None, None, "rng"),
        P(),
        P("date", None, "rng"),
        P("date", None, "rng"),
        P("date", None),
    )
    out_specs = (P("date", None, "rng", None), P("date", None, None, "rng"))
    return jax.shard_map(body, mesh=mesh, in_specs=in_specs, out_specs=out_specs, check_vma=False)
```

```python
import functools

import jax
import jax.numpy as jnp
import numpy as np
from jax import lax
from jax.experimental import pallas as pl
from jax.experimental.pallas import tpu as pltpu
from jax.sharding import PartitionSpec as P

BLK = 64
OVS = 2
LAGS = 32
SPAN = 4
BOXA = 5
BOXR = 19
TAPS = 8
LANES = 128
PAD = 16
EDGE = 32
HROWS = 16
F32 = jnp.float32
BF16 = jnp.bfloat16
HIGHEST = lax.Precision.HIGHEST
VMEM = pl.BlockSpec(memory_space=pltpu.VMEM)
SMEM = pl.BlockSpec(memory_space=pltpu.SMEM)
PARAMS = pltpu.CompilerParams(vmem_limit_bytes=8 << 20)


def dot(a, b):
    return jnp.dot(a, b, preferred_element_type=F32)


def iota(shape, dim):
    return lax.broadcasted_iota(jnp.int32, shape, dim)


def band(table):
    top = 96
    rows = 2 * LANES - top
    step = iota((rows, LANES), 0) + top - iota((rows, LANES), 1) - (LANES - PAD - 3)
    table = table.astype(BF16)
    step = step.astype(F32).astype(BF16) - table[TAPS : TAPS + 1, :]
    out = jnp.zeros((rows, LANES), BF16)
    for tap in range(TAPS):
        out = jnp.where(step == jnp.asarray(tap, BF16), table[tap : tap + 1, :], out)
    return jnp.concatenate([jnp.zeros((top, LANES), BF16), out], axis=0)


def amplitude(real, imag):
    real, imag = real.astype(F32), imag.astype(F32)
    return jnp.sqrt(real * real + imag * imag + 1e-06).astype(BF16)


EVEN, LEFT, RIGHT, PICK = 4, 5, 6, 8


def prep_kernel(
    own_hbm, off_hbm, frac_hbm, partners_hbm, ref_ref, own_ref, cond_ref, taps_ref, low_ref, high_ref, *scratch
):
    off_ref, frac_ref, partners_ref, sems = scratch
    sources = (own_hbm, off_hbm, frac_hbm, partners_hbm)
    targets = (own_ref.at[0 : own_hbm.shape[0]], off_ref, frac_ref, partners_ref)
    copies = [pltpu.make_async_copy(s, t, sems.at[k]) for k, (s, t) in enumerate(zip(sources, targets))]
    for copy in copies:
        copy.start()
    for copy in copies[1:]:
        copy.wait()
    rows, cols = own_hbm.shape[0] // 2, own_ref.shape[1]
    blocks = cols // BLK
    date, dates = lax.axis_index("date"), lax.axis_size("date")
    place, places = lax.axis_index("rng"), lax.axis_size("rng")
    values = [jnp.where(date + 1 + h < dates, partners_ref[0, h], 0) for h in range(SPAN)]
    values += [1 - date % 2, (place > 0).astype(jnp.int32), (place < places - 1).astype(jnp.int32), jnp.int32(0)]
    beside = date + 1 - 2 * (date % 2)
    held = [date, beside, date + 2, date + 4, beside + 2, beside + 4]
    found = [(lax.rem(h, dates) == ref_ref[0]).astype(jnp.int32) for h in held]
    values += found[0:4] + [(found[4] + found[5]) * int(dates == 8)]
    row = iota(cond_ref.shape, 0)
    cond = jnp.zeros(cond_ref.shape, jnp.int32)
    for k, value in enumerate(values):
        cond = jnp.where(row == k, value, cond)
    cond_ref[...] = cond.astype(F32)
    dist = iota((TAPS, blocks), 0).astype(F32) - 3.0 - frac_ref[...]
    arg = jnp.pi * dist
    sinc = jnp.where(arg == 0.0, 1.0, jnp.sin(arg) / jnp.where(arg == 0.0, 1.0, arg))
    weights = sinc * (0.5 + 0.5 * jnp.cos(arg / 4.0))
    shifts = jnp.broadcast_to(off_ref[...].astype(F32), (TAPS, blocks))
    small = jnp.concatenate([weights, shifts], axis=0).astype(BF16)
    block, lane = iota((blocks, LANES), 0), iota((blocks, LANES), 1)
    taps_ref[...] = dot(small, (lane == block + 1).astype(BF16)).astype(BF16)
    low_ref[2 * rows :, :] = dot(small, (block == 0).astype(BF16)).astype(BF16)
    high_ref[2 * rows :, :] = dot(small, (block == blocks - 1).astype(BF16)).astype(BF16)
    copies[0].wait()
    low_ref[0 : 2 * rows, :] = own_ref[0 : 2 * rows, 0:LANES]
    high_ref[0 : 2 * rows, :] = own_ref[0 : 2 * rows, cols - LANES :]


def candidate_kernel(picks, cond_ref, a_ref, b_ref, amp_ref):
    rows = amp_ref.shape[0]
    a, b = (cond_ref[PICK + k : PICK + k + 1, 0:1] > 0.0 for k in picks)
    value = jnp.where(b, b_ref[0 : 2 * rows, :].astype(F32), a_ref[0 : 2 * rows, :].astype(F32))
    value = amplitude(value[0:rows], value[rows:])
    amp_ref[...] = jnp.where(a | b, value.astype(F32), 0.0).astype(BF16)


def join_kernel(halo_ref, main_ref, both_ref):
    rows, width = main_ref.shape[0], halo_ref.shape[1]
    both_ref[0:rows, :] = main_ref[...]
    both_ref[rows:, 0:width] = halo_ref[...]
    both_ref[rows:, width:] = jnp.zeros((HROWS, both_ref.shape[1] - width), BF16)


def halo_kernel(blocks, cond_ref, taps_ref, left_ref, right_ref, out_ref):
    left = jnp.where(cond_ref[LEFT : LEFT + 1, :] > 0.0, left_ref[...].astype(F32), 0.0)
    right = jnp.where(cond_ref[RIGHT : RIGHT + 1, :] > 0.0, right_ref[...].astype(F32), 0.0)
    rows = (left.shape[0] - HROWS) // 2
    lane = iota((2 * rows, LANES), 1)
    both = jnp.where(lane < EDGE, pltpu.roll(left[0 : 2 * rows], EDGE, 1), pltpu.roll(right[0 : 2 * rows], EDGE, 1))
    both = jnp.where(lane < 2 * EDGE, both, 0.0)
    both = (both[0:rows] + pltpu.roll(both[rows:], 2 * EDGE, 1)).astype(BF16)
    groups = rows // HROWS
    for k in range(groups):
        out_ref[:, k * LANES : (k + 1) * LANES] = both[k * HROWS : (k + 1) * HROWS]
    lane = iota((HROWS, LANES), 1)
    taps = jnp.where(lane == 0, left[2 * rows :], taps_ref[...].astype(F32))
    out_ref[:, groups * LANES : (groups + 1) * LANES] = jnp.where(
        lane == blocks + 1, right[2 * rows :], taps
    ).astype(BF16)


def resample(main_ref, halo_ref, use):
    rows, cols = main_ref.shape[0] // (2 * HROWS) * HROWS, main_ref.shape[1]
    rows -= rows % BLK
    main_ref, halo_ref = main_ref.at[0 : 2 * rows], halo_ref.at[halo_ref.shape[0] - HROWS :]
    tiles = cols // LANES
    groups = rows // HROWS
    edge = jnp.concatenate([halo_ref[:, k * LANES : (k + 1) * LANES] for k in range(groups)], axis=0).astype(F32)
    edge = [pltpu.roll(edge, LANES - EDGE, 1), pltpu.roll(edge, EDGE, 1)]
    edge = jnp.concatenate(edge, axis=0).astype(BF16)
    shape = (LANES, cols + LANES)
    place = ((iota(shape, 1) - PAD) >> 6) + 1 == iota(shape, 0)
    table = dot(halo_ref[:, groups * LANES : (groups + 1) * LANES], place.astype(BF16))
    for p in range(tiles + 1):
        if p == 0:
            window = jnp.concatenate([edge, main_ref[:, 0:LANES]], axis=1)
        elif p == tiles:
            window = jnp.concatenate([main_ref[:, cols - LANES :], edge], axis=1)
        else:
            window = main_ref[:, (p - 1) * LANES : (p + 1) * LANES]
        out = dot(window, band(table[:, p * LANES : (p + 1) * LANES])).astype(BF16)
        use(p, out[0:rows], out[rows:])


def range_box():
    gap = iota((2 * LANES, LANES), 0) - iota((2 * LANES, LANES), 1) - PAD
    return (jnp.abs(gap) <= BOXR // 2).astype(BF16)


def line_box(field):
    rows, lanes = field.shape
    base = jnp.concatenate([field, jnp.zeros((8, lanes), F32)], axis=0)
    two = base + pltpu.roll(base, 1, 0)
    four = two + pltpu.roll(two, rows + 8 - BOXA // 2, 0)
    return (four + pltpu.roll(base, BOXA // 2, 0))[0:rows]


def keep_tile(ext_ref, p, real, imag):
    rows, lanes = real.shape[0], slice(p * LANES, (p + 1) * LANES)
    ext_ref[0:rows, lanes] = real
    ext_ref[rows:, lanes] = imag


def power_tile(fields_ref, p, real, imag):
    real, imag = real.astype(F32), imag.astype(F32)
    fields_ref[:, p * LANES : (p + 1) * LANES] = (real * real + imag * imag).astype(BF16)


def cross_tile(fields_ref, ext_ref, p, real, imag):
    rows, lanes = real.shape[0], slice(p * LANES, (p + 1) * LANES)
    own_r, own_i = ext_ref[0:rows, lanes].astype(F32), ext_ref[rows:, lanes].astype(F32)
    r, i = real.astype(F32), imag.astype(F32)
    fields_ref[0:rows, lanes] = (own_r * r + own_i * i).astype(BF16)
    fields_ref[rows : 2 * rows, lanes] = (own_i * r - own_r * i).astype(BF16)


def coherence(sums, own, partner):
    rows = own.shape[0]
    re, im = line_box(sums[0:rows]), line_box(sums[rows : 2 * rows])
    return ((re * re + im * im) / (own * partner + 1e-06)).astype(BF16)


def late_candidate_kernel(picks, earlier_ref, *refs):
    del earlier_ref
    candidate_kernel(picks, *refs)


def own_kernel(earlier_ref, main_ref, halo_ref, ext_ref, power_ref, fields_ref):
    del earlier_ref
    rows, cols = power_ref.shape

    def use(p, real, imag):
        keep_tile(ext_ref, p, real, imag)
        power_tile(fields_ref, p, real, imag)

    resample(main_ref, halo_ref, use)
    box = range_box()
    for p in range(cols // LANES):
        lanes = slice(p * LANES, (p + 1) * LANES)
        power_ref[:, lanes] = line_box(dot(fields_ref[:, p * LANES : (p + 2) * LANES], box))


def pair_kernel(own_ref, own_power_ref, main_ref, halo_ref, ext_ref, power_ref, out_ref, fields_ref):
    rows, cols = out_ref.shape

    def use(p, real, imag):
        keep_tile(ext_ref, p, real, imag)
        power_tile(fields_ref.at[2 * rows :], p, real, imag)
        cross_tile(fields_ref, own_ref, p, real, imag)

    resample(main_ref, halo_ref, use)
    box = range_box()
    for p in range(cols // LANES):
        lanes = slice(p * LANES, (p + 1) * LANES)
        sums = dot(fields_ref[:, p * LANES : (p + 2) * LANES], box)
        power = line_box(sums[2 * rows :])
        power_ref[:, lanes] = power
        out_ref[:, lanes] = coherence(sums, own_power_ref[:, lanes], power)


def beside_kernel(earlier_ref, *refs):
    del earlier_ref
    pair_kernel(*refs)


def again_kernel(own_ref, own_power_ref, ext_ref, power_ref, out_ref, fields_ref):
    rows, cols = out_ref.shape
    for p in range(cols // LANES + 1):
        lanes = slice(p * LANES, (p + 1) * LANES)
        cross_tile(fields_ref, own_ref, p, ext_ref[0:rows, lanes], ext_ref[rows:, lanes])
    box = range_box()
    for p in range(cols // LANES):
        lanes = slice(p * LANES, (p + 1) * LANES)
        sums = dot(fields_ref[:, p * LANES : (p + 2) * LANES], box)
        out_ref[:, lanes] = coherence(sums, own_power_ref[:, lanes], power_ref[:, lanes])


def place_kernel(
    cond_ref, surface_ref, beside_ref, two_ref, four_ref, near_ref, far_ref, surface_hbm, out_hbm, out_ref, sems
):
    copies = [pltpu.make_async_copy(surface_ref, surface_hbm, sems.at[SPAN])]
    copies += [pltpu.make_async_copy(out_ref.at[h], out_hbm.at[h], sems.at[h]) for h in range(SPAN)]
    copies[0].start()
    even = cond_ref[EVEN : EVEN + 1, 0:1] > 0.0
    near = near_ref[...].astype(F32)
    fields = [
        lambda: jnp.where(even, beside_ref[...].astype(F32), near),
        lambda: two_ref[...].astype(F32),
        lambda: jnp.where(even, near, far_ref[...].astype(F32)),
        lambda: four_ref[...].astype(F32),
    ]
    for h, value in enumerate(fields):
        out_ref[h] = (value() * cond_ref[h : h + 1, 0:1]).astype(BF16)
        copies[1 + h].start()
    for copy in copies:
        copy.wait()


def split(table):
    high = table.astype(BF16)
    return high, (table - high.astype(np.float32)).astype(BF16)


def twice(table):
    zero = np.zeros_like(table)
    return np.block([[table, zero], [zero, table]])


def surface_tables():
    index = np.arange(BLK)
    angle = 2.0 * np.pi / BLK * (index[:, None] * index[None, :] % BLK)
    cosine, sine = np.cos(angle).astype(np.float32), np.sin(angle).astype(np.float32)
    signed = np.where(index < BLK // 2, index, index - BLK)
    upsampled = OVS * BLK
    lag_phase = (np.arange(LAGS) - LAGS // 2)[:, None] * signed[None, :] % upsampled
    lag_angle = 2.0 * np.pi / upsampled * lag_phase
    lag_cos, lag_sin = np.cos(lag_angle).astype(np.float32), np.sin(lag_angle).astype(np.float32)
    high, low = split(np.concatenate([cosine, -sine], axis=0))
    first = np.concatenate([high, low, high], axis=1)
    second = np.concatenate(split(np.concatenate([twice(cosine), twice(sine)], axis=1)), axis=0)
    per = LANES // LAGS
    order = np.arange(LAGS).reshape(LAGS // per, per).T.reshape(-1)
    left = np.block([[lag_cos[order], -lag_sin[order]], [lag_sin[order], lag_cos[order]]])
    third = np.concatenate(split(left), axis=1)
    spread = [twice(np.tile(table.T, (1, per))) for table in (lag_cos, -lag_sin)]
    fourth = np.concatenate(split(np.concatenate(spread, axis=0)), axis=0)
    return first, second, third, fourth


def spectrum(amp_ref, rows_ref, first_ref, second_ref, use):
    size, cols = amp_ref.shape
    tiles = cols // LANES
    group = (iota((LANES, LANES), 0) >> 6 == iota((LANES, LANES), 1) >> 6).astype(F32)
    values = [amp_ref[:, p * LANES : (p + 1) * LANES].astype(F32) for p in range(tiles)]
    for p, value in enumerate(values):
        rows_ref[p : p + 1, :] = jnp.sum(value, axis=0, keepdims=True)
    mean = jnp.dot(rows_ref[...], group, precision=HIGHEST) / (BLK * BLK)
    parts = [[], []]
    for p, value in enumerate(values):
        value = value - mean[p : p + 1, :]
        rows_ref[p : p + 1, :] = jnp.sum(value * value, axis=0, keepdims=True)
        parts[0].append(value.astype(BF16))
        parts[1].append((value - parts[0][p].astype(F32)).astype(BF16))
    high, low = (jnp.concatenate(part, axis=1) for part in parts)
    f = dot(first_ref[...], jnp.concatenate([high, high, low], axis=0)).astype(BF16)
    f = jnp.concatenate([f[:, p * LANES : (p + 1) * LANES] for p in range(tiles)], axis=0)
    s = dot(jnp.concatenate([f, f], axis=1), second_ref[...])
    for p in range(tiles):
        at = 2 * size * p
        top, bottom = s[at : at + size], s[at + size : at + 2 * size]
        use(p, top[:, 0:LANES] + bottom[:, LANES:], bottom[:, 0:LANES] - top[:, LANES:])
    return jnp.dot(rows_ref[...], group, precision=HIGHEST)


def spectrum_kernel(own_ref, first_ref, second_ref, third_ref, fourth_ref, spec_ref, energy_ref, amp_ref, rows_ref):
    del third_ref, fourth_ref
    size = amp_ref.shape[0]
    amp_ref[...] = amplitude(own_ref[0:size, :], own_ref[size : 2 * size, :])

    def use(p, real, imag):
        lanes = slice(p * LANES, (p + 1) * LANES)
        spec_ref[0:size, lanes] = real
        spec_ref[size:, lanes] = imag

    energy_ref[...] = spectrum(amp_ref, rows_ref, first_ref, second_ref, use)


def surface_kernel(cond_ref, *refs):
    samples, across_ref, before_ref, refs = refs[0:4], refs[4], refs[5], refs[6:]
    spec_ref, energy_ref, first_ref, second_ref, third_ref, fourth_ref, out_ref = refs[0:7]
    amp_ref, rows_ref, cross_ref, out_scr = refs[7:]
    size, cols = amp_ref.shape
    tiles = cols // LANES
    picks = [cond_ref[PICK + k : PICK + k + 1, 0:1] > 0.0 for k in range(len(samples) + 1)]
    value = samples[0][0 : 2 * size, :].astype(F32)
    for pick, ref in zip(picks[1:4], samples[1:]):
        value = jnp.where(pick, ref[0 : 2 * size, :].astype(F32), value)
    found = functools.reduce(jnp.logical_or, picks[0:4])
    value = amplitude(value[0:size], value[size:]).astype(F32)
    other = jnp.where(picks[4], across_ref[...].astype(F32), before_ref[...].astype(F32))
    amp_ref[...] = jnp.where(found, value, other).astype(BF16)

    def use(p, ref_r, ref_i):
        lanes = slice(p * LANES, (p + 1) * LANES)
        own_r, own_i = spec_ref[0:size, lanes], spec_ref[size:, lanes]
        cross_ref[0:size, lanes] = own_r * ref_r + own_i * ref_i
        cross_ref[size:, lanes] = own_i * ref_r - own_r * ref_i

    energy = spectrum(amp_ref, rows_ref, first_ref, second_ref, use)
    scale = 1.0 / (BLK * jnp.sqrt(energy_ref[...] * energy + 1e-06))
    lag_rows = [[] for _ in range(LANES // LAGS)]
    cross = [cross_ref[:, p * LANES : (p + 1) * LANES] * scale[p : p + 1, :] for p in range(tiles)]
    cross = jnp.concatenate([value.astype(BF16) for value in cross], axis=1)
    lags = dot(third_ref[...], jnp.concatenate([cross, cross], axis=0))
    for p in range(tiles):
        for q in range(LANES // LAGS):
            at = [ri * LAGS + q * 8 for ri in range(2)]
            part = [lags[k : k + 8, p * LANES : (p + 1) * LANES] for k in at]
            lag_rows[q].append(jnp.concatenate(part, axis=1))
    lhs = jnp.concatenate([row for rows in lag_rows for row in rows], axis=0).astype(BF16)
    result = dot(jnp.concatenate([lhs, lhs], axis=1), fourth_ref[...])
    height = 8 * tiles
    quarter = iota((height, 2 * LANES), 1) % LANES // LAGS
    total = result[0:height]
    for q in range(1, LANES // LAGS):
        total = jnp.where(quarter == q, result[q * height : (q + 1) * height], total)
    for p in range(tiles):
        for jj in range(2):
            at = (2 * p + jj) * 8
            out_scr[at : at + 8, :] = total[p * 8 : p * 8 + 8, jj * LANES : (jj + 1) * LANES]
    for a in range(8):
        out_ref[:, a * LANES : (a + 1) * LANES] = out_scr[pl.ds(a, 2 * tiles, stride=8), :]


def shifted(value, axis, steps):
    count = lax.axis_size(axis)
    return lax.ppermute(value, axis, [(s, (s - steps) % count) for s in range(count)])


def swapped(value, axis, step):
    return lax.ppermute(value, axis, [(s, s ^ step) for s in range(lax.axis_size(axis))])


def spread(value, axis):
    count = lax.axis_size(axis)
    step = 2
    while step < count:
        value = jnp.maximum(value, swapped(value, axis, step))
        step *= 2
    return value


def call(kernel, name, out_shape, operands, scratch=()):
    return pl.pallas_call(
        kernel,
        out_shape=out_shape,
        in_specs=[VMEM] * len(operands),
        out_specs=jax.tree.map(lambda _: VMEM, out_shape),
        scratch_shapes=[pltpu.VMEM(*s) for s in scratch],
        compiler_params=PARAMS,
        name=name,
    )(*operands)


def body(slc, ref_date, int_offset, frac_offset, partners):
    sds = jax.ShapeDtypeStruct
    _, _, rows, cols = slc.shape
    tiles = cols // LANES
    dates = lax.axis_size("date")
    even = lax.axis_index("date") % 2 == 0
    field, samples = sds((rows, cols), BF16), sds((2 * rows, cols), BF16)
    payload = sds((2 * rows + HROWS, LANES), BF16)
    inputs = (slc.reshape(2 * rows, cols), int_offset[0], frac_offset[0], partners)
    inputs = [pltpu.with_memory_space_constraint(v, pltpu.HBM) for v in inputs]
    own, cond, taps, low, high = pl.pallas_call(
        prep_kernel,
        out_shape=(sds((2 * rows + 16, cols), BF16), sds((16, LANES), F32), sds((HROWS, LANES), BF16), payload, payload),
        in_specs=[pl.BlockSpec(memory_space=pltpu.HBM)] * 4 + [SMEM],
        out_specs=(VMEM,) * 5,
        scratch_shapes=[
            pltpu.VMEM(int_offset.shape[1:], jnp.int32),
            pltpu.VMEM(frac_offset.shape[1:], F32),
            pltpu.SMEM(partners.shape, jnp.int32),
            pltpu.SemaphoreType.DMA((4,)),
        ],
        compiler_params=PARAMS,
        name="prepare",
    )(*inputs, ref_date)
    beside = swapped(own, "date", 1)
    two = shifted(slc.reshape(2 * rows, cols), "date", 2)
    right = shifted(low, "rng", 1)
    left = shifted(high, "rng", -1)
    width = (rows // HROWS + 1) * LANES
    halo = call(
        functools.partial(halo_kernel, cols // BLK), "halo", sds((HROWS, width), BF16), (cond, taps, left, right)
    )
    joined = sds((2 * rows + HROWS, cols), BF16)
    four = shifted(call(join_kernel, "join", joined, (halo, two)), "date", 2)
    later = call(functools.partial(candidate_kernel, (0, 2)), "later", field, (cond, own, two))
    across = lax.ppermute(later, "date", [(s, (s - 2) % dates ^ 1) for s in range(dates)])
    beside_halo = swapped(halo, "date", 1)
    four_halo = shifted(halo, "date", 4)
    first, second, third, fourth = [jnp.asarray(t) for t in surface_tables()]
    spec, energy = call(
        spectrum_kernel,
        "spectrum",
        (sds((2 * rows, cols), F32), sds((tiles, LANES), F32)),
        (own, first, second, third, fourth),
        [((rows, cols), BF16), ((tiles, LANES), F32)],
    )
    resampled = (sds((2 * rows, cols + LANES), BF16), sds((rows, cols), F32))
    scratch = [[((k * rows, cols + LANES), BF16)] for k in range(4)]
    own_ext = call(own_kernel, "own", resampled, (energy, own, halo), scratch[1])
    *beside_ext, coh_beside = call(
        beside_kernel, "beside", (*resampled, field), (later, *own_ext, beside, beside_halo), scratch[3]
    )
    amp = call(functools.partial(candidate_kernel, (0, 1)), "candidate", field, (cond, own, beside))
    before = shifted(amp, "date", -2) if dates == 8 else spread(amp, "date")
    *two_ext, coh_near = call(pair_kernel, "near", (*resampled, field), (*beside_ext, two, four), scratch[3])
    near = swapped(coh_near, "date", 1)
    coh_two = call(again_kernel, "two", field, (*own_ext, *two_ext), scratch[2])
    *four_ext, coh_far = call(pair_kernel, "far", (*resampled, field), (*beside_ext, four, four_halo), scratch[3])
    far = swapped(coh_far, "date", 1)
    coh_four = call(again_kernel, "four", field, (*own_ext, *four_ext), scratch[2])
    surface = call(
        surface_kernel,
        "surface",
        sds((cols // BLK, LAGS * LAGS), F32),
        (cond, own, beside, two, four, across, before, spec, energy, first, second, third, fourth),
        [
            ((rows, cols), BF16),
            ((tiles, LANES), F32),
            ((2 * rows, cols), F32),
            ((8 * cols // BLK + 8, LANES), F32),
        ],
    )
    operands = (cond, surface, coh_beside, coh_two, coh_four, near, far)
    surface, fields = pl.pallas_call(
        place_kernel,
        out_shape=(sds(surface.shape, F32), sds((SPAN, rows, cols), BF16)),
        in_specs=[VMEM] * len(operands),
        out_specs=(pl.BlockSpec(memory_space=pl.ANY),) * 2,
        scratch_shapes=[pltpu.VMEM((SPAN, rows, cols), BF16), pltpu.SemaphoreType.DMA((SPAN + 1,))],
        compiler_params=PARAMS,
        name="place",
    )(*operands)
    return (surface[None, None], fields[None])


def solution(mesh):
    in_specs = (
        P("date", None, None, "rng"),
        P(),
        P("date", None, "rng"),
        P("date", None, "rng"),
        P("date", None),
    )
    out_specs = (P("date", None, "rng", None), P("date", None, None, "rng"))
    return jax.shard_map(body, mesh=mesh, in_specs=in_specs, out_specs=out_specs, check_vma=False)
```

```python
import functools

import jax
import jax.numpy as jnp
import numpy as np
from jax import lax
from jax.experimental import pallas as pl
from jax.experimental.pallas import tpu as pltpu
from jax.sharding import PartitionSpec as P

BLK = 64
OVS = 2
LAGS = 32
SPAN = 4
BOXA = 5
BOXR = 19
TAPS = 8
LANES = 128
PAD = 16
EDGE = 32
HROWS = 16
F32 = jnp.float32
BF16 = jnp.bfloat16
HIGHEST = lax.Precision.HIGHEST
VMEM = pl.BlockSpec(memory_space=pltpu.VMEM)
SMEM = pl.BlockSpec(memory_space=pltpu.SMEM)
PARAMS = pltpu.CompilerParams(vmem_limit_bytes=8 << 20)


def dot(a, b):
    return jnp.dot(a, b, preferred_element_type=F32)


def iota(shape, dim):
    return lax.broadcasted_iota(jnp.int32, shape, dim)


def band(table):
    top = 96
    rows = 2 * LANES - top
    step = iota((rows, LANES), 0) + top - iota((rows, LANES), 1) - (LANES - PAD - 3)
    table = table.astype(BF16)
    step = step.astype(F32).astype(BF16) - table[TAPS : TAPS + 1, :]
    out = jnp.zeros((rows, LANES), BF16)
    for tap in range(TAPS):
        out = jnp.where(step == jnp.asarray(tap, BF16), table[tap : tap + 1, :], out)
    return jnp.concatenate([jnp.zeros((top, LANES), BF16), out], axis=0)


def amplitude(real, imag):
    real, imag = real.astype(F32), imag.astype(F32)
    return jnp.sqrt(real * real + imag * imag + 1e-06).astype(BF16)


EVEN, LEFT, RIGHT, PICK = 4, 5, 6, 8


def prep_kernel(
    own_hbm, off_hbm, frac_hbm, partners_hbm, ref_ref, own_ref, cond_ref, taps_ref, low_ref, high_ref, *scratch
):
    off_ref, frac_ref, partners_ref, sems = scratch
    sources = (own_hbm, off_hbm, frac_hbm, partners_hbm)
    targets = (own_ref.at[0 : own_hbm.shape[0]], off_ref, frac_ref, partners_ref)
    copies = [pltpu.make_async_copy(s, t, sems.at[k]) for k, (s, t) in enumerate(zip(sources, targets))]
    for copy in copies:
        copy.start()
    for copy in copies[1:]:
        copy.wait()
    rows, cols = own_hbm.shape[0] // 2, own_ref.shape[1]
    blocks = cols // BLK
    date, dates = lax.axis_index("date"), lax.axis_size("date")
    place, places = lax.axis_index("rng"), lax.axis_size("rng")
    values = [jnp.where(date + 1 + h < dates, partners_ref[0, h], 0) for h in range(SPAN)]
    values += [1 - date % 2, (place > 0).astype(jnp.int32), (place < places - 1).astype(jnp.int32), jnp.int32(0)]
    beside = date + 1 - 2 * (date % 2)
    held = [date, beside, date + 2, date + 4, beside + 2, beside + 4]
    found = [(lax.rem(h, dates) == ref_ref[0]).astype(jnp.int32) for h in held]
    values += found[0:4] + [(found[4] + found[5]) * int(dates == 8)]
    row = iota(cond_ref.shape, 0)
    cond = jnp.zeros(cond_ref.shape, jnp.int32)
    for k, value in enumerate(values):
        cond = jnp.where(row == k, value, cond)
    cond_ref[...] = cond.astype(F32)
    dist = iota((TAPS, blocks), 0).astype(F32) - 3.0 - frac_ref[...]
    arg = jnp.pi * dist
    sinc = jnp.where(arg == 0.0, 1.0, jnp.sin(arg) / jnp.where(arg == 0.0, 1.0, arg))
    weights = sinc * (0.5 + 0.5 * jnp.cos(arg / 4.0))
    shifts = jnp.broadcast_to(off_ref[...].astype(F32), (TAPS, blocks))
    small = jnp.concatenate([weights, shifts], axis=0).astype(BF16)
    block, lane = iota((blocks, LANES), 0), iota((blocks, LANES), 1)
    taps_ref[...] = dot(small, (lane == block + 1).astype(BF16)).astype(BF16)
    low_ref[2 * rows :, :] = dot(small, (block == 0).astype(BF16)).astype(BF16)
    high_ref[2 * rows :, :] = dot(small, (block == blocks - 1).astype(BF16)).astype(BF16)
    copies[0].wait()
    low_ref[0 : 2 * rows, :] = own_ref[0 : 2 * rows, 0:LANES]
    high_ref[0 : 2 * rows, :] = own_ref[0 : 2 * rows, cols - LANES :]


def candidate_kernel(picks, cond_ref, a_ref, b_ref, amp_ref):
    rows = amp_ref.shape[0]
    a, b = (cond_ref[PICK + k : PICK + k + 1, 0:1] > 0.0 for k in picks)
    value = jnp.where(b, b_ref[0 : 2 * rows, :].astype(F32), a_ref[0 : 2 * rows, :].astype(F32))
    value = amplitude(value[0:rows], value[rows:])
    amp_ref[...] = jnp.where(a | b, value.astype(F32), 0.0).astype(BF16)


def join_kernel(halo_ref, main_ref, both_ref):
    rows, width = main_ref.shape[0], halo_ref.shape[1]
    both_ref[0:rows, :] = main_ref[...]
    both_ref[rows:, 0:width] = halo_ref[...]
    both_ref[rows:, width:] = jnp.zeros((HROWS, both_ref.shape[1] - width), BF16)


def halo_kernel(blocks, cond_ref, taps_ref, left_ref, right_ref, out_ref):
    left = jnp.where(cond_ref[LEFT : LEFT + 1, :] > 0.0, left_ref[...].astype(F32), 0.0)
    right = jnp.where(cond_ref[RIGHT : RIGHT + 1, :] > 0.0, right_ref[...].astype(F32), 0.0)
    rows = (left.shape[0] - HROWS) // 2
    lane = iota((2 * rows, LANES), 1)
    both = jnp.where(lane < EDGE, pltpu.roll(left[0 : 2 * rows], EDGE, 1), pltpu.roll(right[0 : 2 * rows], EDGE, 1))
    both = jnp.where(lane < 2 * EDGE, both, 0.0)
    both = (both[0:rows] + pltpu.roll(both[rows:], 2 * EDGE, 1)).astype(BF16)
    groups = rows // HROWS
    for k in range(groups):
        out_ref[:, k * LANES : (k + 1) * LANES] = both[k * HROWS : (k + 1) * HROWS]
    lane = iota((HROWS, LANES), 1)
    taps = jnp.where(lane == 0, left[2 * rows :], taps_ref[...].astype(F32))
    out_ref[:, groups * LANES : (groups + 1) * LANES] = jnp.where(
        lane == blocks + 1, right[2 * rows :], taps
    ).astype(BF16)


def resample(main_ref, halo_ref, use):
    rows, cols = main_ref.shape[0] // (2 * HROWS) * HROWS, main_ref.shape[1]
    rows -= rows % BLK
    main_ref, halo_ref = main_ref.at[0 : 2 * rows], halo_ref.at[halo_ref.shape[0] - HROWS :]
    tiles = cols // LANES
    groups = rows // HROWS
    edge = jnp.concatenate([halo_ref[:, k * LANES : (k + 1) * LANES] for k in range(groups)], axis=0).astype(F32)
    edge = [pltpu.roll(edge, LANES - EDGE, 1), pltpu.roll(edge, EDGE, 1)]
    edge = jnp.concatenate(edge, axis=0).astype(BF16)
    shape = (LANES, cols + LANES)
    place = ((iota(shape, 1) - PAD) >> 6) + 1 == iota(shape, 0)
    table = dot(halo_ref[:, groups * LANES : (groups + 1) * LANES], place.astype(BF16))
    for p in range(tiles + 1):
        if p == 0:
            window = jnp.concatenate([edge, main_ref[:, 0:LANES]], axis=1)
        elif p == tiles:
            window = jnp.concatenate([main_ref[:, cols - LANES :], edge], axis=1)
        else:
            window = main_ref[:, (p - 1) * LANES : (p + 1) * LANES]
        out = dot(window, band(table[:, p * LANES : (p + 1) * LANES])).astype(BF16)
        use(p, out[0:rows], out[rows:])


def range_box():
    gap = iota((2 * LANES, LANES), 0) - iota((2 * LANES, LANES), 1) - PAD
    return (jnp.abs(gap) <= BOXR // 2).astype(BF16)


def line_box(field):
    rows, lanes = field.shape
    base = jnp.concatenate([field, jnp.zeros((8, lanes), F32)], axis=0)
    two = base + pltpu.roll(base, 1, 0)
    four = two + pltpu.roll(two, rows + 8 - BOXA // 2, 0)
    return (four + pltpu.roll(base, BOXA // 2, 0))[0:rows]


def keep_tile(ext_ref, p, real, imag):
    rows, lanes = real.shape[0], slice(p * LANES, (p + 1) * LANES)
    ext_ref[0:rows, lanes] = real
    ext_ref[rows:, lanes] = imag


def power_tile(fields_ref, p, real, imag):
    real, imag = real.astype(F32), imag.astype(F32)
    fields_ref[:, p * LANES : (p + 1) * LANES] = (real * real + imag * imag).astype(BF16)


def cross_tile(fields_ref, ext_ref, p, real, imag):
    rows, lanes = real.shape[0], slice(p * LANES, (p + 1) * LANES)
    own_r, own_i = ext_ref[0:rows, lanes].astype(F32), ext_ref[rows:, lanes].astype(F32)
    r, i = real.astype(F32), imag.astype(F32)
    fields_ref[0:rows, lanes] = (own_r * r + own_i * i).astype(BF16)
    fields_ref[rows : 2 * rows, lanes] = (own_i * r - own_r * i).astype(BF16)


def coherence(sums, own, partner):
    rows = own.shape[0]
    re, im = line_box(sums[0:rows]), line_box(sums[rows : 2 * rows])
    return ((re * re + im * im) / (own * partner + 1e-06)).astype(BF16)


def late_candidate_kernel(picks, earlier_ref, *refs):
    del earlier_ref
    candidate_kernel(picks, *refs)


def own_kernel(earlier_ref, main_ref, halo_ref, ext_ref, power_ref, fields_ref):
    del earlier_ref
    rows, cols = power_ref.shape

    def use(p, real, imag):
        keep_tile(ext_ref, p, real, imag)
        power_tile(fields_ref, p, real, imag)

    resample(main_ref, halo_ref, use)
    box = range_box()
    for p in range(cols // LANES):
        lanes = slice(p * LANES, (p + 1) * LANES)
        power_ref[:, lanes] = line_box(dot(fields_ref[:, p * LANES : (p + 2) * LANES], box))


def pair_kernel(own_ref, own_power_ref, main_ref, halo_ref, ext_ref, power_ref, out_ref, fields_ref):
    rows, cols = out_ref.shape

    def use(p, real, imag):
        keep_tile(ext_ref, p, real, imag)
        power_tile(fields_ref.at[2 * rows :], p, real, imag)
        cross_tile(fields_ref, own_ref, p, real, imag)

    resample(main_ref, halo_ref, use)
    box = range_box()
    for p in range(cols // LANES):
        lanes = slice(p * LANES, (p + 1) * LANES)
        sums = dot(fields_ref[:, p * LANES : (p + 2) * LANES], box)
        power = line_box(sums[2 * rows :])
        power_ref[:, lanes] = power
        out_ref[:, lanes] = coherence(sums, own_power_ref[:, lanes], power)


def beside_kernel(earlier_ref, *refs):
    del earlier_ref
    pair_kernel(*refs)


def again_kernel(h, cond_ref, own_ref, own_power_ref, ext_ref, power_ref, out_ref, fields_ref):
    rows, cols = out_ref.shape
    for p in range(cols // LANES + 1):
        lanes = slice(p * LANES, (p + 1) * LANES)
        cross_tile(fields_ref, own_ref, p, ext_ref[0:rows, lanes], ext_ref[rows:, lanes])
    box = range_box()
    for p in range(cols // LANES):
        lanes = slice(p * LANES, (p + 1) * LANES)
        sums = dot(fields_ref[:, p * LANES : (p + 2) * LANES], box)
        value = coherence(sums, own_power_ref[:, lanes], power_ref[:, lanes]).astype(F32)
        out_ref[:, lanes] = (value * cond_ref[h : h + 1, :]).astype(BF16)


def one_kernel(cond_ref, beside_ref, near_ref, out_ref):
    even = cond_ref[EVEN : EVEN + 1, 0:1] > 0.0
    value = jnp.where(even, beside_ref[...].astype(F32), near_ref[...].astype(F32))
    out_ref[...] = (value * cond_ref[0:1, 0:1]).astype(BF16)


def place_kernel(
    cond_ref, surface_ref, one_ref, two_ref, four_ref, near_ref, far_ref, surface_hbm, out_hbm, three_ref, sems
):
    sources = (one_ref, two_ref, three_ref, four_ref)
    copies = [pltpu.make_async_copy(ref, out_hbm.at[h], sems.at[h]) for h, ref in enumerate(sources)]
    copies.append(pltpu.make_async_copy(surface_ref, surface_hbm, sems.at[SPAN]))
    even = cond_ref[EVEN : EVEN + 1, 0:1] > 0.0
    value = jnp.where(even, near_ref[...].astype(F32), far_ref[...].astype(F32))
    for h in (0, 1, 3, 4):
        copies[h].start()
    three_ref[...] = (value * cond_ref[2:3, 0:1]).astype(BF16)
    copies[2].start()
    for copy in copies:
        copy.wait()


def split(table):
    high = table.astype(BF16)
    return high, (table - high.astype(np.float32)).astype(BF16)


def twice(table):
    zero = np.zeros_like(table)
    return np.block([[table, zero], [zero, table]])


def surface_tables():
    index = np.arange(BLK)
    angle = 2.0 * np.pi / BLK * (index[:, None] * index[None, :] % BLK)
    cosine, sine = np.cos(angle).astype(np.float32), np.sin(angle).astype(np.float32)
    signed = np.where(index < BLK // 2, index, index - BLK)
    upsampled = OVS * BLK
    lag_phase = (np.arange(LAGS) - LAGS // 2)[:, None] * signed[None, :] % upsampled
    lag_angle = 2.0 * np.pi / upsampled * lag_phase
    lag_cos, lag_sin = np.cos(lag_angle).astype(np.float32), np.sin(lag_angle).astype(np.float32)
    high, low = split(np.concatenate([cosine, -sine], axis=0))
    first = np.concatenate([high, low, high], axis=1)
    second = np.concatenate(split(np.concatenate([twice(cosine), twice(sine)], axis=1)), axis=0)
    per = LANES // LAGS
    order = np.arange(LAGS).reshape(LAGS // per, per).T.reshape(-1)
    left = np.block([[lag_cos[order], -lag_sin[order]], [lag_sin[order], lag_cos[order]]])
    third = np.concatenate(split(left), axis=1)
    spread = [twice(np.tile(table.T, (1, per))) for table in (lag_cos, -lag_sin)]
    fourth = np.concatenate(split(np.concatenate(spread, axis=0)), axis=0)
    return first, second, third, fourth


def spectrum(amp_ref, rows_ref, first_ref, second_ref, use):
    size, cols = amp_ref.shape
    tiles = cols // LANES
    group = (iota((LANES, LANES), 0) >> 6 == iota((LANES, LANES), 1) >> 6).astype(F32)
    values = [amp_ref[:, p * LANES : (p + 1) * LANES].astype(F32) for p in range(tiles)]
    for p, value in enumerate(values):
        rows_ref[p : p + 1, :] = jnp.sum(value, axis=0, keepdims=True)
    mean = jnp.dot(rows_ref[...], group, precision=HIGHEST) / (BLK * BLK)
    parts = [[], []]
    for p, value in enumerate(values):
        value = value - mean[p : p + 1, :]
        rows_ref[p : p + 1, :] = jnp.sum(value * value, axis=0, keepdims=True)
        parts[0].append(value.astype(BF16))
        parts[1].append((value - parts[0][p].astype(F32)).astype(BF16))
    high, low = (jnp.concatenate(part, axis=1) for part in parts)
    f = dot(first_ref[...], jnp.concatenate([high, high, low], axis=0)).astype(BF16)
    f = jnp.concatenate([f[:, p * LANES : (p + 1) * LANES] for p in range(tiles)], axis=0)
    s = dot(jnp.concatenate([f, f], axis=1), second_ref[...])
    for p in range(tiles):
        at = 2 * size * p
        top, bottom = s[at : at + size], s[at + size : at + 2 * size]
        use(p, top[:, 0:LANES] + bottom[:, LANES:], bottom[:, 0:LANES] - top[:, LANES:])
    return jnp.dot(rows_ref[...], group, precision=HIGHEST)


def spectrum_kernel(own_ref, first_ref, second_ref, third_ref, fourth_ref, spec_ref, energy_ref, amp_ref, rows_ref):
    del third_ref, fourth_ref
    size = amp_ref.shape[0]
    amp_ref[...] = amplitude(own_ref[0:size, :], own_ref[size : 2 * size, :])

    def use(p, real, imag):
        lanes = slice(p * LANES, (p + 1) * LANES)
        spec_ref[0:size, lanes] = real
        spec_ref[size:, lanes] = imag

    energy_ref[...] = spectrum(amp_ref, rows_ref, first_ref, second_ref, use)


def surface_kernel(cond_ref, *refs):
    samples, across_ref, before_ref, refs = refs[0:4], refs[4], refs[5], refs[6:]
    spec_ref, energy_ref, first_ref, second_ref, third_ref, fourth_ref, out_ref = refs[0:7]
    amp_ref, rows_ref, cross_ref, out_scr = refs[7:]
    size, cols = amp_ref.shape
    tiles = cols // LANES
    picks = [cond_ref[PICK + k : PICK + k + 1, 0:1] > 0.0 for k in range(len(samples) + 1)]
    value = samples[0][0 : 2 * size, :].astype(F32)
    for pick, ref in zip(picks[1:4], samples[1:]):
        value = jnp.where(pick, ref[0 : 2 * size, :].astype(F32), value)
    found = functools.reduce(jnp.logical_or, picks[0:4])
    value = amplitude(value[0:size], value[size:]).astype(F32)
    other = jnp.where(picks[4], across_ref[...].astype(F32), before_ref[...].astype(F32))
    amp_ref[...] = jnp.where(found, value, other).astype(BF16)

    def use(p, ref_r, ref_i):
        lanes = slice(p * LANES, (p + 1) * LANES)
        own_r, own_i = spec_ref[0:size, lanes], spec_ref[size:, lanes]
        cross_ref[0:size, lanes] = own_r * ref_r + own_i * ref_i
        cross_ref[size:, lanes] = own_i * ref_r - own_r * ref_i

    energy = spectrum(amp_ref, rows_ref, first_ref, second_ref, use)
    scale = 1.0 / (BLK * jnp.sqrt(energy_ref[...] * energy + 1e-06))
    lag_rows = [[] for _ in range(LANES // LAGS)]
    cross = [cross_ref[:, p * LANES : (p + 1) * LANES] * scale[p : p + 1, :] for p in range(tiles)]
    cross = jnp.concatenate([value.astype(BF16) for value in cross], axis=1)
    lags = dot(third_ref[...], jnp.concatenate([cross, cross], axis=0))
    for p in range(tiles):
        for q in range(LANES // LAGS):
            at = [ri * LAGS + q * 8 for ri in range(2)]
            part = [lags[k : k + 8, p * LANES : (p + 1) * LANES] for k in at]
            lag_rows[q].append(jnp.concatenate(part, axis=1))
    lhs = jnp.concatenate([row for rows in lag_rows for row in rows], axis=0).astype(BF16)
    result = dot(jnp.concatenate([lhs, lhs], axis=1), fourth_ref[...])
    height = 8 * tiles
    quarter = iota((height, 2 * LANES), 1) % LANES // LAGS
    total = result[0:height]
    for q in range(1, LANES // LAGS):
        total = jnp.where(quarter == q, result[q * height : (q + 1) * height], total)
    for p in range(tiles):
        for jj in range(2):
            at = (2 * p + jj) * 8
            out_scr[at : at + 8, :] = total[p * 8 : p * 8 + 8, jj * LANES : (jj + 1) * LANES]
    for a in range(8):
        out_ref[:, a * LANES : (a + 1) * LANES] = out_scr[pl.ds(a, 2 * tiles, stride=8), :]


def shifted(value, axis, steps):
    count = lax.axis_size(axis)
    return lax.ppermute(value, axis, [(s, (s - steps) % count) for s in range(count)])


def swapped(value, axis, step):
    return lax.ppermute(value, axis, [(s, s ^ step) for s in range(lax.axis_size(axis))])


def spread(value, axis):
    count = lax.axis_size(axis)
    step = 2
    while step < count:
        value = jnp.maximum(value, swapped(value, axis, step))
        step *= 2
    return value


def call(kernel, name, out_shape, operands, scratch=()):
    return pl.pallas_call(
        kernel,
        out_shape=out_shape,
        in_specs=[VMEM] * len(operands),
        out_specs=jax.tree.map(lambda _: VMEM, out_shape),
        scratch_shapes=[pltpu.VMEM(*s) for s in scratch],
        compiler_params=PARAMS,
        name=name,
    )(*operands)


def body(slc, ref_date, int_offset, frac_offset, partners):
    sds = jax.ShapeDtypeStruct
    _, _, rows, cols = slc.shape
    tiles = cols // LANES
    dates = lax.axis_size("date")
    even = lax.axis_index("date") % 2 == 0
    field, samples = sds((rows, cols), BF16), sds((2 * rows, cols), BF16)
    payload = sds((2 * rows + HROWS, LANES), BF16)
    inputs = (slc.reshape(2 * rows, cols), int_offset[0], frac_offset[0], partners)
    inputs = [pltpu.with_memory_space_constraint(v, pltpu.HBM) for v in inputs]
    own, cond, taps, low, high = pl.pallas_call(
        prep_kernel,
        out_shape=(sds((2 * rows + 16, cols), BF16), sds((16, LANES), F32), sds((HROWS, LANES), BF16), payload, payload),
        in_specs=[pl.BlockSpec(memory_space=pltpu.HBM)] * 4 + [SMEM],
        out_specs=(VMEM,) * 5,
        scratch_shapes=[
            pltpu.VMEM(int_offset.shape[1:], jnp.int32),
            pltpu.VMEM(frac_offset.shape[1:], F32),
            pltpu.SMEM(partners.shape, jnp.int32),
            pltpu.SemaphoreType.DMA((4,)),
        ],
        compiler_params=PARAMS,
        name="prepare",
    )(*inputs, ref_date)
    beside = swapped(own, "date", 1)
    two = shifted(slc.reshape(2 * rows, cols), "date", 2)
    right = shifted(low, "rng", 1)
    left = shifted(high, "rng", -1)
    width = (rows // HROWS + 1) * LANES
    halo = call(
        functools.partial(halo_kernel, cols // BLK), "halo", sds((HROWS, width), BF16), (cond, taps, left, right)
    )
    joined = sds((2 * rows + HROWS, cols), BF16)
    four = shifted(call(join_kernel, "join", joined, (halo, two)), "date", 2)
    later = call(functools.partial(candidate_kernel, (0, 2)), "later", field, (cond, own, two))
    across = lax.ppermute(later, "date", [(s, (s - 2) % dates ^ 1) for s in range(dates)])
    beside_halo = swapped(halo, "date", 1)
    four_halo = shifted(halo, "date", 4)
    first, second, third, fourth = [jnp.asarray(t) for t in surface_tables()]
    spec, energy = call(
        spectrum_kernel,
        "spectrum",
        (sds((2 * rows, cols), F32), sds((tiles, LANES), F32)),
        (own, first, second, third, fourth),
        [((rows, cols), BF16), ((tiles, LANES), F32)],
    )
    resampled = (sds((2 * rows, cols + LANES), BF16), sds((rows, cols), F32))
    scratch = [[((k * rows, cols + LANES), BF16)] for k in range(4)]
    own_ext = call(own_kernel, "own", resampled, (energy, own, halo), scratch[1])
    *beside_ext, coh_beside = call(
        beside_kernel, "beside", (*resampled, field), (energy, *own_ext, beside, beside_halo), scratch[3]
    )
    amp = call(functools.partial(late_candidate_kernel, (0, 1)), "candidate", field, (coh_beside, cond, own, beside))
    before = shifted(amp, "date", -2) if dates == 8 else spread(amp, "date")
    *two_ext, coh_near = call(pair_kernel, "near", (*resampled, field), (*beside_ext, two, four), scratch[3])
    near = swapped(coh_near, "date", 1)
    coh_two = call(functools.partial(again_kernel, 1), "two", field, (cond, *own_ext, *two_ext), scratch[2])
    *four_ext, coh_far = call(pair_kernel, "far", (*resampled, field), (*beside_ext, four, four_halo), scratch[3])
    far = swapped(coh_far, "date", 1)
    coh_four = call(functools.partial(again_kernel, 3), "four", field, (cond, *own_ext, *four_ext), scratch[2])
    surface = call(
        surface_kernel,
        "surface",
        sds((cols // BLK, LAGS * LAGS), F32),
        (cond, own, beside, two, four, across, before, spec, energy, first, second, third, fourth),
        [
            ((rows, cols), BF16),
            ((tiles, LANES), F32),
            ((2 * rows, cols), F32),
            ((8 * cols // BLK + 8, LANES), F32),
        ],
    )
    coh_one = call(one_kernel, "one", field, (cond, coh_beside, near))
    operands = (cond, surface, coh_one, coh_two, coh_four, near, far)
    surface, fields = pl.pallas_call(
        place_kernel,
        out_shape=(sds(surface.shape, F32), sds((SPAN, rows, cols), BF16)),
        in_specs=[VMEM] * len(operands),
        out_specs=(pl.BlockSpec(memory_space=pl.ANY),) * 2,
        scratch_shapes=[pltpu.VMEM((rows, cols), BF16), pltpu.SemaphoreType.DMA((SPAN + 1,))],
        compiler_params=PARAMS,
        name="place",
    )(*operands)
    return (surface[None, None], fields[None])


def solution(mesh):
    in_specs = (
        P("date", None, None, "rng"),
        P(),
        P("date", None, "rng"),
        P("date", None, "rng"),
        P("date", None),
    )
    out_specs = (P("date", None, "rng", None), P("date", None, None, "rng"))
    return jax.shard_map(body, mesh=mesh, in_specs=in_specs, out_specs=out_specs, check_vma=False)
```
